256 devices in a mesh: box: 64 (over x, z, core), ch: 4 (over y).
Axes of the slice: x: 4, y: 4, z: 8, core: 2. Of those that a mesh axis runs over, the one named last changes fastest.
Arguments:
- features: bfloat16 [256, 262144], P('ch', 'box'), may hold values from -6 to 6
- occupied: int32 [262144], P('box'), may hold values 0 or 1
- send_lists: int32 [64, 2, 8], P('box'), may hold values from 0 to 32, as said below
- kernel_map: int32 [64, 27, 32], P('box'), may hold values from 0 to 48, as said below
- weights: bfloat16 [27, 256, 256], P(None, 'ch'), may hold values from -0.078125 to 0.078125
- norm_gain: float32 [256], P('ch'), may hold values from 0.25 to 1.75
- norm_shift: float32 [256], P('ch'), may hold values from -3 to 3
- out_grad: bfloat16 [256, 262144], P('ch', 'box'), may hold values from -6 to 6
Outputs:
- out_features: bfloat16 [256, 262144], P('ch', 'box')
- in_grad: bfloat16 [256, 262144], P('ch', 'box')
- weight_grad: float32 [27, 256, 256], P(None, 'ch')
- gain_grad: float32 [256], P('ch')
- shift_grad: float32 [256], P('ch')
The draws below stay inside these ranges and needn't reach their ends.
Inputs may be any that keep to these rules, and one draw needn't show every extreme that they name: `send_lists`: each entry names a local block, or 32 for an empty slot; the first slot of box 0's list to the lower box is empty and the first slot of its list to the upper box is block 0. `kernel_map`: each entry indexes the extended blocks; 48 is the zero block; offset 13 maps every block to itself.
All inputs are finite; a program needn't handle non-finite values. No bound on the sum of `occupied` on one device may be relied on, other than what follows from the above.
Results may differ from the reference program's by a relative error of at most 0.01295.
Values may be sent and summed in bfloat16 or wider, within the bound.
A program may use at most 64 MiB of HBM per device.

```python
import jax
import jax.numpy as jnp
from jax import lax

CH = 256
OFFSETS = 27
BLOCK = 128
BLOCKS = 32
SLOTS = 8
BOXES = 64
ROWS = 262144


def draw_send_lists(key, part):
    key = jax.random.fold_in(key, 11)
    send_picks = jax.random.randint(key, (BOXES, 2, SLOTS), 0, BLOCKS)
    send_picks = send_picks.at[0, 0, 0].set(BLOCKS)
    send_picks = send_picks.at[0, 1, 0].set(0)
    return send_picks.astype(jnp.int32)


def draw_kernel_map(key, part):
    key = jax.random.fold_in(key, 12)
    offset_table = jax.random.randint(key, (BOXES, OFFSETS, BLOCKS), 0, BLOCKS + 2 * SLOTS + 1)
    centre = jnp.broadcast_to(jnp.arange(BLOCKS, dtype=jnp.int32)[None, :], (BOXES, BLOCKS))
    offset_table = offset_table.at[:, 13, :].set(centre)
    offset_table = offset_table.at[:, 0, 0].set(BLOCKS + 2 * SLOTS)
    offset_table = offset_table.at[:, 1, 0].set(BLOCKS)
    offset_table = offset_table.at[:, 26, 0].set(BLOCKS + SLOTS)
    return offset_table.astype(jnp.int32)


def plant(array, stream_key, low, high):
    longest = array.shape.index(max(array.shape))
    spots = []
    for shift in (0, 1):
        where = [jax.random.randint(jax.random.fold_in(stream_key, axis), (), 0, length) for axis, length in enumerate(array.shape)]
        where[longest] = (where[longest] + shift) % array.shape[longest]
        spots.append(tuple(where))
    return array.at[spots[0]].set(low).at[spots[1]].set(high)


def block_scale(stream_key, extent, cuts, least, largest):
    factor_of = 1.0
    for position, shards_of in cuts:
        steps = jax.random.uniform(jax.random.fold_in(jax.random.fold_in(stream_key, 6), position), (shards_of,), jnp.float32, least / len(cuts), largest / len(cuts))
        factor_of = factor_of * jnp.repeat(jnp.exp(steps), extent[position] // shards_of).reshape((-1,) + (1,) * (len(extent) - 1 - position))
    return factor_of


def noise(rng, extent, scale, bound, cuts=(), kind=jnp.bfloat16):
    level = block_scale(rng, extent, cuts, -0.22, 0.18) if cuts else 1.0
    entries = jax.random.normal(rng, extent, jnp.float32) * scale * level
    return jnp.minimum(jnp.maximum(entries, -bound), bound).astype(kind)


def setup_inputs(seed: int = 0) -> dict:
    seeds = jax.random.split(jax.random.key(seed), 9)
    features = noise(seeds[0], (CH, ROWS), 1.0, 6.0, ((0, 4), (1, 64)))
    occupied = plant((jax.random.randint(seeds[1], (ROWS,), 0, 4) < 3).astype(jnp.int32), jax.random.fold_in(seeds[1], 1), 0, 1)
    send_lists = draw_send_lists(jax.random.fold_in(seeds[8], 71), 0)
    kernel_map = draw_kernel_map(jax.random.fold_in(seeds[8], 71), 0)
    weights = noise(seeds[4], (OFFSETS, CH, CH), (OFFSETS * CH) ** -0.5, 0.078125, ((1, 4),))
    norm_gain = jnp.clip(1.0 + 0.15 * jax.random.normal(seeds[5], (CH,), jnp.float32), 0.25, 1.75)
    norm_shift = noise(seeds[6], (CH,), 0.5, 3.0, ((0, 4),), jnp.float32)
    out_grad = noise(seeds[7], (CH, ROWS), 1.0, 6.0, ((0, 4), (1, 64)))
    return {"features": features, "occupied": occupied, "send_lists": send_lists, "kernel_map": kernel_map, "weights": weights, "norm_gain": norm_gain, "norm_shift": norm_shift, "out_grad": out_grad}


def extend_all(masked, send_lists):
    blocks = masked.reshape(BOXES, BLOCKS, BLOCK, CH)
    empty_block = jnp.zeros((BOXES, 1, BLOCK, CH), masked.dtype)
    padded = jnp.concatenate([blocks, empty_block], axis=1)
    outgoing = jax.vmap(lambda source, picks: source[picks])(padded, send_lists)
    edge_block = jnp.zeros((1, SLOTS, BLOCK, CH), masked.dtype)
    from_below = jnp.concatenate([edge_block, outgoing[:-1, 1]], axis=0)
    from_above = jnp.concatenate([outgoing[1:, 0], edge_block], axis=0)
    return jnp.concatenate([blocks, from_below, from_above, empty_block], axis=1)

def reference(features, occupied, send_lists, kernel_map, weights, norm_gain, norm_shift, out_grad):
    features_rows = features.T
    out_grad_rows = out_grad.T
    kernel_in_out = jnp.transpose(weights, (0, 2, 1))
    occupancy = occupied.astype(jnp.float32)[:, None]
    masked = features_rows * occupied.astype(jnp.bfloat16)[:, None]
    extended = extend_all(masked, send_lists)

    def box_conv(box_item):
        ext_box, offset_table = box_item

        def conv_step(running, step_inputs):
            source_row, kernel_slab = step_inputs
            gathered = ext_box[source_row].reshape(BLOCKS * BLOCK, CH)
            return (running + jnp.dot(gathered, kernel_slab, preferred_element_type=jnp.float32), None)
        conv_out, _ = lax.scan(conv_step, jnp.zeros((BLOCKS * BLOCK, CH), jnp.float32), (offset_table, kernel_in_out))
        return conv_out
    conv = lax.map(box_conv, (extended, kernel_map)).reshape(ROWS, CH)
    voxel_count = jnp.sum(occupancy)
    stat_mean = lax.optimization_barrier(jnp.sum(occupancy * conv, axis=0)) / voxel_count
    stat_var = lax.optimization_barrier(jnp.sum(occupancy * conv * conv, axis=0)) / voxel_count - stat_mean * stat_mean
    inv_std = 1.0 / jnp.sqrt(stat_var + 1e-05)
    normed = (conv - stat_mean) * inv_std
    shifted = normed * norm_gain + norm_shift
    out_features = (occupancy * jnp.maximum(shifted, 0.0)).astype(jnp.bfloat16)
    relu_grad = occupancy * out_grad_rows.astype(jnp.float32) * (shifted > 0.0).astype(jnp.float32)
    shift_grad = lax.optimization_barrier(jnp.sum(relu_grad, axis=0))
    gain_grad = lax.optimization_barrier(jnp.sum(relu_grad * normed, axis=0))
    conv_grad = (occupancy * inv_std * norm_gain * (relu_grad - shift_grad / voxel_count - normed * gain_grad / voxel_count)).astype(jnp.bfloat16)
    grad_boxes = conv_grad.reshape(BOXES, BLOCKS * BLOCK, CH)
    ext_count = BLOCKS + 2 * SLOTS + 1

    def box_back(box_item):
        ext_box, offset_table, grad_box = box_item

        def back_step(running, step_inputs):
            source_row, kernel_slab = step_inputs
            gathered = ext_box[source_row].reshape(BLOCKS * BLOCK, CH)
            kernel_term = lax.dot_general(gathered, grad_box, (((0,), (0,)), ((), ())), preferred_element_type=jnp.float32)
            contrib = lax.dot_general(grad_box, kernel_slab, (((1,), (1,)), ((), ())), preferred_element_type=jnp.float32)
            running = running.at[source_row].add(contrib.reshape(BLOCKS, BLOCK, CH))
            return (running, kernel_term)
        start = jnp.zeros((ext_count, BLOCK, CH), jnp.float32)
        return lax.scan(back_step, start, (offset_table, kernel_in_out))
    ext_grad, kernel_terms = lax.map(box_back, (extended, kernel_map, grad_boxes))
    weight_grad = jnp.transpose(lax.optimization_barrier(jnp.sum(kernel_terms, axis=0)), (0, 2, 1))
    own_part = ext_grad[:, :BLOCKS]
    below_slots = ext_grad[:, BLOCKS:BLOCKS + SLOTS]
    above_slots = ext_grad[:, BLOCKS + SLOTS:BLOCKS + 2 * SLOTS]
    edge_block = jnp.zeros((1, SLOTS, BLOCK, CH), jnp.float32)
    to_upper_list = jnp.concatenate([below_slots[1:], edge_block], axis=0)
    to_lower_list = jnp.concatenate([edge_block, above_slots[:-1]], axis=0)
    padded = jnp.concatenate([own_part, jnp.zeros((BOXES, 1, BLOCK, CH), jnp.float32)], axis=1)

    def settle(target, picks, upper_part, lower_part):
        return target.at[picks[1]].add(upper_part).at[picks[0]].add(lower_part)
    padded = jax.vmap(settle)(padded, send_lists, to_upper_list, to_lower_list)
    input_grad = padded[:, :BLOCKS].reshape(ROWS, CH)
    in_grad = (occupancy * input_grad).astype(jnp.bfloat16)
    return (out_features.T, in_grad.T, weight_grad, gain_grad, shift_grad)
```

```python
import functools

import jax
import jax.numpy as jnp
from jax import lax
from jax.experimental import pallas as pl
from jax.experimental.pallas import tpu as pltpu
from jax.sharding import PartitionSpec as P

F32 = jnp.float32
BF16 = jnp.bfloat16
MESH = pl.DeviceIdType.MESH
VMEM = pl.BlockSpec(memory_space=pltpu.VMEM)
SMEM = pl.BlockSpec(memory_space=pltpu.SMEM)
VMEM_LIMIT = 56 * 2**20

BLOCK = 128
BLOCKS = 32
HALF = 16
SLOTS = 8
EXT = BLOCKS + 2 * SLOTS
OFFSETS = 27
CH = 256
LOC = 64
KCH = 9
CHUNKS = OFFSETS // KCH
CROWS = KCH * LOC
WPAD = 1792
NBOX = 64
NA = 4


def params(cid=None):
    if cid is None:
        return pltpu.CompilerParams(vmem_limit_bytes=VMEM_LIMIT)
    return pltpu.CompilerParams(
        vmem_limit_bytes=VMEM_LIMIT, collective_id=cid, has_side_effects=True
    )


def rcopy(src, dst, ssem, rsem, dev):
    return pltpu.make_async_remote_copy(
        src_ref=src, dst_ref=dst, send_sem=ssem, recv_sem=rsem, device_id=dev, device_id_type=MESH
    )


def greet(devs):
    barrier = pltpu.get_barrier_semaphore()
    for dev in devs:
        pl.semaphore_signal(barrier, inc=1, device_id=dev, device_id_type=MESH)
    pl.semaphore_wait(barrier, len(devs))


def rows_of(q):
    return pl.ds(pl.multiple_of(q * LOC, LOC), LOC)


class YGather:
    def __init__(self, own, from_dn, from_up, opp, ssem, rsem):
        q = lax.axis_index("ch")
        self.up = {"ch": lax.rem(q + 1, 4)}
        self.dn = {"ch": lax.rem(q + 3, 4)}
        lo, hi = pl.ds(0, HALF), pl.ds(HALF, HALF)
        mk = lambda src, dst, half, i, dev: rcopy(src.at[half], dst.at[half], ssem.at[i], rsem.at[i], dev)
        self.c = [
            mk(own, from_dn, lo, 0, self.up),
            mk(own, from_up, hi, 1, self.dn),
            mk(own, from_dn, hi, 2, self.up),
            mk(own, from_up, lo, 3, self.dn),
            mk(from_dn, opp, lo, 4, self.up),
            mk(from_up, opp, hi, 5, self.dn),
        ]

    def start(self):
        for i in range(4):
            self.c[i].start()

    def forward(self):
        self.c[0].wait_recv()
        self.c[4].start()
        self.c[1].wait_recv()
        self.c[5].start()

    def wait_near(self):
        self.c[2].wait_recv()
        self.c[3].wait_recv()

    def wait_far(self):
        self.c[4].wait_recv()
        self.c[5].wait_recv()

    def wait_sends(self):
        for c in self.c:
            c.wait_send()


def ext_kernel(
    send_ref, feat_ref, occ_ref, ext_ref, own, from_dn, from_up, opp, fout, fin, ysend, yrecv, fsend, frecv
):
    q = lax.axis_index("ch")
    b = lax.axis_index("box")
    above = {"box": lax.rem(b + 1, NBOX)}
    below = {"box": lax.rem(b + NBOX - 1, NBOX)}
    gather = YGather(own, from_dn, from_up, opp, ysend, yrecv)

    def mask(e, _):
        x = feat_ref[:, pl.ds(pl.multiple_of(e * BLOCK, BLOCK), BLOCK)].astype(F32)
        own[e] = (x * occ_ref[e]).astype(BF16)
        return 0

    lax.fori_loop(0, BLOCKS, mask, 0)
    greet([gather.up, gather.dn, above, below])
    gather.start()

    def pack(r, src):
        for d in range(2):
            for s in range(SLOTS):
                pick = send_ref[d * SLOTS + s]
                blk = src[jnp.minimum(pick, BLOCKS - 1)].astype(F32)
                fout[r, d, s] = jnp.where(pick < BLOCKS, blk, 0.0).astype(BF16)
        up = rcopy(fout.at[r, 1], fin.at[r, 0], fsend.at[r, 1], frecv.at[r, 0], above)
        dn = rcopy(fout.at[r, 0], fin.at[r, 1], fsend.at[r, 0], frecv.at[r, 1], below)
        up.start()
        dn.start()
        return up, dn

    def place(r_abs, src):
        rows = rows_of(r_abs)

        def one(e, _):
            ext_ref[e, rows, :] = src[e]
            return 0

        lax.fori_loop(0, BLOCKS, one, 0)

    q_dn, q_up, q_opp = lax.rem(q + 3, 4), lax.rem(q + 1, 4), lax.rem(q + 2, 4)
    copies = [pack(0, own)]
    place(q, own)
    ext_ref[EXT] = jnp.zeros((CH, BLOCK), BF16)
    gather.forward()
    gather.wait_near()
    copies.append(pack(1, from_dn))
    copies.append(pack(2, from_up))
    place(q_dn, from_dn)
    place(q_up, from_up)
    gather.wait_far()
    copies.append(pack(3, opp))
    place(q_opp, opp)
    keep_below = jnp.where(b > 0, 1.0, 0.0)
    keep_above = jnp.where(b < NBOX - 1, 1.0, 0.0)
    for r, r_abs in enumerate((q, q_dn, q_up, q_opp)):
        up, dn = copies[r]
        up.wait_recv()
        dn.wait_recv()
        rows = rows_of(r_abs)
        for s in range(SLOTS):
            ext_ref[BLOCKS + s, rows, :] = (fin[r, 0, s].astype(F32) * keep_below).astype(BF16)
            ext_ref[BLOCKS + SLOTS + s, rows, :] = (fin[r, 1, s].astype(F32) * keep_above).astype(BF16)
    gather.wait_sends()
    for up, dn in copies:
        up.wait_send()
        dn.wait_send()


def make_ext(send, features, occ):
    quarter = pltpu.VMEM((BLOCKS, LOC, BLOCK), BF16)
    return pl.pallas_call(
        ext_kernel,
        out_shape=jax.ShapeDtypeStruct((EXT + 1, CH, BLOCK), BF16),
        in_specs=[SMEM, VMEM, VMEM],
        out_specs=VMEM,
        scratch_shapes=[
            quarter,
            quarter,
            quarter,
            quarter,
            pltpu.VMEM((4, 2, SLOTS, LOC, BLOCK), BF16),
            pltpu.VMEM((4, 2, SLOTS, LOC, BLOCK), BF16),
            pltpu.SemaphoreType.DMA((6,)),
            pltpu.SemaphoreType.DMA((6,)),
            pltpu.SemaphoreType.DMA((4, 2)),
            pltpu.SemaphoreType.DMA((4, 2)),
        ],
        compiler_params=params(1),
        name="extend",
    )(send, features, occ)


def conv_kernel(map_ref, w_ref, ext_ref, occ_ref, conv_ref, sum_ref, p_ref):
    p_ref[EXT] = jnp.zeros((CROWS, BLOCK), F32)
    for c in range(CHUNKS):

        def tile(t, _):
            rhs = jnp.concatenate([ext_ref[2 * t], ext_ref[2 * t + 1]], axis=1)
            res = jnp.dot(w_ref[pl.ds(c * CROWS, CROWS), :], rhs, preferred_element_type=F32)
            p_ref[2 * t] = res[:, :BLOCK]
            p_ref[2 * t + 1] = res[:, BLOCK:]
            return 0

        lax.fori_loop(0, EXT // 2, tile, 0)

        def out(j, _):
            acc = None
            for k in range(KCH):
                v = p_ref[map_ref[(c * KCH + k) * BLOCKS + j], pl.ds(LOC * k, LOC), :]
                acc = v if acc is None else acc + v
            if c == 0:
                conv_ref[j] = acc
            else:
                conv_ref[j] += acc
            return 0

        lax.fori_loop(0, BLOCKS, out, 0)

    def stats(j, carry):
        a, b = carry
        x = conv_ref[j]
        o = occ_ref[j] * x
        return a + o, b + o * x

    zero = jnp.zeros((LOC, BLOCK), F32)
    a, b = lax.fori_loop(0, BLOCKS, stats, (zero, zero))
    sum_ref[0] = a
    sum_ref[1] = b


def conv_call(kmap, w, ext, occ):
    return pl.pallas_call(
        conv_kernel,
        out_shape=(
            jax.ShapeDtypeStruct((BLOCKS, LOC, BLOCK), F32),
            jax.ShapeDtypeStruct((2, LOC, BLOCK), F32),
        ),
        in_specs=[SMEM, VMEM, VMEM, VMEM],
        out_specs=(VMEM, VMEM),
        scratch_shapes=[pltpu.VMEM((EXT + 1, CROWS, BLOCK), F32)],
        compiler_params=params(),
        name="conv",
    )(kmap, w, ext, occ)


def lane_masks():
    ch = lax.broadcasted_iota(jnp.int32, (LOC, BLOCK), 0)
    lane = lax.broadcasted_iota(jnp.int32, (LOC, BLOCK), 1)
    return lane == ch, lane == ch + LOC


def to_row(first, second):
    m0, m1 = lane_masks()
    c0 = jnp.sum(first, axis=1, keepdims=True)
    c1 = jnp.sum(second, axis=1, keepdims=True)
    return jnp.sum(jnp.where(m0, c0, 0.0) + jnp.where(m1, c1, 0.0), axis=0, keepdims=True)


def to_cols(row):
    m0, m1 = lane_masks()
    return (
        jnp.sum(jnp.where(m0, row, 0.0), axis=1, keepdims=True),
        jnp.sum(jnp.where(m1, row, 0.0), axis=1, keepdims=True),
    )


def box_groups():
    b = lax.axis_index("box")
    hi, lo = b // 8, lax.rem(b, 8)
    near = [{"box": hi * 8 + lax.rem(lo + d, 8)} for d in range(1, 8)]
    far = [{"box": lax.rem(hi + d, 8) * 8 + lo} for d in range(1, 8)]
    return (lo, near), (hi, far)


def box_sum(mine, buf, ssem, rsem):
    for step, (me, peers) in enumerate(box_groups()):
        buf[step, me] = mine
        copies = []
        for d, dev in enumerate(peers):
            c = rcopy(buf.at[step, me], buf.at[step, me], ssem.at[step, d], rsem.at[step, d], dev)
            c.start()
            copies.append(c)
        for c in copies:
            c.wait_recv()
        mine = buf[step, 0]
        for d in range(1, 8):
            mine = mine + buf[step, d]
        for c in copies:
            c.wait_send()
    return mine


def norm_kernel(
    map_ref,
    conv_ref,
    sum_ref,
    grad_ref,
    occ_ref,
    gs_ref,
    ext_ref,
    out_ref,
    cga_ref,
    wg_ref,
    stat_ref,
    normed,
    rgrad,
    own,
    from_dn,
    from_up,
    opp,
    sbuf,
    ysend,
    yrecv,
    ssend,
    srecv,
):
    q = lax.axis_index("ch")
    gather = YGather(own, from_dn, from_up, opp, ysend, yrecv)
    (_, near), (_, far) = box_groups()
    sub = lax.broadcasted_iota(jnp.int32, (8, BLOCK), 0)
    count = jnp.sum(occ_ref[...], axis=0)
    count = jnp.broadcast_to(jnp.sum(count, axis=1, keepdims=True), (1, BLOCK))
    row = to_row(sum_ref[0], sum_ref[1])
    pay = jnp.where(sub == 0, row, jnp.where(sub == 1, count, 0.0))
    greet([gather.up, gather.dn] + near + far)
    tot = box_sum(pay, sbuf.at[0], ssend.at[0], srecv.at[0])
    n_vox = tot[1:2, 0:1]
    s1, s2 = to_cols(tot[0:1, :])
    mean = s1 / n_vox
    var = s2 / n_vox - mean * mean
    inv = 1.0 / jnp.sqrt(var + 1e-05)
    gain, shift = to_cols(gs_ref[...])

    def fwd(j, carry):
        a, b = carry
        cols = pl.ds(pl.multiple_of(j * BLOCK, BLOCK), BLOCK)
        occ = occ_ref[j]
        nd = (conv_ref[j] - mean) * inv
        sh = nd * gain + shift
        out_ref[:, cols] = (occ * jnp.maximum(sh, 0.0)).astype(BF16)
        rg = jnp.where(sh > 0.0, occ * grad_ref[:, cols].astype(F32), 0.0)
        normed[j] = nd
        rgrad[j] = rg
        return a + rg, b + rg * nd

    zero = jnp.zeros((LOC, BLOCK), F32)
    a, b = lax.fori_loop(0, BLOCKS, fwd, (zero, zero))
    row = to_row(a, b)
    tot = box_sum(jnp.where(sub == 0, row, 0.0), sbuf.at[1], ssend.at[1], srecv.at[1])
    stat_ref[...] = tot[0:1, :]
    sg, gg = to_cols(tot[0:1, :])
    scale = inv * gain
    sgm = sg / n_vox

    def bwd(j, _):
        nd = normed[j]
        own[j] = (occ_ref[j] * scale * (rgrad[j] - sgm - nd * gg / n_vox)).astype(BF16)
        return 0

    lax.fori_loop(0, BLOCKS, bwd, 0)
    gather.start()
    gather.forward()

    def kterm(k, _):
        acc = jnp.zeros((LOC, CH), F32)
        for t in range(BLOCKS // 2):
            lhs = jnp.concatenate([own[2 * t], own[2 * t + 1]], axis=1)
            rhs = jnp.concatenate(
                [ext_ref[map_ref[k * BLOCKS + 2 * t]], ext_ref[map_ref[k * BLOCKS + 2 * t + 1]]], axis=1
            )
            acc += lax.dot_general(lhs, rhs, (((1,), (1,)), ((), ())), preferred_element_type=F32)
        wg_ref[k] = acc
        return 0

    lax.fori_loop(0, OFFSETS, kterm, 0)

    def place(r_abs, src):
        rows = rows_of(r_abs)

        def one(e, _):
            cga_ref[e, rows, :] = src[e]
            return 0

        lax.fori_loop(0, BLOCKS, one, 0)

    place(q, own)
    gather.wait_near()
    place(lax.rem(q + 3, 4), from_dn)
    place(lax.rem(q + 1, 4), from_up)
    gather.wait_far()
    place(lax.rem(q + 2, 4), opp)
    gather.wait_sends()


def norm_call(kmap, conv, sums, out_grad, occ, gs, ext):
    quarter = pltpu.VMEM((BLOCKS, LOC, BLOCK), BF16)
    return pl.pallas_call(
        norm_kernel,
        out_shape=(
            jax.ShapeDtypeStruct((LOC, BLOCKS * BLOCK), BF16),
            jax.ShapeDtypeStruct((BLOCKS, CH, BLOCK), BF16),
            jax.ShapeDtypeStruct((OFFSETS, LOC, CH), F32),
            jax.ShapeDtypeStruct((1, BLOCK), F32),
        ),
        in_specs=[SMEM] + [VMEM] * 6,
        out_specs=(VMEM,) * 4,
        scratch_shapes=[
            pltpu.VMEM((BLOCKS, LOC, BLOCK), F32),
            pltpu.VMEM((BLOCKS, LOC, BLOCK), F32),
            quarter,
            quarter,
            quarter,
            quarter,
            pltpu.VMEM((2, 2, 8, 8, BLOCK), F32),
            pltpu.SemaphoreType.DMA((6,)),
            pltpu.SemaphoreType.DMA((6,)),
            pltpu.SemaphoreType.DMA((2, 2, 7)),
            pltpu.SemaphoreType.DMA((2, 2, 7)),
        ],
        compiler_params=params(2),
        name="norm",
    )(kmap, conv, sums, out_grad, occ, gs, ext)


def back_kernel(map_ref, w_ref, cg_ref, eg_ref, q_ref, *accs):
    for a in accs:

        def zero(e, _):
            a[e] = jnp.zeros((LOC, BLOCK), F32)
            return 0

        lax.fori_loop(0, EXT + 1, zero, 0)
    for c in range(CHUNKS):

        def tile(t, _):
            rhs = jnp.concatenate([cg_ref[2 * t], cg_ref[2 * t + 1]], axis=1)
            res = jnp.dot(w_ref[pl.ds(c * CROWS, CROWS), :], rhs, preferred_element_type=F32)
            q_ref[2 * t] = res[:, :BLOCK]
            q_ref[2 * t + 1] = res[:, BLOCK:]
            return 0

        lax.fori_loop(0, BLOCKS // 2, tile, 0)

        def scatter(t, _):
            for k in range(KCH):
                for i in range(NA):
                    j = t * NA + i
                    m = map_ref[(c * KCH + k) * BLOCKS + j]
                    accs[i][m] = accs[i][m] + q_ref[j, pl.ds(LOC * k, LOC), :]
            return 0

        lax.fori_loop(0, BLOCKS // NA, scatter, 0)

    def finish(e, _):
        s = accs[0][e]
        for a in accs[1:]:
            s = s + a[e]
        eg_ref[e] = s
        return 0

    lax.fori_loop(0, EXT, finish, 0)


def back_call(kmap, w, cga):
    return pl.pallas_call(
        back_kernel,
        out_shape=jax.ShapeDtypeStruct((EXT, LOC, BLOCK), F32),
        in_specs=[SMEM, VMEM, VMEM],
        out_specs=VMEM,
        scratch_shapes=[pltpu.VMEM((BLOCKS, CROWS, BLOCK), F32)]
        + [pltpu.VMEM((EXT + 1, LOC, BLOCK), F32)] * NA,
        compiler_params=params(),
        name="back",
    )(kmap, w, cga)


def final_kernel(
    send_ref, eg_ref, occ_ref, wg_ref, in_ref, wout_ref, fout, fin, half, halfin, zbuf, zin, red, xin, res, fsend, frecv, csend, crecv, zsend, zrecv, xsend, xrecv, asend, arecv, esend, erecv
):
    b = lax.axis_index("box")
    core = lax.rem(b, 2)
    z = lax.rem(b // 2, 8)
    x = b // 16
    dev = lambda xx, zz, cc: {"box": xx * 16 + zz * 2 + cc}
    above = {"box": lax.rem(b + 1, NBOX)}
    below = {"box": lax.rem(b + NBOX - 1, NBOX)}
    mate = dev(x, z, 1 - core)
    zpeers = [dev(x, lax.rem(z + d, 8), core) for d in range(1, 8)]
    xpeers = [dev(lax.rem(x + d, 4), z, core) for d in range(1, 4)]
    KP = 28

    def cut(k, _):
        lo, hi = wg_ref[k, :, :BLOCK], wg_ref[k, :, BLOCK:]
        keep = jnp.where(core == 0, lo, hi)
        give = jnp.where(core == 0, hi, lo)
        half[k] = give.astype(BF16)
        red[k] = keep
        return 0

    lax.fori_loop(0, OFFSETS, cut, 0)
    half[OFFSETS] = jnp.zeros((LOC, BLOCK), BF16)
    red[OFFSETS] = jnp.zeros((LOC, BLOCK), F32)
    for s in range(SLOTS):
        fout[0, s] = eg_ref[BLOCKS + s].astype(BF16)
        fout[1, s] = eg_ref[BLOCKS + SLOTS + s].astype(BF16)
    greet([above, below, mate] + zpeers + xpeers)
    cm = rcopy(half, halfin, csend, crecv, mate)
    cm.start()
    f0 = rcopy(fout.at[0], fin.at[0], fsend.at[0], frecv.at[0], below)
    f1 = rcopy(fout.at[1], fin.at[1], fsend.at[1], frecv.at[1], above)
    f0.start()
    f1.start()
    cm.wait_recv()
    rows = KP * LOC // 8

    def add(k, _):
        t = red[k] + halfin[k].astype(F32)
        red[k] = t
        zbuf[pl.ds(pl.multiple_of(k * LOC, LOC), LOC), :] = t.astype(BF16)
        return 0

    lax.fori_loop(0, KP, add, 0)
    part = lambda zz: pl.ds(pl.multiple_of(zz * rows, 16), rows)
    zc = []
    for d in range(1, 8):
        c = rcopy(zbuf.at[part(lax.rem(z + d, 8))], zin.at[d - 1], zsend.at[d - 1], zrecv.at[d - 1], zpeers[d - 1])
        c.start()
        zc.append(c)

    f0.wait_recv()
    f1.wait_recv()
    up_ok = b < NBOX - 1
    dn_ok = b > 0

    def settle(d, _):
        t = eg_ref[d]
        for s in range(SLOTS):
            t = t + jnp.where((send_ref[SLOTS + s] == d) & up_ok, fin[0, s].astype(F32), 0.0)
            t = t + jnp.where((send_ref[s] == d) & dn_ok, fin[1, s].astype(F32), 0.0)
        in_ref[:, pl.ds(pl.multiple_of(d * BLOCK, BLOCK), BLOCK)] = (occ_ref[d] * t).astype(BF16)
        return 0

    lax.fori_loop(0, BLOCKS, settle, 0)

    for c in zc:
        c.wait_recv()
    tot = zbuf[part(z), :].astype(F32)
    for d in range(7):
        tot = tot + zin[d].astype(F32)
    xin[x] = tot.astype(BF16)
    xc = []
    for d in range(1, 4):
        c = rcopy(xin.at[x], xin.at[x], xsend.at[d - 1], xrecv.at[d - 1], xpeers[d - 1])
        c.start()
        xc.append(c)
    for c in xc:
        c.wait_recv()
    tot = xin[0].astype(F32)
    for d in range(1, 4):
        tot = tot + xin[d].astype(F32)
    for c in xc:
        c.wait_send()
    for c in zc:
        c.wait_send()
    res[0, part(z), :] = tot.astype(BF16)
    ac = []
    for d in range(1, 8):
        c = rcopy(res.at[0, part(z)], res.at[0, part(z)], asend.at[d - 1], arecv.at[d - 1], zpeers[d - 1])
        c.start()
        ac.append(c)
    for d in range(1, 8):
        src = lax.rem(z + 8 - d, 8)
        rcopy(res.at[0, part(src)], res.at[0, part(src)], asend.at[d - 1], arecv.at[d - 1], zpeers[d - 1]).wait_recv()
    e = rcopy(res.at[0], res.at[1], esend, erecv, mate)
    e.start()
    e.wait_recv()

    def put(k, _):
        r = pl.ds(pl.multiple_of(k * LOC, LOC), LOC)
        m = res[0, r, :].astype(F32)
        o = res[1, r, :].astype(F32)
        wout_ref[k, :, :BLOCK] = jnp.where(core == 0, m, o)
        wout_ref[k, :, BLOCK:] = jnp.where(core == 0, o, m)
        return 0

    lax.fori_loop(0, OFFSETS, put, 0)
    e.wait_send()
    for c in ac:
        c.wait_send()
    cm.wait_send()
    f0.wait_send()
    f1.wait_send()


def final_call(send, eg, occ, wg):
    KP = 28
    rows = KP * LOC // 8
    dma = pltpu.SemaphoreType.DMA
    return pl.pallas_call(
        final_kernel,
        out_shape=(
            jax.ShapeDtypeStruct((LOC, BLOCKS * BLOCK), BF16),
            jax.ShapeDtypeStruct((OFFSETS, LOC, CH), F32),
        ),
        in_specs=[SMEM, VMEM, VMEM, VMEM],
        out_specs=(VMEM, VMEM),
        scratch_shapes=[
            pltpu.VMEM((2, SLOTS, LOC, BLOCK), BF16),
            pltpu.VMEM((2, SLOTS, LOC, BLOCK), BF16),
            pltpu.VMEM((KP, LOC, BLOCK), BF16),
            pltpu.VMEM((KP, LOC, BLOCK), BF16),
            pltpu.VMEM((KP * LOC, BLOCK), BF16),
            pltpu.VMEM((7, rows, BLOCK), BF16),
            pltpu.VMEM((KP, LOC, BLOCK), F32),
            pltpu.VMEM((4, rows, BLOCK), BF16),
            pltpu.VMEM((2, KP * LOC, BLOCK), BF16),
            dma((2,)),
            dma((2,)),
            dma,
            dma,
            dma((7,)),
            dma((7,)),
            dma((3,)),
            dma((3,)),
            dma((7,)),
            dma((7,)),
            dma,
            dma,
        ],
        compiler_params=params(3),
        name="final",
    )(send, eg, occ, wg)


def per_device(
    features, occupied, send_lists, kernel_map, weights, norm_gain, norm_shift, out_grad
):
    occ = occupied.astype(F32).reshape(BLOCKS, 1, BLOCK)
    send = send_lists.reshape(2 * SLOTS)
    kmap = kernel_map.reshape(OFFSETS * BLOCKS)
    w = weights.reshape(OFFSETS * LOC, CH)
    gs = jnp.concatenate([norm_gain, norm_shift]).reshape(1, BLOCK)
    parts = weights.reshape(OFFSETS, LOC, 4, LOC).transpose(2, 0, 3, 1)
    whole = lax.all_to_all(parts, "ch", split_axis=0, concat_axis=0)
    w_in = whole.transpose(1, 2, 0, 3).reshape(OFFSETS * LOC, CH)

    ext = make_ext(send, features, occ)
    conv, sums = conv_call(kmap, w, ext, occ)
    out_features, cga, wg, stat = norm_call(kmap, conv, sums, out_grad, occ, gs, ext)
    eg = back_call(kmap, w_in, cga)
    in_grad, weight_grad = final_call(send, eg, occ, wg)
    return (out_features, in_grad, weight_grad, stat[0, LOC:], stat[0, :LOC])


def solution(mesh):
    in_specs = (
        P("ch", "box"),
        P("box"),
        P("box", None, None),
        P("box", None, None),
        P(None, "ch", None),
        P("ch"),
        P("ch"),
        P("ch", "box"),
    )
    out_specs = (P("ch", "box"), P("ch", "box"), P(None, "ch", None), P("ch"), P("ch"))
    return jax.shard_map(
        per_device, mesh=mesh, in_specs=in_specs, out_specs=out_specs, check_vma=False
    )
```

```python
import functools

import jax
import jax.numpy as jnp
from jax import lax
from jax.experimental import pallas as pl
from jax.experimental.pallas import tpu as pltpu
from jax.sharding import PartitionSpec as P

F32 = jnp.float32
BF16 = jnp.bfloat16
MESH = pl.DeviceIdType.MESH
VMEM = pl.BlockSpec(memory_space=pltpu.VMEM)
SMEM = pl.BlockSpec(memory_space=pltpu.SMEM)
VMEM_LIMIT = 60 * 2**20

BLOCK = 128
BLOCKS = 32
CHUNK = 8
SLOTS = 8
EXT = BLOCKS + 2 * SLOTS
OFFSETS = 27
CH = 256
LOC = 64
WPAD = 1792
WROWS = 2048
XROWS = WROWS // 4
ZROWS = XROWS // 8
NBOX = 64
NA = 4


def params(cid=None):
    if cid is None:
        return pltpu.CompilerParams(vmem_limit_bytes=VMEM_LIMIT)
    return pltpu.CompilerParams(
        vmem_limit_bytes=VMEM_LIMIT, collective_id=cid, has_side_effects=True
    )


def rcopy(src, dst, ssem, rsem, dev):
    return pltpu.make_async_remote_copy(
        src_ref=src, dst_ref=dst, send_sem=ssem, recv_sem=rsem, device_id=dev, device_id_type=MESH
    )


def greet(devs):
    barrier = pltpu.get_barrier_semaphore()
    for dev in devs:
        pl.semaphore_signal(barrier, inc=1, device_id=dev, device_id_type=MESH)
    pl.semaphore_wait(barrier, len(devs))


def rows_of(q):
    return pl.ds(pl.multiple_of(q * LOC, LOC), LOC)


class YGather:
    def __init__(self, own, from_dn, from_up, opp, ssem, rsem):
        q = lax.axis_index("ch")
        self.up = {"ch": lax.rem(q + 1, 4)}
        self.dn = {"ch": lax.rem(q + 3, 4)}

        def mk(src, dst, chunk, i, dev):
            part = pl.ds(chunk * CHUNK, CHUNK)
            return rcopy(src.at[part], dst.at[part], ssem.at[i], rsem.at[i], dev)

        self.own_up = [mk(own, from_dn, c, c, self.up) for c in range(4)]
        self.own_dn = [mk(own, from_up, c, 4 + c, self.dn) for c in range(4)]
        self.far_up = [mk(from_dn, opp, c, 8 + c, self.up) for c in (0, 1)]
        self.far_dn = [mk(from_up, opp, c, 8 + c, self.dn) for c in (2, 3)]

    def start(self):
        self.own_up[0].start()
        self.own_dn[2].start()
        self.own_up[1].start()
        self.own_dn[3].start()

    def forward(self, i):
        self.own_up[i].wait_recv()
        self.far_up[i].start()
        self.own_up[2 + i].start()
        self.own_dn[2 + i].wait_recv()
        self.far_dn[i].start()
        self.own_dn[i].start()

    def wait_part(self, i):
        self.own_up[2 + i].wait_recv()
        self.own_dn[i].wait_recv()
        self.far_up[i].wait_recv()
        self.far_dn[i].wait_recv()

    def wait_sends(self):
        for c in self.own_up + self.own_dn + self.far_up + self.far_dn:
            c.wait_send()


def conv_kernel(
    send_ref,
    map_ref,
    feat_ref,
    occ_ref,
    w_ref,
    conv_ref,
    sum_ref,
    extt_ref,
    parts_ref,
    own,
    from_dn,
    from_up,
    opp,
    fout,
    fin,
    ext,
    prod,
    ysend,
    yrecv,
    fsend,
    frecv,
):
    q = lax.axis_index("ch")
    b = lax.axis_index("box")
    above = {"box": lax.rem(b + 1, NBOX)}
    below = {"box": lax.rem(b + NBOX - 1, NBOX)}
    gather = YGather(own, from_dn, from_up, opp, ysend, yrecv)
    quarters = ((q, own), (lax.rem(q + 3, 4), from_dn), (lax.rem(q + 1, 4), from_up), (lax.rem(q + 2, 4), opp))

    def mask(e, _):
        x = feat_ref[:, pl.ds(pl.multiple_of(e * BLOCK, BLOCK), BLOCK)].astype(F32)
        own[e] = (x * occ_ref[e]).astype(BF16)
        return 0

    lax.fori_loop(0, BLOCKS, mask, 0)
    greet([gather.up, gather.dn, above, below])
    gather.start()

    def pack(r, src):
        for d in range(2):
            for s in range(SLOTS):
                pick = send_ref[d * SLOTS + s]
                blk = src[jnp.minimum(pick, BLOCKS - 1)].astype(F32)
                fout[r, d, s] = jnp.where(pick < BLOCKS, blk, 0.0).astype(BF16)
        up = rcopy(fout.at[r, 1], fin.at[r, 0], fsend.at[r, 1], frecv.at[r, 0], above)
        dn = rcopy(fout.at[r, 0], fin.at[r, 1], fsend.at[r, 0], frecv.at[r, 1], below)
        up.start()
        dn.start()
        return up, dn

    def tile(t):
        for e in (2 * t, 2 * t + 1):
            extt_ref[e] = ext[e].T
        rhs = jnp.concatenate([ext[2 * t], ext[2 * t + 1]], axis=1)
        res = jnp.dot(w_ref[...], rhs, preferred_element_type=F32)
        prod[2 * t] = res[:, :BLOCK]
        prod[2 * t + 1] = res[:, BLOCK:]

    def part_tiles(i):
        def one(t, _):
            t = t + i * (CHUNK // 2) + (t // (CHUNK // 2)) * (CHUNK // 2)
            for r_abs, src in quarters:
                rows = rows_of(r_abs)
                ext[2 * t, rows, :] = src[2 * t]
                ext[2 * t + 1, rows, :] = src[2 * t + 1]
            tile(t)
            return 0

        lax.fori_loop(0, CHUNK, one, 0)

    copies = [pack(0, own)]
    prod[EXT] = jnp.zeros((OFFSETS * LOC, BLOCK), F32)
    extt_ref[EXT] = jnp.zeros((BLOCK, CH), BF16)
    low = lax.broadcasted_iota(jnp.int32, (LOC, BLOCK), 1) < LOC
    for p in range(WPAD // BLOCK):
        for h in range(2):
            cols = pl.ds(h * BLOCK, BLOCK)
            first = w_ref[pl.ds(2 * p * LOC, LOC), cols].astype(F32)
            if 2 * p + 1 < OFFSETS:
                second = w_ref[pl.ds((2 * p + 1) * LOC, LOC), cols].astype(F32)
            else:
                second = jnp.zeros((LOC, BLOCK), F32)
            put = pl.ds(p * BLOCK, BLOCK)
            parts_ref[2 * h, :, put] = jnp.where(low, first, pltpu.roll(second, LOC, 1)).astype(BF16)
            parts_ref[2 * h + 1, :, put] = jnp.where(low, pltpu.roll(first, LOC, 1), second).astype(BF16)
    gather.forward(0)
    gather.forward(1)
    gather.wait_part(0)
    part_tiles(0)
    gather.wait_part(1)
    copies.append(pack(1, from_dn))
    copies.append(pack(2, from_up))
    copies.append(pack(3, opp))
    part_tiles(1)
    keep_below = jnp.where(b > 0, 1.0, 0.0)
    keep_above = jnp.where(b < NBOX - 1, 1.0, 0.0)
    for r, (r_abs, _) in enumerate(quarters):
        up, dn = copies[r]
        up.wait_recv()
        dn.wait_recv()
        rows = rows_of(r_abs)
        for s in range(SLOTS):
            ext[BLOCKS + s, rows, :] = (fin[r, 0, s].astype(F32) * keep_below).astype(BF16)
            ext[BLOCKS + SLOTS + s, rows, :] = (fin[r, 1, s].astype(F32) * keep_above).astype(BF16)

    def face_tile(t, _):
        tile(t)
        return 0

    lax.fori_loop(BLOCKS // 2, EXT // 2, face_tile, 0)

    def out(j, carry):
        a, s = carry
        acc = prod[map_ref[j], pl.ds(0, LOC), :]
        for k in range(1, OFFSETS):
            acc = acc + prod[map_ref[k * BLOCKS + j], pl.ds(LOC * k, LOC), :]
        conv_ref[j] = acc
        o = occ_ref[j] * acc
        return a + o, s + o * acc

    zero = jnp.zeros((LOC, BLOCK), F32)
    a, s = lax.fori_loop(0, BLOCKS, out, (zero, zero))
    sum_ref[0] = a
    sum_ref[1] = s
    gather.wait_sends()
    for up, dn in copies:
        up.wait_send()
        dn.wait_send()


def conv_call(send, kmap, features, occ, w):
    quarter = pltpu.VMEM((BLOCKS, LOC, BLOCK), BF16)
    faces = pltpu.VMEM((4, 2, SLOTS, LOC, BLOCK), BF16)
    dma = pltpu.SemaphoreType.DMA
    return pl.pallas_call(
        conv_kernel,
        out_shape=(
            jax.ShapeDtypeStruct((BLOCKS, LOC, BLOCK), F32),
            jax.ShapeDtypeStruct((2, LOC, BLOCK), F32),
            jax.ShapeDtypeStruct((EXT + 1, BLOCK, CH), BF16),
            jax.ShapeDtypeStruct((4, LOC, WPAD), BF16),
        ),
        in_specs=[SMEM, SMEM, VMEM, VMEM, VMEM],
        out_specs=(VMEM,) * 4,
        scratch_shapes=[
            quarter,
            quarter,
            quarter,
            quarter,
            faces,
            faces,
            pltpu.VMEM((EXT, CH, BLOCK), BF16),
            pltpu.VMEM((EXT + 1, OFFSETS * LOC, BLOCK), F32),
            dma((12,)),
            dma((12,)),
            dma((4, 2)),
            dma((4, 2)),
        ],
        compiler_params=params(1),
        name="conv",
    )(send, kmap, features, occ, w)


def lane_masks():
    ch = lax.broadcasted_iota(jnp.int32, (LOC, BLOCK), 0)
    lane = lax.broadcasted_iota(jnp.int32, (LOC, BLOCK), 1)
    return lane == ch, lane == ch + LOC


def to_row(first, second):
    m0, m1 = lane_masks()
    c0 = jnp.sum(first, axis=1, keepdims=True)
    c1 = jnp.sum(second, axis=1, keepdims=True)
    return jnp.sum(jnp.where(m0, c0, 0.0) + jnp.where(m1, c1, 0.0), axis=0, keepdims=True)


def to_cols(row):
    m0, m1 = lane_masks()
    return (
        jnp.sum(jnp.where(m0, row, 0.0), axis=1, keepdims=True),
        jnp.sum(jnp.where(m1, row, 0.0), axis=1, keepdims=True),
    )


def at_box(x, z, core):
    return {"box": x * 16 + z * 2 + core}


def box_groups():
    b = lax.axis_index("box")
    x, z, core = b // 16, lax.rem(b // 2, 8), lax.rem(b, 2)
    first = [at_box(lax.rem(x + d // 2, 4), z, lax.rem(core + d % 2, 2)) for d in range(1, 8)]
    second = [at_box(x, lax.rem(z + d, 8), core) for d in range(1, 8)]
    return (x * 2 + core, first), (z, second)


def box_sum(mine, buf, ssem, rsem, idle=None):
    sent = []
    for step, (me, peers) in enumerate(box_groups()):
        buf[step, me] = mine
        copies = []
        for d, dev in enumerate(peers):
            c = rcopy(buf.at[step, me], buf.at[step, me], ssem.at[step, d], rsem.at[step, d], dev)
            c.start()
            copies.append(c)
        if idle is not None and step == 1:
            idle()
        for c in copies:
            c.wait_recv()
        mine = buf[step, 0]
        for d in range(1, 8):
            mine = mine + buf[step, d]
        sent += copies
    return mine, sent


def norm_kernel(
    map_ref,
    conv_ref,
    sum_ref,
    grad_ref,
    occ_ref,
    gs_ref,
    extt_ref,
    parts_ref,
    out_ref,
    cga_ref,
    wg_ref,
    stat_ref,
    win_ref,
    wrecv,
    normed,
    rgrad,
    own,
    from_dn,
    from_up,
    opp,
    sbuf,
    sbuf2,
    ysend,
    yrecv,
    ssend,
    srecv,
    wsend,
    wrecvs,
):
    q = lax.axis_index("ch")
    gather = YGather(own, from_dn, from_up, opp, ysend, yrecv)
    (_, near), (_, far) = box_groups()
    sub = lax.broadcasted_iota(jnp.int32, (2, BLOCK), 0)
    count = jnp.sum(occ_ref[...], axis=0)
    count = jnp.broadcast_to(jnp.sum(count, axis=1, keepdims=True), (1, BLOCK))
    row = to_row(sum_ref[0], sum_ref[1])
    pay = jnp.where(sub == 0, row, count)
    ypeers = [{"ch": lax.rem(q + d, 4)} for d in range(1, 4)]
    greet(ypeers + near + far)
    wcopies = []
    for d in range(1, 4):
        c = rcopy(parts_ref.at[lax.rem(q + d, 4)], wrecv.at[rows_of(q)], wsend.at[d - 1], wrecvs.at[d - 1], ypeers[d - 1])
        c.start()
        wcopies.append(c)
    wrecv[rows_of(q), :] = parts_ref[q]
    tot, sent = box_sum(pay, sbuf, ssend.at[0], srecv.at[0])
    n_vox = tot[1:2, 0:1]
    s1, s2 = to_cols(tot[0:1, :])
    mean = s1 / n_vox
    var = s2 / n_vox - mean * mean
    inv = 1.0 / jnp.sqrt(var + 1e-05)
    gain, shift = to_cols(gs_ref[...])

    def fwd(j, carry):
        a, b = carry
        cols = pl.ds(pl.multiple_of(j * BLOCK, BLOCK), BLOCK)
        occ = occ_ref[j]
        nd = (conv_ref[j] - mean) * inv
        sh = nd * gain + shift
        out_ref[:, cols] = (occ * jnp.maximum(sh, 0.0)).astype(BF16)
        rg = jnp.where(sh > 0.0, occ * grad_ref[:, cols].astype(F32), 0.0)
        normed[j] = nd
        rgrad[j] = rg
        return a + rg, b + rg * nd

    zero = jnp.zeros((LOC, BLOCK), F32)
    a, b = lax.fori_loop(0, BLOCKS, fwd, (zero, zero))
    row = to_row(a, b)

    def turn():
        for c in wcopies:
            c.wait_recv()
        for p in range(WPAD // BLOCK):
            win_ref[pl.ds(p * BLOCK, BLOCK), :] = wrecv[:, pl.ds(p * BLOCK, BLOCK)].T

    tot, sent2 = box_sum(row, sbuf2, ssend.at[1], srecv.at[1], turn)
    stat_ref[...] = tot
    sg, gg = to_cols(tot)
    scale = inv * gain
    sgm = sg / n_vox

    def bwd(j, _):
        nd = normed[j]
        own[j] = (occ_ref[j] * scale * (rgrad[j] - sgm - nd * gg / n_vox)).astype(BF16)
        return 0

    lax.fori_loop(0, BLOCKS, bwd, 0)
    gather.start()

    def kterm(k, _):
        lhs = jnp.concatenate([own[j] for j in range(BLOCKS)], axis=1)
        rhs = jnp.concatenate([extt_ref[map_ref[k * BLOCKS + j]] for j in range(BLOCKS)], axis=0)
        wg_ref[k] = jnp.dot(lhs, rhs, preferred_element_type=F32)
        return 0

    def place(r_abs, src):
        rows = rows_of(r_abs)

        def one(e, _):
            cga_ref[e, rows, :] = src[e]
            return 0

        lax.fori_loop(0, BLOCKS, one, 0)

    place(q, own)
    lax.fori_loop(0, 8, kterm, 0)
    gather.forward(0)
    lax.fori_loop(8, 14, kterm, 0)
    gather.forward(1)
    lax.fori_loop(14, OFFSETS, kterm, 0)
    gather.wait_part(0)
    gather.wait_part(1)
    place(lax.rem(q + 3, 4), from_dn)
    place(lax.rem(q + 1, 4), from_up)
    place(lax.rem(q + 2, 4), opp)
    gather.wait_sends()
    for c in wcopies + sent + sent2:
        c.wait_send()


def norm_call(kmap, conv, sums, out_grad, occ, gs, extt, parts):
    quarter = pltpu.VMEM((BLOCKS, LOC, BLOCK), BF16)
    return pl.pallas_call(
        norm_kernel,
        out_shape=(
            jax.ShapeDtypeStruct((LOC, BLOCKS * BLOCK), BF16),
            jax.ShapeDtypeStruct((BLOCKS, CH, BLOCK), BF16),
            jax.ShapeDtypeStruct((OFFSETS, LOC, CH), F32),
            jax.ShapeDtypeStruct((1, BLOCK), F32),
            jax.ShapeDtypeStruct((WPAD, CH), BF16),
        ),
        in_specs=[SMEM] + [VMEM] * 7,
        out_specs=(VMEM,) * 5,
        scratch_shapes=[
            pltpu.VMEM((CH, WPAD), BF16),
            pltpu.VMEM((BLOCKS, LOC, BLOCK), F32),
            pltpu.VMEM((BLOCKS, LOC, BLOCK), F32),
            quarter,
            quarter,
            quarter,
            quarter,
            pltpu.VMEM((2, 8, 2, BLOCK), F32),
            pltpu.VMEM((2, 8, 1, BLOCK), F32),
            pltpu.SemaphoreType.DMA((12,)),
            pltpu.SemaphoreType.DMA((12,)),
            pltpu.SemaphoreType.DMA((2, 2, 7)),
            pltpu.SemaphoreType.DMA((2, 2, 7)),
            pltpu.SemaphoreType.DMA((3,)),
            pltpu.SemaphoreType.DMA((3,)),
        ],
        compiler_params=params(2),
        name="norm",
    )(kmap, conv, sums, out_grad, occ, gs, extt, parts)


def back_kernel(map_ref, w_ref, cg_ref, eg_ref, prod, *accs):
    for a in accs:

        def zero(e, _):
            a[e] = jnp.zeros((LOC, BLOCK), F32)
            return 0

        lax.fori_loop(0, EXT + 1, zero, 0)

    def tile(t, _):
        rhs = jnp.concatenate([cg_ref[2 * t], cg_ref[2 * t + 1]], axis=1)
        res = jnp.dot(w_ref[pl.ds(0, OFFSETS * LOC), :], rhs, preferred_element_type=F32)
        prod[2 * t] = res[:, :BLOCK]
        prod[2 * t + 1] = res[:, BLOCK:]
        return 0

    lax.fori_loop(0, BLOCKS // 2, tile, 0)

    def scatter(t, _):
        for k in range(OFFSETS):
            at = [map_ref[k * BLOCKS + t * NA + i] for i in range(NA)]
            new = [accs[i][at[i]] + prod[t * NA + i, pl.ds(LOC * k, LOC), :] for i in range(NA)]
            for i in range(NA):
                accs[i][at[i]] = new[i]
        return 0

    lax.fori_loop(0, BLOCKS // NA, scatter, 0)

    def finish(e, _):
        s = accs[0][e]
        for a in accs[1:]:
            s = s + a[e]
        eg_ref[e] = s
        return 0

    lax.fori_loop(0, EXT, finish, 0)


def back_call(kmap, w, cga):
    return pl.pallas_call(
        back_kernel,
        out_shape=jax.ShapeDtypeStruct((EXT, LOC, BLOCK), F32),
        in_specs=[SMEM, VMEM, VMEM],
        out_specs=VMEM,
        scratch_shapes=[pltpu.VMEM((BLOCKS, OFFSETS * LOC, BLOCK), F32)]
        + [pltpu.VMEM((EXT + 1, LOC, BLOCK), F32)] * NA,
        compiler_params=params(),
        name="back",
    )(kmap, w, cga)


def final_kernel(
    send_ref,
    eg_ref,
    occ_ref,
    wg_ref,
    in_ref,
    wout_ref,
    fout,
    fin,
    give,
    given,
    keep,
    xbuf,
    xin,
    zbuf,
    zin,
    res,
    fsend,
    frecv,
    sem,
    sems,
):
    b = lax.axis_index("box")
    x, z, core = b // 16, lax.rem(b // 2, 8), lax.rem(b, 2)
    above = {"box": lax.rem(b + 1, NBOX)}
    below = {"box": lax.rem(b + NBOX - 1, NBOX)}
    mate = at_box(x, z, 1 - core)
    zpeers = [at_box(x, lax.rem(z + d, 8), core) for d in range(1, 8)]
    xpeers = [at_box(lax.rem(x + d, 4), z, core) for d in range(1, 4)]
    sent = []

    def send(src, dst, i, dev):
        c = rcopy(src, dst, sem.at[i], sems.at[i], dev)
        c.start()
        sent.append(c)
        return c

    def cut(k, _):
        rows = pl.ds(pl.multiple_of(k * LOC, LOC), LOC)
        lo, hi = wg_ref[k, :, :BLOCK], wg_ref[k, :, BLOCK:]
        keep[rows, :] = jnp.where(core == 0, lo, hi)
        give[rows, :] = jnp.where(core == 0, hi, lo).astype(BF16)
        return 0

    lax.fori_loop(0, OFFSETS, cut, 0)
    for s in range(SLOTS):
        fout[0, s] = eg_ref[BLOCKS + s].astype(BF16)
        fout[1, s] = eg_ref[BLOCKS + SLOTS + s].astype(BF16)
    greet([above, below, mate] + zpeers + xpeers)
    pair = send(give, given, 0, mate)
    f0 = rcopy(fout.at[0], fin.at[0], fsend.at[0], frecv.at[0], below)
    f1 = rcopy(fout.at[1], fin.at[1], fsend.at[1], frecv.at[1], above)
    f0.start()
    f1.start()
    sent += [f0, f1]
    xbuf[pl.ds(OFFSETS * LOC, WROWS - OFFSETS * LOC), :] = jnp.zeros((WROWS - OFFSETS * LOC, BLOCK), BF16)
    pair.wait_recv()

    def add(k, _):
        rows = pl.ds(pl.multiple_of(k * LOC, LOC), LOC)
        xbuf[rows, :] = (keep[rows, :] + given[rows, :].astype(F32)).astype(BF16)
        return 0

    lax.fori_loop(0, OFFSETS, add, 0)
    xpart = lambda i: pl.ds(pl.multiple_of(i * XROWS, XROWS), XROWS)
    zpart = lambda i: pl.ds(pl.multiple_of(i * ZROWS, ZROWS), ZROWS)
    xc = [send(xbuf.at[xpart(lax.rem(x + d, 4))], xin.at[d - 1], d, xpeers[d - 1]) for d in range(1, 4)]
    for c in xc:
        c.wait_recv()
    tot = xbuf[xpart(x), :].astype(F32)
    for d in range(3):
        tot = tot + xin[d].astype(F32)
    zbuf[...] = tot.astype(BF16)
    zc = [send(zbuf.at[zpart(lax.rem(z + d, 8))], zin.at[d - 1], 3 + d, zpeers[d - 1]) for d in range(1, 8)]

    f0.wait_recv()
    f1.wait_recv()
    up_ok = b < NBOX - 1
    dn_ok = b > 0

    def settle(d, _):
        t = eg_ref[d]
        for s in range(SLOTS):
            t = t + jnp.where((send_ref[SLOTS + s] == d) & up_ok, fin[0, s].astype(F32), 0.0)
            t = t + jnp.where((send_ref[s] == d) & dn_ok, fin[1, s].astype(F32), 0.0)
        in_ref[:, pl.ds(pl.multiple_of(d * BLOCK, BLOCK), BLOCK)] = (occ_ref[d] * t).astype(BF16)
        return 0

    lax.fori_loop(0, BLOCKS, settle, 0)

    for c in zc:
        c.wait_recv()
    tot = zbuf[zpart(z), :].astype(F32)
    for d in range(7):
        tot = tot + zin[d].astype(F32)
    mine = pl.ds(pl.multiple_of(x * XROWS + z * ZROWS, ZROWS), ZROWS)
    res[0, mine, :] = tot.astype(BF16)
    zc = [send(res.at[0, mine], res.at[0, mine], 10 + d, zpeers[d - 1]) for d in range(1, 8)]
    for c in zc:
        c.wait_recv()
    xc = [send(res.at[0, xpart(x)], res.at[0, xpart(x)], 17 + d, xpeers[d - 1]) for d in range(1, 4)]
    for c in xc:
        c.wait_recv()
    valid = pl.ds(0, OFFSETS * LOC)
    pair = send(res.at[0, valid], res.at[1, valid], 21, mate)
    pair.wait_recv()

    def put(k, _):
        r = pl.ds(pl.multiple_of(k * LOC, LOC), LOC)
        m = res[0, r, :].astype(F32)
        o = res[1, r, :].astype(F32)
        wout_ref[k, :, :BLOCK] = jnp.where(core == 0, m, o)
        wout_ref[k, :, BLOCK:] = jnp.where(core == 0, o, m)
        return 0

    lax.fori_loop(0, OFFSETS, put, 0)
    for c in sent:
        c.wait_send()


def final_call(send, eg, occ, wg):
    dma = pltpu.SemaphoreType.DMA
    return pl.pallas_call(
        final_kernel,
        out_shape=(
            jax.ShapeDtypeStruct((LOC, BLOCKS * BLOCK), BF16),
            jax.ShapeDtypeStruct((OFFSETS, LOC, CH), F32),
        ),
        in_specs=[SMEM, VMEM, VMEM, VMEM],
        out_specs=(VMEM, VMEM),
        scratch_shapes=[
            pltpu.VMEM((2, SLOTS, LOC, BLOCK), BF16),
            pltpu.VMEM((2, SLOTS, LOC, BLOCK), BF16),
            pltpu.VMEM((OFFSETS * LOC, BLOCK), BF16),
            pltpu.VMEM((OFFSETS * LOC, BLOCK), BF16),
            pltpu.VMEM((OFFSETS * LOC, BLOCK), F32),
            pltpu.VMEM((WROWS, BLOCK), BF16),
            pltpu.VMEM((3, XROWS, BLOCK), BF16),
            pltpu.VMEM((XROWS, BLOCK), BF16),
            pltpu.VMEM((7, ZROWS, BLOCK), BF16),
            pltpu.VMEM((2, WROWS, BLOCK), BF16),
            dma((2,)),
            dma((2,)),
            dma((22,)),
            dma((22,)),
        ],
        compiler_params=params(3),
        name="final",
    )(send, eg, occ, wg)


def per_device(
    features, occupied, send_lists, kernel_map, weights, norm_gain, norm_shift, out_grad
):
    occ = occupied.astype(F32).reshape(BLOCKS, 1, BLOCK)
    send = send_lists.reshape(2 * SLOTS)
    kmap = kernel_map.reshape(OFFSETS * BLOCKS)
    w = weights.reshape(OFFSETS * LOC, CH)
    gs = jnp.concatenate([norm_gain, norm_shift]).reshape(1, BLOCK)

    conv, sums, extt, parts = conv_call(send, kmap, features, occ, w)
    out_features, cga, wg, stat, w_in = norm_call(kmap, conv, sums, out_grad, occ, gs, extt, parts)
    eg = back_call(kmap, w_in, cga)
    in_grad, weight_grad = final_call(send, eg, occ, wg)
    return (out_features, in_grad, weight_grad, stat[0, LOC:], stat[0, :LOC])


def solution(mesh):
    in_specs = (
        P("ch", "box"),
        P("box"),
        P("box", None, None),
        P("box", None, None),
        P(None, "ch", None),
        P("ch"),
        P("ch"),
        P("ch", "box"),
    )
    out_specs = (P("ch", "box"), P("ch", "box"), P(None, "ch", None), P("ch"), P("ch"))
    return jax.shard_map(
        per_device, mesh=mesh, in_specs=in_specs, out_specs=out_specs, check_vma=False
    )
```

```python
import functools

import jax
import jax.numpy as jnp
from jax import lax
from jax.experimental import pallas as pl
from jax.experimental.pallas import tpu as pltpu
from jax.sharding import PartitionSpec as P

F32 = jnp.float32
BF16 = jnp.bfloat16
MESH = pl.DeviceIdType.MESH
VMEM = pl.BlockSpec(memory_space=pltpu.VMEM)
SMEM = pl.BlockSpec(memory_space=pltpu.SMEM)
VMEM_LIMIT = 62 * 2**20

BLOCK = 128
BLOCKS = 32
CHUNK = 8
SLOTS = 8
EXT = BLOCKS + 2 * SLOTS
OFFSETS = 27
CH = 256
LOC = 64
WPAD = 1792
KHALF = 14
KCOUNT = (14, 13)
WROWS = 1024
XROWS = WROWS // 4
ZROWS = XROWS // 8
NBOX = 64
HROWS = 32
WALK = 16


def params(cid=None):
    if cid is None:
        return pltpu.CompilerParams(vmem_limit_bytes=VMEM_LIMIT)
    return pltpu.CompilerParams(
        vmem_limit_bytes=VMEM_LIMIT, collective_id=cid, has_side_effects=True
    )


def rcopy(src, dst, ssem, rsem, dev):
    return pltpu.make_async_remote_copy(
        src_ref=src, dst_ref=dst, send_sem=ssem, recv_sem=rsem, device_id=dev, device_id_type=MESH
    )


def greet(devs):
    barrier = pltpu.get_barrier_semaphore()
    for dev in devs:
        pl.semaphore_signal(barrier, inc=1, device_id=dev, device_id_type=MESH)
    pl.semaphore_wait(barrier, len(devs))


def occ_of(occ_ref, j):
    return occ_ref[j].astype(F32)


def rows_of(q):
    return pl.ds(pl.multiple_of(q * LOC, LOC), LOC)


class YGather:
    def __init__(self, own, from_dn, from_up, opp, ssem, rsem):
        q = lax.axis_index("ch")
        self.up = {"ch": lax.rem(q + 1, 4)}
        self.dn = {"ch": lax.rem(q + 3, 4)}

        def mk(src, dst, chunk, i, dev):
            part = pl.ds(chunk * CHUNK, CHUNK)
            return rcopy(src.at[part], dst.at[part], ssem.at[i], rsem.at[i], dev)

        self.own_up = [mk(own, from_dn, c, c, self.up) for c in range(4)]
        self.own_dn = [mk(own, from_up, c, 4 + c, self.dn) for c in range(4)]
        self.far_up = [mk(from_dn, opp, c, 8 + c, self.up) for c in (0, 1)]
        self.far_dn = [mk(from_up, opp, c, 8 + c, self.dn) for c in (2, 3)]

    def start(self):
        self.own_up[0].start()
        self.own_dn[2].start()
        self.own_up[1].start()
        self.own_dn[3].start()

    def forward(self, i):
        self.own_up[i].wait_recv()
        self.far_up[i].start()
        self.own_up[2 + i].start()
        self.own_dn[2 + i].wait_recv()
        self.far_dn[i].start()
        self.own_dn[i].start()

    def wait_part(self, i):
        self.own_up[2 + i].wait_recv()
        self.own_dn[i].wait_recv()
        self.far_up[i].wait_recv()
        self.far_dn[i].wait_recv()

    def wait_sends(self):
        for c in self.own_up + self.own_dn + self.far_up + self.far_dn:
            c.wait_send()


def rank_pairs(map_ref):
    at = lax.broadcasted_iota(jnp.int32, (8, BLOCK), 0) * BLOCK + lax.broadcasted_iota(jnp.int32, (8, BLOCK), 1)

    def fill(k, target):
        for j in range(BLOCKS):
            target = jnp.where(at == k * BLOCKS + j, map_ref[0, k, j], target)
        return target

    target = lax.fori_loop(0, OFFSETS, fill, jnp.full((8, BLOCK), 63, jnp.int32))
    keys = target * 1024 + at

    def count(k, rank):
        for j in range(BLOCKS):
            rank = rank + (keys > map_ref[0, k, j] * 1024 + (k * BLOCKS + j)).astype(jnp.int32)
        return rank

    return target, lax.fori_loop(0, OFFSETS, count, jnp.zeros((8, BLOCK), jnp.int32))


def sort_pairs(target, rank):
    lane = lax.broadcasted_iota(jnp.int32, (BLOCK, BLOCK), 1)
    sub = lax.broadcasted_iota(jnp.int32, (BLOCK, BLOCK), 0)
    pair = [jnp.zeros((1, BLOCK), F32) for _ in range(7)]
    goal = [jnp.zeros((1, BLOCK), F32) for _ in range(7)]
    last = jnp.full((1, BLOCK), -1.0, F32)
    for s in range(7):
        rcol = jnp.broadcast_to(rank[s : s + 1, :].astype(F32), (BLOCK, BLOCK)).T
        tcol = jnp.broadcast_to(target[s : s + 1, :].astype(F32), (BLOCK, BLOCK)).T
        i = sub + s * BLOCK
        number = (lax.rem(i, BLOCKS) * (2 * OFFSETS) + 2 * (i // BLOCKS)).astype(F32)
        for r in range(7):
            hit = rcol == (lane + r * BLOCK).astype(F32)
            pair[r] = pair[r] + jnp.sum(jnp.where(hit, number, 0.0), axis=0, keepdims=True)
            goal[r] = goal[r] + jnp.sum(jnp.where(hit, tcol, 0.0), axis=0, keepdims=True)
        mine = tcol == lane.astype(F32)
        last = jnp.maximum(last, jnp.max(jnp.where(mine, rcol, -1.0), axis=0, keepdims=True))
    fresh = []
    first = lax.broadcasted_iota(jnp.int32, (1, BLOCK), 1) == 0
    for r in range(7):
        before = pltpu.roll(goal[r], 1, 1)
        carry = pltpu.roll(goal[r - 1], 1, 1) if r else jnp.full((1, BLOCK), -1.0, F32)
        before = jnp.where(first, carry, before)
        fresh.append(jnp.where(goal[r] == before, 0.0, 1.0))
    some = [jnp.where(last >= 0.0, 1.0, 0.0)]
    return jnp.concatenate(pair + [jnp.maximum(last, 0.0)] + fresh + some, axis=0).astype(jnp.int32)


def conv_kernel(
    send_ref,
    map_ref,
    feat_ref,
    occ_ref,
    w_ref,
    conv_ref,
    sum_ref,
    ext,
    parts_ref,
    meta_ref,
    own,
    from_dn,
    from_up,
    opp,
    fout,
    fin,
    prod,
    ysend,
    yrecv,
    fsend,
    frecv,
):
    q = lax.axis_index("ch")
    b = lax.axis_index("box")
    above = {"box": lax.rem(b + 1, NBOX)}
    below = {"box": lax.rem(b + NBOX - 1, NBOX)}
    gather = YGather(own, from_dn, from_up, opp, ysend, yrecv)
    quarters = ((q, own), (lax.rem(q + 3, 4), from_dn), (lax.rem(q + 1, 4), from_up), (lax.rem(q + 2, 4), opp))

    def mask(e, _):
        x = feat_ref[:, pl.ds(pl.multiple_of(e * BLOCK, BLOCK), BLOCK)].astype(F32)
        own[e] = (x * occ_of(occ_ref, e)).astype(BF16)
        return 0

    lax.fori_loop(0, BLOCKS, mask, 0)
    greet([gather.up, gather.dn, above, below])
    gather.start()

    def pack(r, src):
        for d in range(2):
            for s in range(SLOTS):
                pick = send_ref[0, d, s]
                blk = src[jnp.minimum(pick, BLOCKS - 1)].astype(F32)
                fout[r, d, s] = jnp.where(pick < BLOCKS, blk, 0.0).astype(BF16)
        up = rcopy(fout.at[r, 1], fin.at[r, 0], fsend.at[r, 1], frecv.at[r, 0], above)
        dn = rcopy(fout.at[r, 0], fin.at[r, 1], fsend.at[r, 0], frecv.at[r, 1], below)
        up.start()
        dn.start()
        return up, dn

    def tile(t):
        rhs = jnp.concatenate([ext[2 * t], ext[2 * t + 1]], axis=1)
        res = jnp.dot(w_ref[...], rhs, preferred_element_type=F32)
        prod[2 * t] = res[:, :BLOCK]
        prod[2 * t + 1] = res[:, BLOCK:]

    def part_tiles(i):
        def one(t, _):
            t = t + i * (CHUNK // 2) + (t // (CHUNK // 2)) * (CHUNK // 2)
            for r_abs, src in quarters:
                rows = rows_of(r_abs)
                ext[2 * t, rows, :] = src[2 * t]
                ext[2 * t + 1, rows, :] = src[2 * t + 1]
            tile(t)
            return 0

        lax.fori_loop(0, CHUNK, one, 0)

    copies = [pack(0, own)]
    prod[EXT] = jnp.zeros((OFFSETS * LOC, BLOCK), F32)
    ext[EXT] = jnp.zeros((CH, BLOCK), BF16)
    low = lax.broadcasted_iota(jnp.int32, (LOC, BLOCK), 1) < LOC
    for p in range(WPAD // BLOCK):
        for h in range(2):
            cols = pl.ds(h * BLOCK, BLOCK)
            first = w_ref[pl.ds(2 * p * LOC, LOC), cols].astype(F32)
            if 2 * p + 1 < OFFSETS:
                second = w_ref[pl.ds((2 * p + 1) * LOC, LOC), cols].astype(F32)
            else:
                second = jnp.zeros((LOC, BLOCK), F32)
            put = pl.ds(p * BLOCK, BLOCK)
            parts_ref[2 * h, :, put] = jnp.where(low, first, pltpu.roll(second, LOC, 1)).astype(BF16)
            parts_ref[2 * h + 1, :, put] = jnp.where(low, pltpu.roll(first, LOC, 1), second).astype(BF16)
    gather.forward(0)
    ranks = rank_pairs(map_ref)
    gather.forward(1)
    meta_ref[...] = sort_pairs(*ranks)
    gather.wait_part(0)
    part_tiles(0)
    gather.wait_part(1)
    copies.append(pack(1, from_dn))
    copies.append(pack(2, from_up))
    copies.append(pack(3, opp))
    part_tiles(1)
    keep_below = jnp.where(b > 0, 1.0, 0.0)
    keep_above = jnp.where(b < NBOX - 1, 1.0, 0.0)
    for r, (r_abs, _) in enumerate(quarters):
        up, dn = copies[r]
        up.wait_recv()
        dn.wait_recv()
        rows = rows_of(r_abs)
        for s in range(SLOTS):
            ext[BLOCKS + s, rows, :] = (fin[r, 0, s].astype(F32) * keep_below).astype(BF16)
            ext[BLOCKS + SLOTS + s, rows, :] = (fin[r, 1, s].astype(F32) * keep_above).astype(BF16)

    def face_tile(t, _):
        tile(t)
        return 0

    lax.fori_loop(BLOCKS // 2, EXT // 2, face_tile, 0)

    def out(j, carry):
        a, s = carry
        acc = prod[map_ref[0, 0, j], pl.ds(0, LOC), :]
        for k in range(1, OFFSETS):
            acc = acc + prod[map_ref[0, k, j], pl.ds(LOC * k, LOC), :]
        conv_ref[j] = acc
        o = occ_of(occ_ref, j) * acc
        return a + o, s + o * acc

    zero = jnp.zeros((LOC, BLOCK), F32)
    a, s = lax.fori_loop(0, BLOCKS, out, (zero, zero))
    sum_ref[0] = a
    sum_ref[1] = s
    gather.wait_sends()
    for up, dn in copies:
        up.wait_send()
        dn.wait_send()


def conv_call(send, kmap, features, occ, w):
    quarter = pltpu.VMEM((BLOCKS, LOC, BLOCK), BF16)
    faces = pltpu.VMEM((4, 2, SLOTS, LOC, BLOCK), BF16)
    dma = pltpu.SemaphoreType.DMA
    return pl.pallas_call(
        conv_kernel,
        out_shape=(
            jax.ShapeDtypeStruct((BLOCKS, LOC, BLOCK), F32),
            jax.ShapeDtypeStruct((2, LOC, BLOCK), F32),
            jax.ShapeDtypeStruct((EXT + 1, CH, BLOCK), BF16),
            jax.ShapeDtypeStruct((4, LOC, WPAD), BF16),
            jax.ShapeDtypeStruct((16, BLOCK), jnp.int32),
        ),
        in_specs=[SMEM, SMEM, VMEM, VMEM, VMEM],
        out_specs=(VMEM,) * 5,
        scratch_shapes=[
            quarter,
            quarter,
            quarter,
            quarter,
            faces,
            faces,
            pltpu.VMEM((EXT + 1, OFFSETS * LOC, BLOCK), F32),
            dma((12,)),
            dma((12,)),
            dma((4, 2)),
            dma((4, 2)),
        ],
        compiler_params=params(1),
        name="conv",
    )(send, kmap, features, occ, w)


def lane_masks():
    ch = lax.broadcasted_iota(jnp.int32, (LOC, BLOCK), 0)
    lane = lax.broadcasted_iota(jnp.int32, (LOC, BLOCK), 1)
    return lane == ch, lane == ch + LOC


def to_row(first, second):
    m0, m1 = lane_masks()
    c0 = jnp.sum(first, axis=1, keepdims=True)
    c1 = jnp.sum(second, axis=1, keepdims=True)
    return jnp.sum(jnp.where(m0, c0, 0.0) + jnp.where(m1, c1, 0.0), axis=0, keepdims=True)


def to_cols(row):
    m0, m1 = lane_masks()
    return (
        jnp.sum(jnp.where(m0, row, 0.0), axis=1, keepdims=True),
        jnp.sum(jnp.where(m1, row, 0.0), axis=1, keepdims=True),
    )


def at_box(x, z, core):
    return {"box": x * 16 + z * 2 + core}


def to_col(row):
    ch = lax.broadcasted_iota(jnp.int32, (LOC, LOC), 0)
    lane = lax.broadcasted_iota(jnp.int32, (LOC, LOC), 1)
    return jnp.sum(jnp.where(ch == lane, row, 0.0), axis=1, keepdims=True)


def box_groups():
    b = lax.axis_index("box")
    x, z, core = b // 16, lax.rem(b // 2, 8), lax.rem(b, 2)
    first = [at_box(lax.rem(x + d // 2, 4), z, lax.rem(core + d % 2, 2)) for d in range(1, 8)]
    second = [at_box(x, lax.rem(z + d, 8), core) for d in range(1, 8)]
    return (x * 2 + core, first), (z, second)


def box_sum(mine, buf, ssem, rsem, idle):
    sent = []
    for step, (me, peers) in enumerate(box_groups()):
        buf[step, me] = mine
        copies = []
        for d, dev in enumerate(peers):
            c = rcopy(buf.at[step, me], buf.at[step, me], ssem.at[step, d], rsem.at[step, d], dev)
            c.start()
            copies.append(c)
        idle(step)
        for c in copies:
            c.wait_recv()
        mine = buf[step, 0]
        for d in range(1, 8):
            mine = mine + buf[step, d]
        sent += copies
    return mine, sent


def norm_kernel(
    send_ref,
    map_ref,
    meta_ref,
    conv_ref,
    sum_ref,
    grad_ref,
    occ_ref,
    gain_ref,
    shift_ref,
    ext_ref,
    parts_ref,
    out_ref,
    in_ref,
    wout_ref,
    stat_ref,
    extt,
    wg,
    wrecv,
    win,
    prod,
    run,
    eg,
    own,
    from_dn,
    from_up,
    opp,
    sbuf,
    sbuf2,
    fout,
    fin,
    give,
    given,
    xbuf,
    xin,
    zbuf,
    zin,
    res,
    ysend,
    yrecv,
    ssend,
    srecv,
    wsend,
    wrecvs,
    fsend,
    frecv,
    gsend,
    grecv,
):
    q = lax.axis_index("ch")
    b = lax.axis_index("box")
    x, z, core = b // 16, lax.rem(b // 2, 8), lax.rem(b, 2)
    gather = YGather(own, from_dn, from_up, opp, ysend, yrecv)
    (_, near), (_, far) = box_groups()
    ypeers = [{"ch": lax.rem(q + d, 4)} for d in range(1, 4)]
    above = {"box": lax.rem(b + 1, NBOX)}
    below = {"box": lax.rem(b + NBOX - 1, NBOX)}
    mate = at_box(x, z, 1 - core)
    xpeers = [at_box(lax.rem(x + d, 4), z, core) for d in range(1, 4)]
    zpeers = far
    sent = []

    count = jnp.sum(occ_ref[...].astype(F32), axis=0)
    count = jnp.broadcast_to(jnp.sum(count, axis=1, keepdims=True), (1, BLOCK))
    row = to_row(sum_ref[0], sum_ref[1])
    sub = lax.broadcasted_iota(jnp.int32, (2, BLOCK), 0)
    pay = jnp.where(sub == 0, row, count)
    greet(ypeers + near + far + [above, below])
    wcopies = []
    for d, slot in ((1, 1), (3, 2), (2, 3)):
        dst = wrecv.at[pl.ds(slot * LOC, LOC)]
        c = rcopy(parts_ref.at[lax.rem(q + d, 4)], dst, wsend.at[d - 1], wrecvs.at[d - 1], ypeers[d - 1])
        c.start()
        wcopies.append(c)
    wrecv[pl.ds(0, LOC), :] = parts_ref[q]

    def flip(step):
        def one(e, _):
            extt[e] = ext_ref[e].T
            return 0

        lax.fori_loop(*((0, EXT // 2) if step == 0 else (EXT // 2, EXT + 1)), one, 0)

    tot, more = box_sum(pay, sbuf, ssend.at[0], srecv.at[0], flip)
    sent += wcopies + more
    n_vox = tot[1:2, 0:1]
    s1, s2 = to_cols(tot[0:1, :])
    mean = s1 / n_vox
    var = s2 / n_vox - mean * mean
    inv = 1.0 / jnp.sqrt(var + 1e-05)
    gain, shift = to_col(gain_ref[...]), to_col(shift_ref[...])

    def fwd(j, carry):
        a, s = carry
        cols = pl.ds(pl.multiple_of(j * BLOCK, BLOCK), BLOCK)
        occ = occ_of(occ_ref, j)
        nd = (conv_ref[j] - mean) * inv
        sh = nd * gain + shift
        out_ref[:, cols] = (occ * jnp.maximum(sh, 0.0)).astype(BF16)
        rg = jnp.where(sh > 0.0, occ * grad_ref[:, cols].astype(F32), 0.0)
        prod[pl.ds(4 * j, 2)] = nd.reshape(2, HROWS, BLOCK)
        prod[pl.ds(4 * j + 2, 2)] = rg.reshape(2, HROWS, BLOCK)
        return a + rg, s + rg * nd

    zero = jnp.zeros((LOC, BLOCK), F32)
    a, s = lax.fori_loop(0, BLOCKS, fwd, (zero, zero))
    row = to_row(a, s)

    def turn(step):
        if step == 0:
            return
        for c in wcopies:
            c.wait_recv()
        for p in range(WPAD // BLOCK):
            win[pl.ds(p * BLOCK, BLOCK), :] = wrecv[:, pl.ds(p * BLOCK, BLOCK)].T

    tot, more = box_sum(row, sbuf2, ssend.at[1], srecv.at[1], turn)
    sent += more
    stat_ref[...] = tot
    sg, gg = to_cols(tot)
    scale = inv * gain
    sgm = sg / n_vox

    def bwd(j, _):
        nd = prod[pl.ds(4 * j, 2)].reshape(LOC, BLOCK)
        rg = prod[pl.ds(4 * j + 2, 2)].reshape(LOC, BLOCK)
        own[j] = (occ_of(occ_ref, j) * scale * (rg - sgm - nd * gg / n_vox)).astype(BF16)
        return 0

    lax.fori_loop(0, BLOCKS, bwd, 0)
    gather.start()

    def kterm(k, _):
        lhs = jnp.concatenate([own[j] for j in range(BLOCKS)], axis=1)
        rhs = jnp.concatenate([extt[map_ref[0, k, j]] for j in range(BLOCKS)], axis=0)
        wg[k] = jnp.dot(lhs, rhs, preferred_element_type=F32)
        return 0

    def send(src, dst, h, i, dev):
        c = rcopy(src, dst, gsend.at[h, i], grecv.at[h, i], dev)
        c.start()
        sent.append(c)
        return c

    flight = [None, None]
    xpart = lambda i: pl.ds(pl.multiple_of(i * XROWS, XROWS), XROWS)
    zpart = lambda i: pl.ds(pl.multiple_of(i * ZROWS, ZROWS), ZROWS)
    mine = pl.ds(pl.multiple_of(x * XROWS + z * ZROWS, ZROWS), ZROWS)

    def arrive(h):
        for c in flight[h]:
            c.wait_recv()

    def each_k(h, body):
        def one(k, _):
            body(k + h * KHALF, pl.ds(pl.multiple_of(k * LOC, LOC), LOC))
            return 0

        lax.fori_loop(0, KCOUNT[h], one, 0)

    def step0(h):
        def cut(k, rows):
            give[h, rows, :] = jnp.where(core == 0, wg[k, :, BLOCK:], wg[k, :, :BLOCK]).astype(BF16)

        each_k(h, cut)
        rows = pl.ds(0, KCOUNT[h] * LOC)
        flight[h] = [send(give.at[h, rows], given.at[h, rows], h, 0, mate)]

    def step1(h):
        arrive(h)

        def add(k, rows):
            keep = jnp.where(core == 0, wg[k, :, :BLOCK], wg[k, :, BLOCK:])
            xbuf[h, rows, :] = (keep + given[h, rows, :].astype(F32)).astype(BF16)

        each_k(h, add)
        rest = pl.ds(KCOUNT[h] * LOC, WROWS - KCOUNT[h] * LOC)
        xbuf[h, rest, :] = jnp.zeros((WROWS - KCOUNT[h] * LOC, BLOCK), BF16)
        flight[h] = [
            send(xbuf.at[h, xpart(lax.rem(x + d, 4))], xin.at[h, d - 1], h, d, xpeers[d - 1]) for d in range(1, 4)
        ]

    def step2(h):
        arrive(h)
        t = xbuf[h, xpart(x), :].astype(F32)
        for d in range(3):
            t = t + xin[h, d].astype(F32)
        zbuf[h] = t.astype(BF16)
        flight[h] = [
            send(zbuf.at[h, zpart(lax.rem(z + d, 8))], zin.at[h, d - 1], h, 3 + d, zpeers[d - 1]) for d in range(1, 8)
        ]

    def step3(h):
        arrive(h)
        t = zbuf[h, zpart(z), :].astype(F32)
        for d in range(7):
            t = t + zin[h, d].astype(F32)
        res[h, 0, mine, :] = t.astype(BF16)
        flight[h] = [
            send(res.at[h, 0, mine], res.at[h, 0, mine], h, 10 + d, zpeers[d - 1]) for d in range(1, 8)
        ]

    def step4(h):
        arrive(h)
        part = xpart(x)
        flight[h] = [
            send(res.at[h, 0, part], res.at[h, 0, part], h, 17 + d, xpeers[d - 1]) for d in range(1, 4)
        ]

    def step5(h):
        arrive(h)
        rows = pl.ds(0, KCOUNT[h] * LOC)
        flight[h] = [send(res.at[h, 0, rows], res.at[h, 1, rows], h, 21, mate)]

    def step6(h):
        arrive(h)

        def put(k, rows):
            m, o = res[h, 0, rows, :], res[h, 1, rows, :]
            wout_ref[k, :, :BLOCK] = jnp.where(core == 0, m, o)
            wout_ref[k, :, BLOCK:] = jnp.where(core == 0, o, m)

        each_k(h, put)

    lax.fori_loop(0, 8, kterm, 0)
    gather.forward(0)
    lax.fori_loop(8, KHALF, kterm, 0)
    step0(0)
    gather.forward(1)
    lax.fori_loop(KHALF, 19, kterm, 0)
    step1(0)
    lax.fori_loop(19, OFFSETS, kterm, 0)
    step0(1)
    gather.wait_part(0)
    gather.wait_part(1)
    step2(0)
    step1(1)

    def tile(t, _):
        halves = []
        for e in (2 * t, 2 * t + 1):
            halves.append(jnp.concatenate([own[e], from_dn[e], from_up[e], opp[e]], axis=0))
        rhs = jnp.concatenate(halves, axis=1)
        r = jnp.dot(win[pl.ds(0, OFFSETS * LOC), :], rhs, preferred_element_type=F32)
        place = 4 * OFFSETS * t
        prod[pl.ds(place, 2 * OFFSETS)] = r[:, :BLOCK].reshape(2 * OFFSETS, HROWS, BLOCK)
        prod[pl.ds(place + 2 * OFFSETS, 2 * OFFSETS)] = r[:, BLOCK:].reshape(2 * OFFSETS, HROWS, BLOCK)
        return 0

    lax.fori_loop(0, BLOCKS // 4, tile, 0)
    step2(1)
    lax.fori_loop(BLOCKS // 4, BLOCKS // 2, tile, 0)
    step3(0)

    fcopies = []
    for h in range(2):

        def walk(g, acc):
            for u in range(WALK):
                row, col = g // (BLOCK // WALK), lax.rem(g, BLOCK // WALK) * WALK + u
                acc = jnp.where(meta_ref[8 + row, col] > 0, 0.0, acc) + prod[meta_ref[row, col] + h]
                run[g * WALK + u] = acc
            return acc

        lax.fori_loop(0, OFFSETS * BLOCKS // WALK, walk, jnp.zeros((HROWS, BLOCK), F32))
        rows = pl.ds(h * HROWS, HROWS)

        def total(d):
            return jnp.where(meta_ref[15, d] > 0, run[meta_ref[7, d]], 0.0)

        for s in range(2 * SLOTS):
            fout[h, s // SLOTS, s % SLOTS] = total(BLOCKS + s).astype(BF16)
        for d, dev in enumerate((below, above)):
            c = rcopy(fout.at[h, d], fin.at[h, d], fsend.at[h, d], frecv.at[h, d], dev)
            c.start()
            fcopies.append(c)

        def keep(d, _):
            eg[d, rows, :] = total(d)
            return 0

        lax.fori_loop(0, BLOCKS, keep, 0)
        if h == 0:
            step3(1)
    step4(0)
    step4(1)
    for c in fcopies:
        c.wait_recv()
    sent += fcopies
    up_ok = b < NBOX - 1
    dn_ok = b > 0

    def settle(d, _):
        cols = pl.ds(pl.multiple_of(d * BLOCK, BLOCK), BLOCK)
        for h in range(2):
            rows = pl.ds(h * HROWS, HROWS)
            t = eg[d, rows, :]
            for s in range(SLOTS):
                t = t + jnp.where((send_ref[0, 1, s] == d) & up_ok, fin[h, 0, s].astype(F32), 0.0)
                t = t + jnp.where((send_ref[0, 0, s] == d) & dn_ok, fin[h, 1, s].astype(F32), 0.0)
            in_ref[rows, cols] = (occ_of(occ_ref, d) * t).astype(BF16)
        return 0

    lax.fori_loop(0, BLOCKS, settle, 0)
    step5(0)
    step5(1)
    step6(0)
    step6(1)
    gather.wait_sends()
    for c in sent:
        c.wait_send()


def norm_call(send, kmap, meta, conv, sums, out_grad, occ, gain, shift, ext, parts):
    quarter = pltpu.VMEM((BLOCKS, LOC, BLOCK), BF16)
    faces = pltpu.VMEM((2, 2, SLOTS, HROWS, BLOCK), BF16)
    dma = pltpu.SemaphoreType.DMA
    return pl.pallas_call(
        norm_kernel,
        out_shape=(
            jax.ShapeDtypeStruct((LOC, BLOCKS * BLOCK), BF16),
            jax.ShapeDtypeStruct((LOC, BLOCKS * BLOCK), BF16),
            jax.ShapeDtypeStruct((OFFSETS, LOC, CH), BF16),
            jax.ShapeDtypeStruct((1, BLOCK), F32),
        ),
        in_specs=[SMEM] * 3 + [VMEM] * 8,
        out_specs=(VMEM,) * 4,
        scratch_shapes=[
            pltpu.VMEM((EXT + 1, BLOCK, CH), BF16),
            pltpu.VMEM((OFFSETS, LOC, CH), F32),
            pltpu.VMEM((CH, WPAD), BF16),
            pltpu.VMEM((WPAD, CH), BF16),
            pltpu.VMEM((BLOCKS * 2 * OFFSETS, HROWS, BLOCK), F32),
            pltpu.VMEM((OFFSETS * BLOCKS, HROWS, BLOCK), F32),
            pltpu.VMEM((BLOCKS, LOC, BLOCK), F32),
            quarter,
            quarter,
            quarter,
            quarter,
            pltpu.VMEM((2, 8, 2, BLOCK), F32),
            pltpu.VMEM((2, 8, 1, BLOCK), F32),
            faces,
            faces,
            pltpu.VMEM((2, KHALF * LOC, BLOCK), BF16),
            pltpu.VMEM((2, KHALF * LOC, BLOCK), BF16),
            pltpu.VMEM((2, WROWS, BLOCK), BF16),
            pltpu.VMEM((2, 3, XROWS, BLOCK), BF16),
            pltpu.VMEM((2, XROWS, BLOCK), BF16),
            pltpu.VMEM((2, 7, ZROWS, BLOCK), BF16),
            pltpu.VMEM((2, 2, WROWS, BLOCK), BF16),
            dma((12,)),
            dma((12,)),
            dma((2, 2, 7)),
            dma((2, 2, 7)),
            dma((3,)),
            dma((3,)),
            dma((2, 2)),
            dma((2, 2)),
            dma((2, 22)),
            dma((2, 22)),
        ],
        compiler_params=params(2),
        name="norm",
    )(send, kmap, meta, conv, sums, out_grad, occ, gain, shift, ext, parts)


def per_device(
    features, occupied, send_lists, kernel_map, weights, norm_gain, norm_shift, out_grad
):
    occ = occupied.reshape(BLOCKS, 1, BLOCK)
    w = weights.reshape(OFFSETS * LOC, CH)
    gain, shift = norm_gain.reshape(1, LOC), norm_shift.reshape(1, LOC)
    conv, sums, ext, parts, meta = conv_call(send_lists, kernel_map, features, occ, w)
    out_features, in_grad, weight_grad, stat = norm_call(
        send_lists, kernel_map, meta, conv, sums, out_grad, occ, gain, shift, ext, parts
    )
    return (out_features, in_grad, weight_grad.astype(F32), stat[0, LOC:], stat[0, :LOC])


def solution(mesh):
    in_specs = (
        P("ch", "box"),
        P("box"),
        P("box", None, None),
        P("box", None, None),
        P(None, "ch", None),
        P("ch"),
        P("ch"),
        P("ch", "box"),
    )
    out_specs = (P("ch", "box"), P("ch", "box"), P(None, "ch", None), P("ch"), P("ch"))
    return jax.shard_map(
        per_device, mesh=mesh, in_specs=in_specs, out_specs=out_specs, check_vma=False
    )
```

```python
import functools

import jax
import jax.numpy as jnp
from jax import lax
from jax.experimental import pallas as pl
from jax.experimental.pallas import tpu as pltpu
from jax.sharding import PartitionSpec as P

F32 = jnp.float32
BF16 = jnp.bfloat16
MESH = pl.DeviceIdType.MESH
VMEM = pl.BlockSpec(memory_space=pltpu.VMEM)
SMEM = pl.BlockSpec(memory_space=pltpu.SMEM)
VMEM_LIMIT = 62 * 2**20

BLOCK = 128
BLOCKS = 32
CHUNK = 8
SLOTS = 8
EXT = BLOCKS + 2 * SLOTS
OFFSETS = 27
CH = 256
LOC = 64
WPAD = 1792
PARTS = 4
KFIRST = (0, 8, 16, 24)
KCOUNT = (8, 8, 8, 3)
WROWS = 512
XROWS = WROWS // 4
ZROWS = XROWS // 8
NBOX = 64
WALK = 16


def params(cid=None):
    if cid is None:
        return pltpu.CompilerParams(vmem_limit_bytes=VMEM_LIMIT)
    return pltpu.CompilerParams(
        vmem_limit_bytes=VMEM_LIMIT, collective_id=cid, has_side_effects=True
    )


def rcopy(src, dst, ssem, rsem, dev):
    return pltpu.make_async_remote_copy(
        src_ref=src, dst_ref=dst, send_sem=ssem, recv_sem=rsem, device_id=dev, device_id_type=MESH
    )


def greet(devs):
    barrier = pltpu.get_barrier_semaphore()
    for dev in devs:
        pl.semaphore_signal(barrier, inc=1, device_id=dev, device_id_type=MESH)
    pl.semaphore_wait(barrier, len(devs))


def occ_of(occ_ref, j):
    return occ_ref[j].astype(F32)


def rows_of(q):
    return pl.ds(pl.multiple_of(q * LOC, LOC), LOC)


class YGather:
    def __init__(self, own, from_dn, from_up, opp, ssem, rsem):
        q = lax.axis_index("ch")
        self.up = {"ch": lax.rem(q + 1, 4)}
        self.dn = {"ch": lax.rem(q + 3, 4)}

        def mk(src, dst, chunk, i, dev):
            part = pl.ds(chunk * CHUNK, CHUNK)
            return rcopy(src.at[part], dst.at[part], ssem.at[i], rsem.at[i], dev)

        self.own_up = [mk(own, from_dn, c, c, self.up) for c in range(4)]
        self.own_dn = [mk(own, from_up, c, 4 + c, self.dn) for c in range(4)]
        self.far_up = [mk(from_dn, opp, c, 8 + c, self.up) for c in (0, 1)]
        self.far_dn = [mk(from_up, opp, c, 8 + c, self.dn) for c in (2, 3)]

    def start(self):
        self.own_up[0].start()
        self.own_dn[2].start()
        self.own_up[1].start()
        self.own_dn[3].start()

    def forward(self, i):
        self.own_up[i].wait_recv()
        self.far_up[i].start()
        self.own_up[2 + i].start()
        self.own_dn[2 + i].wait_recv()
        self.far_dn[i].start()
        self.own_dn[i].start()

    def wait_part(self, i):
        self.own_up[2 + i].wait_recv()
        self.own_dn[i].wait_recv()
        self.far_up[i].wait_recv()
        self.far_dn[i].wait_recv()

    def wait_sends(self):
        for c in self.own_up + self.own_dn + self.far_up + self.far_dn:
            c.wait_send()


def rank_pairs(map_ref):
    at = lax.broadcasted_iota(jnp.int32, (8, BLOCK), 0) * BLOCK + lax.broadcasted_iota(jnp.int32, (8, BLOCK), 1)

    def fill(k, target):
        for j in range(BLOCKS):
            target = jnp.where(at == k * BLOCKS + j, map_ref[k, 0, j], target)
        return target

    target = lax.fori_loop(0, OFFSETS, fill, jnp.full((8, BLOCK), 63, jnp.int32))
    keys = target * 1024 + at

    def count(k, rank):
        for j in range(BLOCKS):
            rank = rank + (keys > map_ref[k, 0, j] * 1024 + (k * BLOCKS + j)).astype(jnp.int32)
        return rank

    return target, lax.fori_loop(0, OFFSETS, count, jnp.zeros((8, BLOCK), jnp.int32))


def sort_pairs(target, rank):
    lane = lax.broadcasted_iota(jnp.int32, (BLOCK, BLOCK), 1)
    sub = lax.broadcasted_iota(jnp.int32, (BLOCK, BLOCK), 0)
    pair = [jnp.zeros((1, BLOCK), F32) for _ in range(7)]
    goal = [jnp.zeros((1, BLOCK), F32) for _ in range(7)]
    last = jnp.full((1, BLOCK), -1.0, F32)
    for s in range(7):
        rcol = jnp.broadcast_to(rank[s : s + 1, :].astype(F32), (BLOCK, BLOCK)).T
        tcol = jnp.broadcast_to(target[s : s + 1, :].astype(F32), (BLOCK, BLOCK)).T
        i = sub + s * BLOCK
        number = (lax.rem(i, BLOCKS) * OFFSETS + i // BLOCKS).astype(F32)
        for r in range(7):
            hit = rcol == (lane + r * BLOCK).astype(F32)
            pair[r] = pair[r] + jnp.sum(jnp.where(hit, number, 0.0), axis=0, keepdims=True)
            goal[r] = goal[r] + jnp.sum(jnp.where(hit, tcol, 0.0), axis=0, keepdims=True)
        mine = tcol == lane.astype(F32)
        last = jnp.maximum(last, jnp.max(jnp.where(mine, rcol, -1.0), axis=0, keepdims=True))
    fresh = []
    first = lax.broadcasted_iota(jnp.int32, (1, BLOCK), 1) == 0
    for r in range(7):
        before = pltpu.roll(goal[r], 1, 1)
        carry = pltpu.roll(goal[r - 1], 1, 1) if r else jnp.full((1, BLOCK), -1.0, F32)
        before = jnp.where(first, carry, before)
        fresh.append(jnp.where(goal[r] == before, 0.0, 1.0))
    some = [jnp.where(last >= 0.0, 1.0, 0.0)]
    return jnp.concatenate(pair + [jnp.maximum(last, 0.0)] + fresh + some, axis=0).astype(jnp.int32)


def conv_kernel(
    send_ref,
    map_ref,
    feat_ref,
    occ_ref,
    w_ref,
    conv_ref,
    sum_ref,
    ext,
    parts_ref,
    meta_ref,
    own,
    from_dn,
    from_up,
    opp,
    fout,
    fin,
    prod,
    ysend,
    yrecv,
    fsend,
    frecv,
):
    q = lax.axis_index("ch")
    b = lax.axis_index("box")
    above = {"box": lax.rem(b + 1, NBOX)}
    below = {"box": lax.rem(b + NBOX - 1, NBOX)}
    gather = YGather(own, from_dn, from_up, opp, ysend, yrecv)
    quarters = ((q, own), (lax.rem(q + 3, 4), from_dn), (lax.rem(q + 1, 4), from_up), (lax.rem(q + 2, 4), opp))

    def mask(e, _):
        x = feat_ref[:, pl.ds(pl.multiple_of(e * BLOCK, BLOCK), BLOCK)].astype(F32)
        own[e] = (x * occ_of(occ_ref, e)).astype(BF16)
        return 0

    lax.fori_loop(0, BLOCKS, mask, 0)
    greet([gather.up, gather.dn, above, below])
    gather.start()

    def pack(r, src):
        for d in range(2):
            for s in range(SLOTS):
                pick = send_ref[0, d, s]
                blk = src[jnp.minimum(pick, BLOCKS - 1)].astype(F32)
                fout[r, d, s] = jnp.where(pick < BLOCKS, blk, 0.0).astype(BF16)
        up = rcopy(fout.at[r, 1], fin.at[r, 0], fsend.at[r, 1], frecv.at[r, 0], above)
        dn = rcopy(fout.at[r, 0], fin.at[r, 1], fsend.at[r, 0], frecv.at[r, 1], below)
        up.start()
        dn.start()
        return up, dn

    def tile(t):
        rhs = jnp.concatenate([ext[2 * t], ext[2 * t + 1]], axis=1)
        res = jnp.dot(w_ref[...], rhs, preferred_element_type=F32)
        prod[2 * t] = res[:, :BLOCK]
        prod[2 * t + 1] = res[:, BLOCK:]

    def part_tiles(i):
        def one(t, _):
            t = t + i * (CHUNK // 2) + (t // (CHUNK // 2)) * (CHUNK // 2)
            for r_abs, src in quarters:
                rows = rows_of(r_abs)
                ext[2 * t, rows, :] = src[2 * t]
                ext[2 * t + 1, rows, :] = src[2 * t + 1]
            tile(t)
            return 0

        lax.fori_loop(0, CHUNK, one, 0, unroll=2)

    copies = [pack(0, own)]
    prod[EXT] = jnp.zeros((OFFSETS * LOC, BLOCK), F32)
    ext[EXT] = jnp.zeros((CH, BLOCK), BF16)
    low = lax.broadcasted_iota(jnp.int32, (LOC, BLOCK), 1) < LOC
    for p in range(WPAD // BLOCK):
        for h in range(2):
            cols = pl.ds(h * BLOCK, BLOCK)
            first = w_ref[pl.ds(2 * p * LOC, LOC), cols].astype(F32)
            if 2 * p + 1 < OFFSETS:
                second = w_ref[pl.ds((2 * p + 1) * LOC, LOC), cols].astype(F32)
            else:
                second = jnp.zeros((LOC, BLOCK), F32)
            put = pl.ds(p * BLOCK, BLOCK)
            parts_ref[2 * h, :, put] = jnp.where(low, first, pltpu.roll(second, LOC, 1)).astype(BF16)
            parts_ref[2 * h + 1, :, put] = jnp.where(low, pltpu.roll(first, LOC, 1), second).astype(BF16)
    gather.forward(0)
    gather.forward(1)
    meta_ref[...] = sort_pairs(*rank_pairs(map_ref))
    gather.wait_part(0)
    part_tiles(0)
    gather.wait_part(1)
    copies.append(pack(1, from_dn))
    copies.append(pack(2, from_up))
    copies.append(pack(3, opp))
    part_tiles(1)
    keep_below = jnp.where(b > 0, 1.0, 0.0)
    keep_above = jnp.where(b < NBOX - 1, 1.0, 0.0)
    for r, (r_abs, _) in enumerate(quarters):
        up, dn = copies[r]
        up.wait_recv()
        dn.wait_recv()
        rows = rows_of(r_abs)
        for s in range(SLOTS):
            ext[BLOCKS + s, rows, :] = (fin[r, 0, s].astype(F32) * keep_below).astype(BF16)
            ext[BLOCKS + SLOTS + s, rows, :] = (fin[r, 1, s].astype(F32) * keep_above).astype(BF16)

    def face_tile(t, _):
        tile(t)
        return 0

    lax.fori_loop(BLOCKS // 2, EXT // 2, face_tile, 0, unroll=2)

    def out(j, carry):
        a, s = carry
        acc = prod[map_ref[0, 0, j], pl.ds(0, LOC), :]
        for k in range(1, OFFSETS):
            acc = acc + prod[map_ref[k, 0, j], pl.ds(LOC * k, LOC), :]
        conv_ref[j] = acc
        o = occ_of(occ_ref, j) * acc
        return a + o, s + o * acc

    zero = jnp.zeros((LOC, BLOCK), F32)
    a, s = lax.fori_loop(0, BLOCKS, out, (zero, zero), unroll=2)
    sum_ref[0] = a
    sum_ref[1] = s
    gather.wait_sends()
    for up, dn in copies:
        up.wait_send()
        dn.wait_send()


def conv_call(send, kmap, features, occ, w):
    quarter = pltpu.VMEM((BLOCKS, LOC, BLOCK), BF16)
    faces = pltpu.VMEM((4, 2, SLOTS, LOC, BLOCK), BF16)
    dma = pltpu.SemaphoreType.DMA
    return pl.pallas_call(
        conv_kernel,
        out_shape=(
            jax.ShapeDtypeStruct((BLOCKS, LOC, BLOCK), F32),
            jax.ShapeDtypeStruct((2, LOC, BLOCK), F32),
            jax.ShapeDtypeStruct((EXT + 1, CH, BLOCK), BF16),
            jax.ShapeDtypeStruct((4, LOC, WPAD), BF16),
            jax.ShapeDtypeStruct((16, BLOCK), jnp.int32),
        ),
        in_specs=[SMEM, SMEM, VMEM, VMEM, VMEM],
        out_specs=(VMEM,) * 5,
        scratch_shapes=[
            quarter,
            quarter,
            quarter,
            quarter,
            faces,
            faces,
            pltpu.VMEM((EXT + 1, OFFSETS * LOC, BLOCK), F32),
            dma((12,)),
            dma((12,)),
            dma((4, 2)),
            dma((4, 2)),
        ],
        compiler_params=params(1),
        name="conv",
    )(send, kmap, features, occ, w)


def lane_masks():
    ch = lax.broadcasted_iota(jnp.int32, (LOC, BLOCK), 0)
    lane = lax.broadcasted_iota(jnp.int32, (LOC, BLOCK), 1)
    return lane == ch, lane == ch + LOC


def to_row(first, second):
    m0, m1 = lane_masks()
    c0 = jnp.sum(first, axis=1, keepdims=True)
    c1 = jnp.sum(second, axis=1, keepdims=True)
    return jnp.sum(jnp.where(m0, c0, 0.0) + jnp.where(m1, c1, 0.0), axis=0, keepdims=True)


def to_cols(row):
    m0, m1 = lane_masks()
    return (
        jnp.sum(jnp.where(m0, row, 0.0), axis=1, keepdims=True),
        jnp.sum(jnp.where(m1, row, 0.0), axis=1, keepdims=True),
    )


def at_box(x, z, core):
    return {"box": x * 16 + z * 2 + core}


def to_col(row):
    ch = lax.broadcasted_iota(jnp.int32, (LOC, LOC), 0)
    lane = lax.broadcasted_iota(jnp.int32, (LOC, LOC), 1)
    return jnp.sum(jnp.where(ch == lane, row, 0.0), axis=1, keepdims=True)


def box_groups():
    b = lax.axis_index("box")
    x, z, core = b // 16, lax.rem(b // 2, 8), lax.rem(b, 2)
    first = [at_box(lax.rem(x + d // 2, 4), z, lax.rem(core + d % 2, 2)) for d in range(1, 8)]
    second = [at_box(x, lax.rem(z + d, 8), core) for d in range(1, 8)]
    return (x * 2 + core, first), (z, second)


def box_sum(mine, buf, ssem, rsem, idle):
    sent = []
    for step, (me, peers) in enumerate(box_groups()):
        buf[step, me] = mine
        copies = []
        for d, dev in enumerate(peers):
            c = rcopy(buf.at[step, me], buf.at[step, me], ssem.at[step, d], rsem.at[step, d], dev)
            c.start()
            copies.append(c)
        idle(step)
        for c in copies:
            c.wait_recv()
        mine = buf[step, 0]
        for d in range(1, 8):
            mine = mine + buf[step, d]
        sent += copies
    return mine, sent


def norm_kernel(
    send_ref,
    map_ref,
    meta_ref,
    conv_ref,
    sum_ref,
    grad_ref,
    occ_ref,
    gain_ref,
    shift_ref,
    ext_ref,
    parts_ref,
    out_ref,
    eg,
    fin,
    res,
    stat_ref,
    extt,
    wg,
    wrecv,
    win,
    prod,
    run,
    own,
    from_dn,
    from_up,
    opp,
    sbuf,
    sbuf2,
    fout,
    give,
    given,
    xbuf,
    xin,
    zbuf,
    zin,
    ysend,
    yrecv,
    ssend,
    srecv,
    wsend,
    wrecvs,
    fsend,
    frecv,
    gsend,
    grecv,
):
    q = lax.axis_index("ch")
    b = lax.axis_index("box")
    x, z, core = b // 16, lax.rem(b // 2, 8), lax.rem(b, 2)
    gather = YGather(own, from_dn, from_up, opp, ysend, yrecv)
    (_, near), (_, far) = box_groups()
    ypeers = [{"ch": lax.rem(q + d, 4)} for d in range(1, 4)]
    above = {"box": lax.rem(b + 1, NBOX)}
    below = {"box": lax.rem(b + NBOX - 1, NBOX)}
    mate = at_box(x, z, 1 - core)
    xpeers = [at_box(lax.rem(x + d, 4), z, core) for d in range(1, 4)]
    zpeers = far
    sent = []

    count = jnp.sum(occ_ref[...].astype(F32), axis=0)
    count = jnp.broadcast_to(jnp.sum(count, axis=1, keepdims=True), (1, BLOCK))
    row = to_row(sum_ref[0], sum_ref[1])
    sub = lax.broadcasted_iota(jnp.int32, (2, BLOCK), 0)
    pay = jnp.where(sub == 0, row, count)
    greet(ypeers + near + far + [above, below])
    wcopies = []
    for d, slot in ((1, 1), (3, 2), (2, 3)):
        dst = wrecv.at[pl.ds(slot * LOC, LOC)]
        c = rcopy(parts_ref.at[lax.rem(q + d, 4)], dst, wsend.at[d - 1], wrecvs.at[d - 1], ypeers[d - 1])
        c.start()
        wcopies.append(c)
    wrecv[pl.ds(0, LOC), :] = parts_ref[q]

    def flip(step):
        def one(e, _):
            extt[e] = ext_ref[e].T
            return 0

        lax.fori_loop(*((0, EXT // 2) if step == 0 else (EXT // 2, EXT + 1)), one, 0)

    tot, more = box_sum(pay, sbuf, ssend.at[0], srecv.at[0], flip)
    sent += wcopies + more
    n_vox = tot[1:2, 0:1]
    s1, s2 = to_cols(tot[0:1, :])
    mean = s1 / n_vox
    var = s2 / n_vox - mean * mean
    inv = 1.0 / jnp.sqrt(var + 1e-05)
    gain, shift = to_col(gain_ref[...]), to_col(shift_ref[...])

    def fwd(j, carry):
        a, s = carry
        cols = pl.ds(pl.multiple_of(j * BLOCK, BLOCK), BLOCK)
        occ = occ_of(occ_ref, j)
        nd = (conv_ref[j] - mean) * inv
        sh = nd * gain + shift
        out_ref[:, cols] = (occ * jnp.maximum(sh, 0.0)).astype(BF16)
        rg = jnp.where(sh > 0.0, occ * grad_ref[:, cols].astype(F32), 0.0)
        run[2 * j] = nd
        run[2 * j + 1] = rg
        return a + rg, s + rg * nd

    zero = jnp.zeros((LOC, BLOCK), F32)
    a, s = lax.fori_loop(0, BLOCKS, fwd, (zero, zero))
    row = to_row(a, s)

    def turn():
        for c in wcopies:
            c.wait_recv()
        for p in range(WPAD // BLOCK):
            win[pl.ds(p * BLOCK, BLOCK), :] = wrecv[:, pl.ds(p * BLOCK, BLOCK)].T

    tot, more = box_sum(row, sbuf2, ssend.at[1], srecv.at[1], lambda step: None)
    sent += more
    stat_ref[...] = tot
    sg, gg = to_cols(tot)
    scale = inv * gain
    sgm = sg / n_vox

    def bwd(j, _):
        nd, rg = run[2 * j], run[2 * j + 1]
        own[j] = (occ_of(occ_ref, j) * scale * (rg - sgm - nd * gg / n_vox)).astype(BF16)
        return 0

    lax.fori_loop(0, BLOCKS, bwd, 0)
    gather.start()

    def kterm(k, _):
        lhs = jnp.concatenate([own[j] for j in range(BLOCKS)], axis=1)
        rhs = jnp.concatenate([extt[map_ref[k, 0, j]] for j in range(BLOCKS)], axis=0)
        wg[k] = jnp.dot(lhs, rhs, preferred_element_type=F32)
        return 0

    def send(src, dst, h, i, dev):
        c = rcopy(src, dst, gsend.at[h, i], grecv.at[h, i], dev)
        c.start()
        sent.append(c)
        return c

    flight = [None] * PARTS
    xpart = lambda i: pl.ds(pl.multiple_of(i * XROWS, XROWS), XROWS)
    zpart = lambda i: pl.ds(pl.multiple_of(i * ZROWS, ZROWS), ZROWS)
    mine = pl.ds(pl.multiple_of(x * XROWS + z * ZROWS, ZROWS), ZROWS)

    def arrive(h):
        for c in flight[h]:
            c.wait_recv()

    def each_k(h, body):
        def one(k, _):
            body(k + KFIRST[h], pl.ds(pl.multiple_of(k * LOC, LOC), LOC))
            return 0

        lax.fori_loop(0, KCOUNT[h], one, 0)

    def step0(h):
        def cut(k, rows):
            give[h, rows, :] = jnp.where(core == 0, wg[k, :, BLOCK:], wg[k, :, :BLOCK]).astype(BF16)

        each_k(h, cut)
        rows = pl.ds(0, KCOUNT[h] * LOC)
        flight[h] = [send(give.at[h, rows], given.at[h, rows], h, 0, mate)]

    def step1(h):
        arrive(h)

        def add(k, rows):
            keep = jnp.where(core == 0, wg[k, :, :BLOCK], wg[k, :, BLOCK:])
            xbuf[h, rows, :] = (keep + given[h, rows, :].astype(F32)).astype(BF16)

        each_k(h, add)
        rest = WROWS - KCOUNT[h] * LOC
        if rest:
            xbuf[h, pl.ds(KCOUNT[h] * LOC, rest), :] = jnp.zeros((rest, BLOCK), BF16)
        flight[h] = [
            send(xbuf.at[h, xpart(lax.rem(x + d, 4))], xin.at[h, d - 1], h, d, xpeers[d - 1]) for d in range(1, 4)
        ]

    def step2(h):
        arrive(h)
        t = xbuf[h, xpart(x), :].astype(F32)
        for d in range(3):
            t = t + xin[h, d].astype(F32)
        zbuf[h] = t.astype(BF16)
        flight[h] = [
            send(zbuf.at[h, zpart(lax.rem(z + d, 8))], zin.at[h, d - 1], h, 3 + d, zpeers[d - 1]) for d in range(1, 8)
        ]

    def step3(h):
        arrive(h)
        t = zbuf[h, zpart(z), :].astype(F32)
        for d in range(7):
            t = t + zin[h, d].astype(F32)
        res[h, 0, mine, :] = t.astype(BF16)
        flight[h] = [
            send(res.at[h, 0, mine], res.at[h, 0, mine], h, 10 + d, zpeers[d - 1]) for d in range(1, 8)
        ]

    def step4(h):
        arrive(h)
        part = xpart(x)
        flight[h] = [
            send(res.at[h, 0, part], res.at[h, 0, part], h, 17 + d, xpeers[d - 1]) for d in range(1, 4)
        ]

    def step5(h):
        arrive(h)
        rows = pl.ds(0, KCOUNT[h] * LOC)
        flight[h] = [send(res.at[h, 0, rows], res.at[h, 1, rows], h, 21, mate)]

    def kterms(first, last):
        lax.fori_loop(first, last, kterm, 0)

    kterms(0, 8)
    step0(0)
    gather.forward(0)
    kterms(8, 12)
    step1(0)
    kterms(12, 16)
    step0(1)
    gather.forward(1)
    kterms(16, 20)
    step2(0)
    step1(1)
    kterms(20, 24)
    step0(2)
    kterms(24, 27)
    step0(3)
    step2(1)
    step1(2)
    turn()
    step3(0)
    step1(3)

    def tile(t, _):
        halves = []
        for e in (2 * t, 2 * t + 1):
            halves.append(jnp.concatenate([own[e], from_dn[e], from_up[e], opp[e]], axis=0))
        rhs = jnp.concatenate(halves, axis=1)
        r = jnp.dot(win[pl.ds(0, OFFSETS * LOC), :], rhs, preferred_element_type=F32)
        r = r.astype(BF16)
        place = 2 * OFFSETS * t
        prod[pl.ds(place, OFFSETS)] = r[:, :BLOCK].reshape(OFFSETS, LOC, BLOCK)
        prod[pl.ds(place + OFFSETS, OFFSETS)] = r[:, BLOCK:].reshape(OFFSETS, LOC, BLOCK)
        return 0

    gather.wait_part(0)
    lax.fori_loop(0, 4, tile, 0)
    lax.fori_loop(8, 12, tile, 0)
    step2(2)
    step2(3)
    gather.wait_part(1)
    lax.fori_loop(4, 8, tile, 0)
    step3(1)
    lax.fori_loop(12, 16, tile, 0)
    step4(0)

    def walk(g, acc):
        for u in range(WALK):
            row, col = g // (BLOCK // WALK), lax.rem(g, BLOCK // WALK) * WALK + u
            term = prod[meta_ref[row, col]].astype(F32)
            acc = jnp.where(meta_ref[8 + row, col] > 0, 0.0, acc) + term
            run[g * WALK + u] = acc
        return acc

    steps = OFFSETS * BLOCKS // WALK
    acc = lax.fori_loop(0, steps // 2, walk, jnp.zeros((LOC, BLOCK), F32))
    step3(2)
    step3(3)
    lax.fori_loop(steps // 2, steps, walk, acc)

    def total(d):
        return jnp.where(meta_ref[15, d] > 0, run[meta_ref[7, d]], 0.0)

    for s in range(2 * SLOTS):
        fout[s // SLOTS, s % SLOTS] = total(BLOCKS + s).astype(BF16)
    fcopies = []
    for d, dev in enumerate((below, above)):
        c = rcopy(fout.at[d], fin.at[d], fsend.at[d], frecv.at[d], dev)
        c.start()
        fcopies.append(c)
    sent += fcopies
    step4(1)
    step5(0)

    def keep(d, _):
        eg[d] = total(d)
        return 0

    lax.fori_loop(0, BLOCKS, keep, 0)
    step4(2)
    step4(3)
    step5(1)
    for c in fcopies:
        c.wait_recv()
    step5(2)
    step5(3)
    for h in range(PARTS):
        arrive(h)
    gather.wait_sends()
    for c in sent:
        c.wait_send()


def norm_call(send, kmap, meta, conv, sums, out_grad, occ, gain, shift, ext, parts):
    quarter = pltpu.VMEM((BLOCKS, LOC, BLOCK), BF16)
    dma = pltpu.SemaphoreType.DMA
    return pl.pallas_call(
        norm_kernel,
        out_shape=(
            jax.ShapeDtypeStruct((LOC, BLOCKS * BLOCK), BF16),
            jax.ShapeDtypeStruct((BLOCKS, LOC, BLOCK), F32),
            jax.ShapeDtypeStruct((2, SLOTS, LOC, BLOCK), BF16),
            jax.ShapeDtypeStruct((PARTS, 2, WROWS, BLOCK), BF16),
            jax.ShapeDtypeStruct((1, BLOCK), F32),
        ),
        in_specs=[SMEM] * 3 + [VMEM] * 8,
        out_specs=(VMEM,) * 5,
        scratch_shapes=[
            pltpu.VMEM((EXT + 1, BLOCK, CH), BF16),
            pltpu.VMEM((OFFSETS, LOC, CH), F32),
            pltpu.VMEM((CH, WPAD), BF16),
            pltpu.VMEM((WPAD, CH), BF16),
            pltpu.VMEM((OFFSETS * BLOCKS, LOC, BLOCK), BF16),
            pltpu.VMEM((OFFSETS * BLOCKS, LOC, BLOCK), F32),
            quarter,
            quarter,
            quarter,
            quarter,
            pltpu.VMEM((2, 8, 2, BLOCK), F32),
            pltpu.VMEM((2, 8, 1, BLOCK), F32),
            pltpu.VMEM((2, SLOTS, LOC, BLOCK), BF16),
            pltpu.VMEM((PARTS, WROWS, BLOCK), BF16),
            pltpu.VMEM((PARTS, WROWS, BLOCK), BF16),
            pltpu.VMEM((PARTS, WROWS, BLOCK), BF16),
            pltpu.VMEM((PARTS, 3, XROWS, BLOCK), BF16),
            pltpu.VMEM((PARTS, XROWS, BLOCK), BF16),
            pltpu.VMEM((PARTS, 7, ZROWS, BLOCK), BF16),
            dma((12,)),
            dma((12,)),
            dma((2, 2, 7)),
            dma((2, 2, 7)),
            dma((3,)),
            dma((3,)),
            dma((2,)),
            dma((2,)),
            dma((PARTS, 22)),
            dma((PARTS, 22)),
        ],
        compiler_params=params(2),
        name="norm",
    )(send, kmap, meta, conv, sums, out_grad, occ, gain, shift, ext, parts)


def emit_kernel(
    send_ref, out_ref, eg_ref, fin_ref, res_ref, stat_ref, occ_ref, out_to, in_to, wg_to, gain_to, shift_to, acc
):
    out_to[...] = out_ref[...]
    b = lax.axis_index("box")
    core = lax.rem(b, 2)
    for h in range(PARTS):

        def put(k, _):
            rows = pl.ds(pl.multiple_of(k * LOC, LOC), LOC)
            m, o = res_ref[h, 0, rows, :].astype(F32), res_ref[h, 1, rows, :].astype(F32)
            wg_to[k + KFIRST[h], :, :BLOCK] = jnp.where(core == 0, m, o)
            wg_to[k + KFIRST[h], :, BLOCK:] = jnp.where(core == 0, o, m)
            return 0

        lax.fori_loop(0, KCOUNT[h], put, 0)
    shift_to[...] = stat_ref[:, :LOC]
    gain_to[...] = stat_ref[:, LOC:]
    acc[pl.ds(0, BLOCKS)] = eg_ref[...]
    acc[BLOCKS] = jnp.zeros((LOC, BLOCK), F32)
    for d, ok in ((0, b < NBOX - 1), (1, b > 0)):
        for s in range(SLOTS):
            at = send_ref[0, 1 - d, s]
            acc[at] = acc[at] + jnp.where(ok, fin_ref[d, s].astype(F32), 0.0)

    def settle(d, _):
        in_to[:, pl.ds(pl.multiple_of(d * BLOCK, BLOCK), BLOCK)] = (occ_of(occ_ref, d) * acc[d]).astype(BF16)
        return 0

    lax.fori_loop(0, BLOCKS, settle, 0)


def emit_call(send, occ, out_features, eg, fin, res, stat):
    whole = jax.ShapeDtypeStruct((LOC, BLOCKS * BLOCK), BF16)
    line = jax.ShapeDtypeStruct((1, LOC), F32)
    return pl.pallas_call(
        emit_kernel,
        out_shape=(whole, whole, jax.ShapeDtypeStruct((OFFSETS, LOC, CH), F32), line, line),
        in_specs=[SMEM] + [VMEM] * 6,
        out_specs=(VMEM,) * 5,
        scratch_shapes=[pltpu.VMEM((BLOCKS + 1, LOC, BLOCK), F32)],
        compiler_params=params(),
        name="emit",
    )(send, out_features, eg, fin, res, stat, occ)


def per_device(
    features, occupied, send_lists, kernel_map, weights, norm_gain, norm_shift, out_grad
):
    occ = occupied.reshape(BLOCKS, 1, BLOCK)
    w = weights.reshape(OFFSETS * LOC, CH)
    kernel_map = kernel_map.transpose(1, 0, 2)
    gain, shift = norm_gain.reshape(1, LOC), norm_shift.reshape(1, LOC)
    conv, sums, ext, parts, meta = conv_call(send_lists, kernel_map, features, occ, w)
    results = norm_call(send_lists, kernel_map, meta, conv, sums, out_grad, occ, gain, shift, ext, parts)
    out_features, in_grad, weight_grad, gain_grad, shift_grad = emit_call(send_lists, occ, *results)
    return (out_features, in_grad, weight_grad, gain_grad.reshape(LOC), shift_grad.reshape(LOC))


def solution(mesh):
    in_specs = (
        P("ch", "box"),
        P("box"),
        P("box", None, None),
        P("box", None, None),
        P(None, "ch", None),
        P("ch"),
        P("ch"),
        P("ch", "box"),
    )
    out_specs = (P("ch", "box"), P("ch", "box"), P(None, "ch", None), P("ch"), P("ch"))
    return jax.shard_map(
        per_device, mesh=mesh, in_specs=in_specs, out_specs=out_specs, check_vma=False
    )
```

```python
import functools

import jax
import jax.numpy as jnp
from jax import lax
from jax.experimental import pallas as pl
from jax.experimental.pallas import tpu as pltpu
from jax.sharding import PartitionSpec as P

F32 = jnp.float32
BF16 = jnp.bfloat16
MESH = pl.DeviceIdType.MESH
VMEM = pl.BlockSpec(memory_space=pltpu.VMEM)
SMEM = pl.BlockSpec(memory_space=pltpu.SMEM)
ANY = pl.BlockSpec(memory_space=pl.ANY)
VMEM_LIMIT = 62 * 2**20

BLOCK = 128
BLOCKS = 32
CHUNK = 4
NCHUNK = 8
NFWD = 4
SLOTS = 8
EXT = BLOCKS + 2 * SLOTS
OFFSETS = 27
CH = 256
LOC = 64
WPAD = 1792
PARTS = 4
KFIRST = (0, 8, 16, 24)
KCOUNT = (8, 8, 8, 3)
WROWS = 512
XROWS = WROWS // 4
ZROWS = XROWS // 8
NBOX = 64
WALK = 16


def params(cid=None):
    if cid is None:
        return pltpu.CompilerParams(vmem_limit_bytes=VMEM_LIMIT)
    return pltpu.CompilerParams(
        vmem_limit_bytes=VMEM_LIMIT, collective_id=cid, has_side_effects=True
    )


def rcopy(src, dst, ssem, rsem, dev):
    return pltpu.make_async_remote_copy(
        src_ref=src, dst_ref=dst, send_sem=ssem, recv_sem=rsem, device_id=dev, device_id_type=MESH
    )


def greet(devs):
    barrier = pltpu.get_barrier_semaphore()
    for dev in devs:
        pl.semaphore_signal(barrier, inc=1, device_id=dev, device_id_type=MESH)
    pl.semaphore_wait(barrier, len(devs))


def occ_of(occ_ref, j):
    return occ_ref[j].astype(F32)


def rows_of(q):
    return pl.ds(pl.multiple_of(q * LOC, LOC), LOC)


class YGather:
    def __init__(self, own, from_dn, from_up, opp, ssem, rsem):
        q = lax.axis_index("ch")
        self.up = {"ch": lax.rem(q + 1, 4)}
        self.dn = {"ch": lax.rem(q + 3, 4)}

        def mk(src, dst, chunk, i, dev):
            part = pl.ds(chunk * CHUNK, CHUNK)
            return rcopy(src.at[part], dst.at[part], ssem.at[i], rsem.at[i], dev)

        lower, upper = range(NFWD), range(NFWD, NCHUNK)
        self.own_up = [mk(own, from_dn, c, c, self.up) for c in range(NCHUNK)]
        self.own_dn = [mk(own, from_up, c, NCHUNK + c, self.dn) for c in range(NCHUNK)]
        self.far_up = [mk(from_dn, opp, c, 2 * NCHUNK + c, self.up) for c in lower]
        self.far_dn = [mk(from_up, opp, c, 2 * NCHUNK + c, self.dn) for c in upper]

    def start(self):
        for c in range(2):
            self.own_up[c].start()
            self.own_dn[NFWD + c].start()

    def forward(self, i):
        self.own_up[i].wait_recv()
        self.far_up[i].start()
        self.own_up[NFWD + i].start()
        self.own_dn[NFWD + i].wait_recv()
        self.far_dn[i].start()
        self.own_dn[i].start()
        if i + 2 < NFWD:
            self.own_up[i + 2].start()
            self.own_dn[NFWD + i + 2].start()

    def wait_part(self, i):
        self.own_up[NFWD + i].wait_recv()
        self.own_dn[i].wait_recv()
        self.far_up[i].wait_recv()
        self.far_dn[i].wait_recv()

    def wait_sends(self):
        for c in self.own_up + self.own_dn + self.far_up + self.far_dn:
            c.wait_send()


def pair_places():
    return lax.broadcasted_iota(jnp.int32, (8, BLOCK), 0) * BLOCK + lax.broadcasted_iota(jnp.int32, (8, BLOCK), 1)


def pair_targets(map_ref):
    at = pair_places()

    def fill(k, target):
        for j in range(BLOCKS):
            target = jnp.where(at == k * BLOCKS + j, map_ref[k, 0, j], target)
        return target

    return lax.fori_loop(0, OFFSETS, fill, jnp.full((8, BLOCK), 63, jnp.int32))


def pair_ranks(map_ref, target):
    keys = target * 1024 + pair_places()

    def count(k, rank):
        for j in range(BLOCKS):
            rank = rank + (keys > map_ref[k, 0, j] * 1024 + (k * BLOCKS + j)).astype(jnp.int32)
        return rank

    return lax.fori_loop(0, OFFSETS, count, jnp.zeros((8, BLOCK), jnp.int32))


def sort_pairs(target, rank):
    lane = lax.broadcasted_iota(jnp.int32, (BLOCK, BLOCK), 1)
    sub = lax.broadcasted_iota(jnp.int32, (BLOCK, BLOCK), 0)
    pair = [jnp.zeros((1, BLOCK), F32) for _ in range(7)]
    goal = [jnp.zeros((1, BLOCK), F32) for _ in range(7)]
    last = jnp.full((1, BLOCK), -1.0, F32)
    for s in range(7):
        rcol = jnp.broadcast_to(rank[s : s + 1, :].astype(F32), (BLOCK, BLOCK)).T
        tcol = jnp.broadcast_to(target[s : s + 1, :].astype(F32), (BLOCK, BLOCK)).T
        i = sub + s * BLOCK
        number = (lax.rem(i, BLOCKS) * OFFSETS + i // BLOCKS).astype(F32)
        for r in range(7):
            hit = rcol == (lane + r * BLOCK).astype(F32)
            pair[r] = pair[r] + jnp.sum(jnp.where(hit, number, 0.0), axis=0, keepdims=True)
            goal[r] = goal[r] + jnp.sum(jnp.where(hit, tcol, 0.0), axis=0, keepdims=True)
        mine = tcol == lane.astype(F32)
        last = jnp.maximum(last, jnp.max(jnp.where(mine, rcol, -1.0), axis=0, keepdims=True))
    fresh = []
    first = lax.broadcasted_iota(jnp.int32, (1, BLOCK), 1) == 0
    for r in range(7):
        before = pltpu.roll(goal[r], 1, 1)
        carry = pltpu.roll(goal[r - 1], 1, 1) if r else jnp.full((1, BLOCK), -1.0, F32)
        before = jnp.where(first, carry, before)
        fresh.append(jnp.where(goal[r] == before, 0.0, 1.0))
    some = [jnp.where(last >= 0.0, 1.0, 0.0)]
    return jnp.concatenate(pair + [jnp.maximum(last, 0.0)] + fresh + some, axis=0).astype(jnp.int32)


def conv_kernel(
    send_ref,
    map_ref,
    feat_ref,
    occ_ref,
    w_ref,
    conv_ref,
    sum_ref,
    ext_to,
    parts_ref,
    meta_ref,
    ext,
    own,
    from_dn,
    from_up,
    opp,
    fout,
    fin,
    prod,
    ysend,
    yrecv,
    fsend,
    frecv,
    esem,
):
    q = lax.axis_index("ch")
    b = lax.axis_index("box")
    above = {"box": lax.rem(b + 1, NBOX)}
    below = {"box": lax.rem(b + NBOX - 1, NBOX)}
    gather = YGather(own, from_dn, from_up, opp, ysend, yrecv)
    quarters = ((q, own), (lax.rem(q + 3, 4), from_dn), (lax.rem(q + 1, 4), from_up), (lax.rem(q + 2, 4), opp))

    def mask(e, _):
        x = feat_ref[:, pl.ds(pl.multiple_of(e * BLOCK, BLOCK), BLOCK)].astype(F32)
        own[e] = (x * occ_of(occ_ref, e)).astype(BF16)
        return 0

    lax.fori_loop(0, BLOCKS, mask, 0)
    greet([gather.up, gather.dn, above, below])
    gather.start()

    def pack(r, src):
        for d in range(2):
            for s in range(SLOTS):
                pick = send_ref[0, d, s]
                blk = src[jnp.minimum(pick, BLOCKS - 1)].astype(F32)
                fout[r, d, s] = jnp.where(pick < BLOCKS, blk, 0.0).astype(BF16)
        up = rcopy(fout.at[r, 1], fin.at[r, 0], fsend.at[r, 1], frecv.at[r, 0], above)
        dn = rcopy(fout.at[r, 0], fin.at[r, 1], fsend.at[r, 0], frecv.at[r, 1], below)
        up.start()
        dn.start()
        return up, dn

    def tile(t):
        rhs = jnp.concatenate([ext[2 * t], ext[2 * t + 1]], axis=1)
        res = jnp.dot(w_ref[...], rhs, preferred_element_type=F32)
        prod[2 * t] = res[:, :BLOCK]
        prod[2 * t + 1] = res[:, BLOCK:]

    def part_tiles(i):
        def one(t, _):
            t = t + i * (CHUNK // 2) + (t // (CHUNK // 2)) * (3 * CHUNK // 2)
            for r_abs, src in quarters:
                rows = rows_of(r_abs)
                ext[2 * t, rows, :] = src[2 * t]
                ext[2 * t + 1, rows, :] = src[2 * t + 1]
            tile(t)
            return 0

        lax.fori_loop(0, CHUNK, one, 0, unroll=2)

    copies = [pack(0, own)]
    prod[EXT] = jnp.zeros((OFFSETS * LOC, BLOCK), F32)
    ext[EXT] = jnp.zeros((CH, BLOCK), BF16)
    low = lax.broadcasted_iota(jnp.int32, (LOC, BLOCK), 1) < LOC
    for p in range(WPAD // BLOCK):
        for h in range(2):
            cols = pl.ds(h * BLOCK, BLOCK)
            first = w_ref[pl.ds(2 * p * LOC, LOC), cols].astype(F32)
            if 2 * p + 1 < OFFSETS:
                second = w_ref[pl.ds((2 * p + 1) * LOC, LOC), cols].astype(F32)
            else:
                second = jnp.zeros((LOC, BLOCK), F32)
            put = pl.ds(p * BLOCK, BLOCK)
            parts_ref[2 * h, :, put] = jnp.where(low, first, pltpu.roll(second, LOC, 1)).astype(BF16)
            parts_ref[2 * h + 1, :, put] = jnp.where(low, pltpu.roll(first, LOC, 1), second).astype(BF16)
    gather.forward(0)
    target = pair_targets(map_ref)
    gather.forward(1)
    rank = pair_ranks(map_ref, target)
    gather.forward(2)
    meta_ref[...] = sort_pairs(target, rank)
    gather.forward(3)
    for i in range(NFWD - 1):
        gather.wait_part(i)
        part_tiles(i)
    gather.wait_part(NFWD - 1)
    copies.append(pack(1, from_dn))
    copies.append(pack(2, from_up))
    copies.append(pack(3, opp))
    part_tiles(NFWD - 1)
    keep_below = jnp.where(b > 0, 1.0, 0.0)
    keep_above = jnp.where(b < NBOX - 1, 1.0, 0.0)
    for r, (r_abs, _) in enumerate(quarters):
        up, dn = copies[r]
        up.wait_recv()
        dn.wait_recv()
        rows = rows_of(r_abs)
        for s in range(SLOTS):
            ext[BLOCKS + s, rows, :] = (fin[r, 0, s].astype(F32) * keep_below).astype(BF16)
            ext[BLOCKS + SLOTS + s, rows, :] = (fin[r, 1, s].astype(F32) * keep_above).astype(BF16)

    def face_tile(t, _):
        tile(t)
        return 0

    lax.fori_loop(BLOCKS // 2, EXT // 2, face_tile, 0, unroll=2)

    leave = pltpu.make_async_copy(ext, ext_to, esem)
    leave.start()

    def out(j, carry):
        a, s = carry
        acc = prod[map_ref[0, 0, j], pl.ds(0, LOC), :]
        for k in range(1, OFFSETS):
            acc = acc + prod[map_ref[k, 0, j], pl.ds(LOC * k, LOC), :]
        conv_ref[j] = acc
        o = occ_of(occ_ref, j) * acc
        return a + o, s + o * acc

    zero = jnp.zeros((LOC, BLOCK), F32)
    a, s = lax.fori_loop(0, BLOCKS, out, (zero, zero), unroll=2)
    sum_ref[0] = a
    sum_ref[1] = s
    leave.wait()
    gather.wait_sends()
    for up, dn in copies:
        up.wait_send()
        dn.wait_send()


def conv_call(send, kmap, features, occ, w):
    quarter = pltpu.VMEM((BLOCKS, LOC, BLOCK), BF16)
    faces = pltpu.VMEM((4, 2, SLOTS, LOC, BLOCK), BF16)
    dma = pltpu.SemaphoreType.DMA
    return pl.pallas_call(
        conv_kernel,
        out_shape=(
            jax.ShapeDtypeStruct((BLOCKS, LOC, BLOCK), F32),
            jax.ShapeDtypeStruct((2, LOC, BLOCK), F32),
            jax.ShapeDtypeStruct((EXT + 1, CH, BLOCK), BF16),
            jax.ShapeDtypeStruct((4, LOC, WPAD), BF16),
            jax.ShapeDtypeStruct((16, BLOCK), jnp.int32),
        ),
        in_specs=[SMEM, SMEM, VMEM, VMEM, VMEM],
        out_specs=(VMEM, VMEM, ANY, VMEM, VMEM),
        scratch_shapes=[
            pltpu.VMEM((EXT + 1, CH, BLOCK), BF16),
            quarter,
            quarter,
            quarter,
            quarter,
            faces,
            faces,
            pltpu.VMEM((EXT + 1, OFFSETS * LOC, BLOCK), F32),
            dma((3 * NCHUNK,)),
            dma((3 * NCHUNK,)),
            dma((4, 2)),
            dma((4, 2)),
            dma,
        ],
        compiler_params=params(1),
        name="conv",
    )(send, kmap, features, occ, w)


def lane_masks():
    ch = lax.broadcasted_iota(jnp.int32, (LOC, BLOCK), 0)
    lane = lax.broadcasted_iota(jnp.int32, (LOC, BLOCK), 1)
    return lane == ch, lane == ch + LOC


def to_row(first, second):
    m0, m1 = lane_masks()
    c0 = jnp.sum(first, axis=1, keepdims=True)
    c1 = jnp.sum(second, axis=1, keepdims=True)
    return jnp.sum(jnp.where(m0, c0, 0.0) + jnp.where(m1, c1, 0.0), axis=0, keepdims=True)


def to_cols(row):
    m0, m1 = lane_masks()
    return (
        jnp.sum(jnp.where(m0, row, 0.0), axis=1, keepdims=True),
        jnp.sum(jnp.where(m1, row, 0.0), axis=1, keepdims=True),
    )


def at_box(x, z, core):
    return {"box": x * 16 + z * 2 + core}


def to_col(row):
    ch = lax.broadcasted_iota(jnp.int32, (LOC, LOC), 0)
    lane = lax.broadcasted_iota(jnp.int32, (LOC, LOC), 1)
    return jnp.sum(jnp.where(ch == lane, row, 0.0), axis=1, keepdims=True)


def box_groups():
    b = lax.axis_index("box")
    x, z, core = b // 16, lax.rem(b // 2, 8), lax.rem(b, 2)
    first = [at_box(lax.rem(x + d // 2, 4), z, lax.rem(core + d % 2, 2)) for d in range(1, 8)]
    second = [at_box(x, lax.rem(z + d, 8), core) for d in range(1, 8)]
    return (x * 2 + core, first), (z, second)


def box_sum(mine, buf, ssem, rsem, idle):
    sent = []
    for step, (me, peers) in enumerate(box_groups()):
        buf[step, me] = mine
        copies = []
        for d, dev in enumerate(peers):
            c = rcopy(buf.at[step, me], buf.at[step, me], ssem.at[step, d], rsem.at[step, d], dev)
            c.start()
            copies.append(c)
        idle(step)
        for c in copies:
            c.wait_recv()
        mine = buf[step, 0]
        for d in range(1, 8):
            mine = mine + buf[step, d]
        sent += copies
    return mine, sent


def norm_kernel(
    send_ref,
    map_ref,
    meta_ref,
    conv_ref,
    sum_ref,
    grad_from,
    occ_ref,
    gain_ref,
    shift_ref,
    ext_from,
    parts_ref,
    out_ref,
    eg,
    fin,
    res,
    stat_ref,
    grad_ref,
    ext_ref,
    relay,
    extt,
    wg,
    wrecv,
    win,
    prod,
    run,
    own,
    from_dn,
    from_up,
    opp,
    sbuf,
    sbuf2,
    fout,
    give,
    given,
    xbuf,
    xin,
    zbuf,
    zin,
    ysend,
    yrecv,
    ssend,
    srecv,
    wsend,
    wrecvs,
    fsend,
    frecv,
    gsend,
    grecv,
    lsem,
):
    q = lax.axis_index("ch")
    b = lax.axis_index("box")
    x, z, core = b // 16, lax.rem(b // 2, 8), lax.rem(b, 2)
    gather = YGather(own, from_dn, from_up, opp, ysend, yrecv)
    (_, near), (_, far) = box_groups()
    above = {"box": lax.rem(b + 1, NBOX)}
    below = {"box": lax.rem(b + NBOX - 1, NBOX)}
    mate = at_box(x, z, 1 - core)
    xpeers = [at_box(lax.rem(x + d, 4), z, core) for d in range(1, 4)]
    zpeers = far
    sent = []
    loads = [pltpu.make_async_copy(ext_from, ext_ref, lsem.at[0]), pltpu.make_async_copy(grad_from, grad_ref, lsem.at[1])]
    for c in loads:
        c.start()

    count = jnp.sum(occ_ref[...].astype(F32), axis=0)
    count = jnp.broadcast_to(jnp.sum(count, axis=1, keepdims=True), (1, BLOCK))
    row = to_row(sum_ref[0], sum_ref[1])
    sub = lax.broadcasted_iota(jnp.int32, (2, BLOCK), 0)
    pay = jnp.where(sub == 0, row, count)
    greet([gather.up, gather.dn] + near + far + [above, below])
    wcopies = []

    def wcopy(src, dst, i, dev):
        c = rcopy(src, dst, wsend.at[i], wrecvs.at[i], dev)
        wcopies.append(c)
        return c

    far_part = parts_ref.at[lax.rem(q + 2, 4)]
    near_rows, far_rows = pl.ds(0, LOC // 2), pl.ds(LOC // 2, LOC // 2)
    lead = [
        wcopy(far_part.at[near_rows], relay.at[0], 0, gather.up),
        wcopy(far_part.at[far_rows], relay.at[1], 1, gather.dn),
    ]
    tail = [
        wcopy(parts_ref.at[lax.rem(q + 1, 4)], wrecv.at[pl.ds(LOC, LOC)], 2, gather.up),
        wcopy(parts_ref.at[lax.rem(q + 3, 4)], wrecv.at[pl.ds(2 * LOC, LOC)], 3, gather.dn),
    ]
    tail_far = [
        wcopy(relay.at[0], wrecv.at[pl.ds(3 * LOC, LOC // 2)], 4, gather.up),
        wcopy(relay.at[1], wrecv.at[pl.ds(3 * LOC + LOC // 2, LOC // 2)], 5, gather.dn),
    ]
    for c in lead + tail:
        c.start()
    wrecv[pl.ds(0, LOC), :] = parts_ref[q]
    loads[0].wait()

    def flip(step):
        if step == 1:
            for c, d in zip(lead, tail_far):
                c.wait_recv()
                d.start()

        def one(e, _):
            extt[e] = ext_ref[e].T
            return 0

        lax.fori_loop(*((0, EXT // 2) if step == 0 else (EXT // 2, EXT + 1)), one, 0)

    tot, more = box_sum(pay, sbuf, ssend.at[0], srecv.at[0], flip)
    sent += wcopies + more
    loads[1].wait()
    n_vox = tot[1:2, 0:1]
    s1, s2 = to_cols(tot[0:1, :])
    mean = s1 / n_vox
    var = s2 / n_vox - mean * mean
    inv = 1.0 / jnp.sqrt(var + 1e-05)
    gain, shift = to_col(gain_ref[...]), to_col(shift_ref[...])

    def fwd(j, carry):
        a, s = carry
        cols = pl.ds(pl.multiple_of(j * BLOCK, BLOCK), BLOCK)
        occ = occ_of(occ_ref, j)
        nd = (conv_ref[j] - mean) * inv
        sh = nd * gain + shift
        out_ref[:, cols] = (occ * jnp.maximum(sh, 0.0)).astype(BF16)
        rg = jnp.where(sh > 0.0, occ * grad_ref[:, cols].astype(F32), 0.0)
        run[2 * j] = nd
        run[2 * j + 1] = rg
        return a + rg, s + rg * nd

    zero = jnp.zeros((LOC, BLOCK), F32)
    a, s = lax.fori_loop(0, BLOCKS, fwd, (zero, zero))
    row = to_row(a, s)

    def turn(step):
        if step == 0:
            return
        for c in tail + tail_far:
            c.wait_recv()
        for p in range(WPAD // BLOCK):
            win[pl.ds(p * BLOCK, BLOCK), :] = wrecv[:, pl.ds(p * BLOCK, BLOCK)].T

    tot, more = box_sum(row, sbuf2, ssend.at[1], srecv.at[1], turn)
    sent += more
    stat_ref[...] = tot
    sg, gg = to_cols(tot)
    scale = inv * gain
    sgm = sg / n_vox

    def bwd(j, _):
        nd, rg = run[2 * j], run[2 * j + 1]
        own[j] = (occ_of(occ_ref, j) * scale * (rg - sgm - nd * gg / n_vox)).astype(BF16)
        return 0

    lax.fori_loop(0, BLOCKS, bwd, 0)
    gather.start()

    def kterm(k, _):
        lhs = jnp.concatenate([own[j] for j in range(BLOCKS)], axis=1)
        rhs = jnp.concatenate([extt[map_ref[k, 0, j]] for j in range(BLOCKS)], axis=0)
        wg[k] = jnp.dot(lhs, rhs, preferred_element_type=F32)
        return 0

    def send(src, dst, h, i, dev):
        c = rcopy(src, dst, gsend.at[h, i], grecv.at[h, i], dev)
        c.start()
        sent.append(c)
        return c

    flight = [None] * PARTS
    xpart = lambda i: pl.ds(pl.multiple_of(i * XROWS, XROWS), XROWS)
    zpart = lambda i: pl.ds(pl.multiple_of(i * ZROWS, ZROWS), ZROWS)
    mine = pl.ds(pl.multiple_of(x * XROWS + z * ZROWS, ZROWS), ZROWS)

    def arrive(h):
        for c in flight[h]:
            c.wait_recv()

    def each_k(h, body):
        def one(k, _):
            body(k + KFIRST[h], pl.ds(pl.multiple_of(k * LOC, LOC), LOC))
            return 0

        lax.fori_loop(0, KCOUNT[h], one, 0)

    def step0(h):
        def cut(k, rows):
            give[h, rows, :] = jnp.where(core == 0, wg[k, :, BLOCK:], wg[k, :, :BLOCK]).astype(BF16)

        each_k(h, cut)
        rows = pl.ds(0, KCOUNT[h] * LOC)
        flight[h] = [send(give.at[h, rows], given.at[h, rows], h, 0, mate)]

    def step1(h):
        arrive(h)

        def add(k, rows):
            keep = jnp.where(core == 0, wg[k, :, :BLOCK], wg[k, :, BLOCK:])
            xbuf[h, rows, :] = (keep + given[h, rows, :].astype(F32)).astype(BF16)

        each_k(h, add)
        rest = WROWS - KCOUNT[h] * LOC
        if rest:
            xbuf[h, pl.ds(KCOUNT[h] * LOC, rest), :] = jnp.zeros((rest, BLOCK), BF16)
        flight[h] = [
            send(xbuf.at[h, xpart(lax.rem(x + d, 4))], xin.at[h, d - 1], h, d, xpeers[d - 1]) for d in range(1, 4)
        ]

    def step2(h):
        arrive(h)
        t = xbuf[h, xpart(x), :].astype(F32)
        for d in range(3):
            t = t + xin[h, d].astype(F32)
        zbuf[h] = t.astype(BF16)
        flight[h] = [
            send(zbuf.at[h, zpart(lax.rem(z + d, 8))], zin.at[h, d - 1], h, 3 + d, zpeers[d - 1]) for d in range(1, 8)
        ]

    def step3(h):
        arrive(h)
        t = zbuf[h, zpart(z), :].astype(F32)
        for d in range(7):
            t = t + zin[h, d].astype(F32)
        res[h, 0, mine, :] = t.astype(BF16)
        flight[h] = [
            send(res.at[h, 0, mine], res.at[h, 0, mine], h, 10 + d, zpeers[d - 1]) for d in range(1, 8)
        ]

    def step4(h):
        arrive(h)
        part = xpart(x)
        flight[h] = [
            send(res.at[h, 0, part], res.at[h, 0, part], h, 17 + d, xpeers[d - 1]) for d in range(1, 4)
        ]

    def step5(h):
        arrive(h)
        rows = pl.ds(0, KCOUNT[h] * LOC)
        flight[h] = [send(res.at[h, 0, rows], res.at[h, 1, rows], h, 21, mate)]

    def kterms(first, last):
        lax.fori_loop(first, last, kterm, 0)

    kterms(0, 8)
    step0(0)
    gather.forward(0)
    kterms(8, 12)
    step1(0)
    kterms(12, 14)
    gather.forward(1)
    kterms(14, 16)
    step0(1)
    kterms(16, 20)
    gather.forward(2)
    step2(0)
    step1(1)
    kterms(20, 24)
    step0(2)
    kterms(24, 25)
    gather.forward(3)
    kterms(25, 27)
    step0(3)
    step2(1)
    step1(2)

    def tile(t, _):
        halves = []
        for e in (2 * t, 2 * t + 1):
            halves.append(jnp.concatenate([own[e], from_dn[e], from_up[e], opp[e]], axis=0))
        rhs = jnp.concatenate(halves, axis=1)
        r = jnp.dot(win[pl.ds(0, OFFSETS * LOC), :], rhs, preferred_element_type=F32)
        r = r.astype(BF16)
        place = 2 * OFFSETS * t
        prod[pl.ds(place, OFFSETS)] = r[:, :BLOCK].reshape(OFFSETS, LOC, BLOCK)
        prod[pl.ds(place + OFFSETS, OFFSETS)] = r[:, BLOCK:].reshape(OFFSETS, LOC, BLOCK)
        return 0

    def tiles(i):
        gather.wait_part(i)
        lax.fori_loop(2 * i, 2 * i + 2, tile, 0)
        lax.fori_loop(2 * i + 8, 2 * i + 10, tile, 0)

    tiles(0)
    step1(3)
    step3(0)
    tiles(1)
    step2(2)
    tiles(2)
    step2(3)
    step3(1)
    tiles(3)
    step4(0)

    def walk(g, acc):
        for u in range(WALK):
            row, col = g // (BLOCK // WALK), lax.rem(g, BLOCK // WALK) * WALK + u
            term = prod[meta_ref[row, col]].astype(F32)
            acc = jnp.where(meta_ref[8 + row, col] > 0, 0.0, acc) + term
            run[g * WALK + u] = acc
        return acc

    third = OFFSETS * BLOCKS // WALK // 3
    acc = lax.fori_loop(0, third, walk, jnp.zeros((LOC, BLOCK), F32))
    step3(2)
    acc = lax.fori_loop(third, 2 * third, walk, acc)
    step3(3)
    step4(1)
    lax.fori_loop(2 * third, 3 * third, walk, acc)
    step5(0)

    def total(d):
        return jnp.where(meta_ref[15, d] > 0, run[meta_ref[7, d]], 0.0)

    for s in range(2 * SLOTS):
        fout[s // SLOTS, s % SLOTS] = total(BLOCKS + s).astype(BF16)
    fcopies = []
    for d, dev in enumerate((below, above)):
        c = rcopy(fout.at[d], fin.at[d], fsend.at[d], frecv.at[d], dev)
        c.start()
        fcopies.append(c)
    sent += fcopies

    def keep(d, _):
        eg[d] = total(d)
        return 0

    lax.fori_loop(0, BLOCKS, keep, 0)
    step4(2)
    step4(3)
    step5(1)
    for c in fcopies:
        c.wait_recv()
    step5(2)
    step5(3)
    for h in range(PARTS):
        arrive(h)
    gather.wait_sends()
    for c in sent:
        c.wait_send()


def norm_call(send, kmap, meta, conv, sums, out_grad, occ, gain, shift, ext, parts):
    quarter = pltpu.VMEM((BLOCKS, LOC, BLOCK), BF16)
    dma = pltpu.SemaphoreType.DMA
    return pl.pallas_call(
        norm_kernel,
        out_shape=(
            jax.ShapeDtypeStruct((LOC, BLOCKS * BLOCK), BF16),
            jax.ShapeDtypeStruct((BLOCKS, LOC, BLOCK), F32),
            jax.ShapeDtypeStruct((2, SLOTS, LOC, BLOCK), BF16),
            jax.ShapeDtypeStruct((PARTS, 2, WROWS, BLOCK), BF16),
            jax.ShapeDtypeStruct((1, BLOCK), F32),
        ),
        in_specs=[SMEM] * 3 + [VMEM, VMEM, ANY, VMEM, VMEM, VMEM, ANY, VMEM],
        out_specs=(VMEM,) * 5,
        scratch_shapes=[
            pltpu.VMEM((LOC, BLOCKS * BLOCK), BF16),
            pltpu.VMEM((EXT + 1, CH, BLOCK), BF16),
            pltpu.VMEM((2, LOC // 2, WPAD), BF16),
            pltpu.VMEM((EXT + 1, BLOCK, CH), BF16),
            pltpu.VMEM((OFFSETS, LOC, CH), F32),
            pltpu.VMEM((CH, WPAD), BF16),
            pltpu.VMEM((WPAD, CH), BF16),
            pltpu.VMEM((OFFSETS * BLOCKS, LOC, BLOCK), BF16),
            pltpu.VMEM((OFFSETS * BLOCKS, LOC, BLOCK), F32),
            quarter,
            quarter,
            quarter,
            quarter,
            pltpu.VMEM((2, 8, 2, BLOCK), F32),
            pltpu.VMEM((2, 8, 1, BLOCK), F32),
            pltpu.VMEM((2, SLOTS, LOC, BLOCK), BF16),
            pltpu.VMEM((PARTS, WROWS, BLOCK), BF16),
            pltpu.VMEM((PARTS, WROWS, BLOCK), BF16),
            pltpu.VMEM((PARTS, WROWS, BLOCK), BF16),
            pltpu.VMEM((PARTS, 3, XROWS, BLOCK), BF16),
            pltpu.VMEM((PARTS, XROWS, BLOCK), BF16),
            pltpu.VMEM((PARTS, 7, ZROWS, BLOCK), BF16),
            dma((3 * NCHUNK,)),
            dma((3 * NCHUNK,)),
            dma((2, 2, 7)),
            dma((2, 2, 7)),
            dma((6,)),
            dma((6,)),
            dma((2,)),
            dma((2,)),
            dma((PARTS, 22)),
            dma((PARTS, 22)),
            dma((2,)),
        ],
        compiler_params=params(2),
        name="norm",
    )(send, kmap, meta, conv, sums, out_grad, occ, gain, shift, ext, parts)


def emit_kernel(
    send_ref, out_ref, eg_ref, fin_ref, res_ref, stat_ref, occ_ref, out_to, in_to, wg_to, gain_to, shift_to, acc
):
    out_to[...] = out_ref[...]
    b = lax.axis_index("box")
    core = lax.rem(b, 2)
    for h in range(PARTS):

        def put(k, _):
            rows = pl.ds(pl.multiple_of(k * LOC, LOC), LOC)
            m, o = res_ref[h, 0, rows, :].astype(F32), res_ref[h, 1, rows, :].astype(F32)
            wg_to[k + KFIRST[h], :, :BLOCK] = jnp.where(core == 0, m, o)
            wg_to[k + KFIRST[h], :, BLOCK:] = jnp.where(core == 0, o, m)
            return 0

        lax.fori_loop(0, KCOUNT[h], put, 0)
    shift_to[...] = stat_ref[:, :LOC]
    gain_to[...] = stat_ref[:, LOC:]
    acc[pl.ds(0, BLOCKS)] = eg_ref[...]
    acc[BLOCKS] = jnp.zeros((LOC, BLOCK), F32)
    for d, ok in ((0, b < NBOX - 1), (1, b > 0)):
        for s in range(SLOTS):
            at = send_ref[0, 1 - d, s]
            acc[at] = acc[at] + jnp.where(ok, fin_ref[d, s].astype(F32), 0.0)

    def settle(d, _):
        in_to[:, pl.ds(pl.multiple_of(d * BLOCK, BLOCK), BLOCK)] = (occ_of(occ_ref, d) * acc[d]).astype(BF16)
        return 0

    lax.fori_loop(0, BLOCKS, settle, 0)


def emit_call(send, occ, out_features, eg, fin, res, stat):
    whole = jax.ShapeDtypeStruct((LOC, BLOCKS * BLOCK), BF16)
    line = jax.ShapeDtypeStruct((1, LOC), F32)
    return pl.pallas_call(
        emit_kernel,
        out_shape=(whole, whole, jax.ShapeDtypeStruct((OFFSETS, LOC, CH), F32), line, line),
        in_specs=[SMEM] + [VMEM] * 6,
        out_specs=(VMEM,) * 5,
        scratch_shapes=[pltpu.VMEM((BLOCKS + 1, LOC, BLOCK), F32)],
        compiler_params=params(),
        name="emit",
    )(send, out_features, eg, fin, res, stat, occ)


def per_device(
    features, occupied, send_lists, kernel_map, weights, norm_gain, norm_shift, out_grad
):
    occ = occupied.reshape(BLOCKS, 1, BLOCK)
    w = weights.reshape(OFFSETS * LOC, CH)
    kernel_map = kernel_map.transpose(1, 0, 2)
    gain, shift = norm_gain.reshape(1, LOC), norm_shift.reshape(1, LOC)
    conv, sums, ext, parts, meta = conv_call(send_lists, kernel_map, features, occ, w)
    results = norm_call(send_lists, kernel_map, meta, conv, sums, out_grad, occ, gain, shift, ext, parts)
    out_features, in_grad, weight_grad, gain_grad, shift_grad = emit_call(send_lists, occ, *results)
    return (out_features, in_grad, weight_grad, gain_grad.reshape(LOC), shift_grad.reshape(LOC))


def solution(mesh):
    in_specs = (
        P("ch", "box"),
        P("box"),
        P("box", None, None),
        P("box", None, None),
        P(None, "ch", None),
        P("ch"),
        P("ch"),
        P("ch", "box"),
    )
    out_specs = (P("ch", "box"), P("ch", "box"), P(None, "ch", None), P("ch"), P("ch"))
    return jax.shard_map(
        per_device, mesh=mesh, in_specs=in_specs, out_specs=out_specs, check_vma=False
    )
```

```python
import functools

import jax
import jax.numpy as jnp
from jax import lax
from jax.experimental import pallas as pl
from jax.experimental.pallas import tpu as pltpu
from jax.sharding import PartitionSpec as P

F32 = jnp.float32
BF16 = jnp.bfloat16
MESH = pl.DeviceIdType.MESH
VMEM = pl.BlockSpec(memory_space=pltpu.VMEM)
SMEM = pl.BlockSpec(memory_space=pltpu.SMEM)
ANY = pl.BlockSpec(memory_space=pl.ANY)
VMEM_LIMIT = 62 * 2**20

BLOCK = 128
BLOCKS = 32
CHUNK = 4
NCHUNK = 8
NFWD = 4
SLOTS = 8
EXT = BLOCKS + 2 * SLOTS
OFFSETS = 27
CH = 256
LOC = 64
WPAD = 1792
PARTS = 4
KFIRST = (0, 8, 16, 24)
KCOUNT = (8, 8, 8, 3)
WROWS = 512
XROWS = WROWS // 4
ZROWS = XROWS // 8
NBOX = 64
WALK = 16


def params(cid=None):
    if cid is None:
        return pltpu.CompilerParams(vmem_limit_bytes=VMEM_LIMIT)
    return pltpu.CompilerParams(
        vmem_limit_bytes=VMEM_LIMIT, collective_id=cid, has_side_effects=True
    )


def rcopy(src, dst, ssem, rsem, dev):
    return pltpu.make_async_remote_copy(
        src_ref=src, dst_ref=dst, send_sem=ssem, recv_sem=rsem, device_id=dev, device_id_type=MESH
    )


def greet(devs):
    barrier = pltpu.get_barrier_semaphore()
    for dev in devs:
        pl.semaphore_signal(barrier, inc=1, device_id=dev, device_id_type=MESH)
    pl.semaphore_wait(barrier, len(devs))


def occ_of(occ_ref, j):
    return occ_ref[j].astype(F32)


def rows_of(q):
    return pl.ds(pl.multiple_of(q * LOC, LOC), LOC)


class YGather:
    def __init__(self, own, from_dn, from_up, opp, ssem, rsem):
        q = lax.axis_index("ch")
        self.up = {"ch": lax.rem(q + 1, 4)}
        self.dn = {"ch": lax.rem(q + 3, 4)}
        self.refs = own, from_dn, from_up, opp
        self.sems = ssem, rsem

    def copy(self, src, dst, chunk, i, dev):
        part = pl.ds(chunk * CHUNK, CHUNK)
        return rcopy(src.at[part], dst.at[part], self.sems[0].at[i], self.sems[1].at[i], dev)

    def own_up(self, c):
        return self.copy(self.refs[0], self.refs[1], c, c, self.up)

    def own_dn(self, c):
        return self.copy(self.refs[0], self.refs[2], c, NCHUNK + c, self.dn)

    def far_up(self, c):
        return self.copy(self.refs[1], self.refs[3], c, 2 * NCHUNK + c, self.up)

    def far_dn(self, c):
        return self.copy(self.refs[2], self.refs[3], c, 2 * NCHUNK + c, self.dn)

    def start(self):
        for c in range(2):
            self.own_up(c).start()
            self.own_dn(NFWD + c).start()

    def start_near(self):
        for c in range(NFWD):
            self.own_up(c).start()
            self.own_dn(NFWD + c).start()

    def advance(self, i):
        self.own_up(i).wait_recv()
        self.own_up(NFWD + i).start()
        self.own_dn(NFWD + i).wait_recv()
        self.own_dn(i).start()

    def start_far(self):
        for c in range(NFWD):
            self.far_up(c).start()
            self.far_dn(NFWD + c).start()

    def wait_near(self):
        for c in range(NFWD):
            self.own_up(NFWD + c).wait_recv()
            self.own_dn(c).wait_recv()

    def wait_far(self, i):
        self.far_up(i).wait_recv()
        self.far_dn(NFWD + i).wait_recv()

    def forward(self, i):
        self.own_up(i).wait_recv()
        self.far_up(i).start()
        self.own_up(NFWD + i).start()
        self.own_dn(NFWD + i).wait_recv()
        self.far_dn(NFWD + i).start()
        self.own_dn(i).start()
        if i + 2 < NFWD:
            self.own_up(i + 2).start()
            self.own_dn(NFWD + i + 2).start()

    def wait_part(self, i):
        self.own_up(NFWD + i).wait_recv()
        self.own_dn(i).wait_recv()
        self.far_up(i).wait_recv()
        self.far_dn(NFWD + i).wait_recv()

    def wait_sends(self):
        for c in range(NCHUNK):
            self.own_up(c).wait_send()
            self.own_dn(c).wait_send()
        for c in range(NFWD):
            self.far_up(c).wait_send()
            self.far_dn(NFWD + c).wait_send()


def pair_places():
    return lax.broadcasted_iota(jnp.int32, (8, BLOCK), 0) * BLOCK + lax.broadcasted_iota(jnp.int32, (8, BLOCK), 1)


def pair_targets(map_ref):
    at = pair_places()

    def fill(k, target):
        for j in range(BLOCKS):
            target = jnp.where(at == k * BLOCKS + j, map_ref[k, 0, j], target)
        return target

    return lax.fori_loop(0, OFFSETS, fill, jnp.full((8, BLOCK), 63, jnp.int32))


def pair_ranks(map_ref, target):
    keys = target * 1024 + pair_places()

    def count(k, rank):
        for j in range(BLOCKS):
            rank = rank + (keys > map_ref[k, 0, j] * 1024 + (k * BLOCKS + j)).astype(jnp.int32)
        return rank

    return lax.fori_loop(0, OFFSETS, count, jnp.zeros((8, BLOCK), jnp.int32))


def sort_pairs(target, rank):
    lane = lax.broadcasted_iota(jnp.int32, (BLOCK, BLOCK), 1)
    sub = lax.broadcasted_iota(jnp.int32, (BLOCK, BLOCK), 0)
    pair = [jnp.zeros((1, BLOCK), F32) for _ in range(7)]
    goal = [jnp.zeros((1, BLOCK), F32) for _ in range(7)]
    last = jnp.full((1, BLOCK), -1.0, F32)
    for s in range(7):
        rcol = jnp.broadcast_to(rank[s : s + 1, :].astype(F32), (BLOCK, BLOCK)).T
        tcol = jnp.broadcast_to(target[s : s + 1, :].astype(F32), (BLOCK, BLOCK)).T
        i = sub + s * BLOCK
        number = (lax.rem(i, BLOCKS) * OFFSETS + i // BLOCKS).astype(F32)
        for r in range(7):
            hit = rcol == (lane + r * BLOCK).astype(F32)
            pair[r] = pair[r] + jnp.sum(jnp.where(hit, number, 0.0), axis=0, keepdims=True)
            goal[r] = goal[r] + jnp.sum(jnp.where(hit, tcol, 0.0), axis=0, keepdims=True)
        mine = tcol == lane.astype(F32)
        last = jnp.maximum(last, jnp.max(jnp.where(mine, rcol, -1.0), axis=0, keepdims=True))
    fresh = []
    first = lax.broadcasted_iota(jnp.int32, (1, BLOCK), 1) == 0
    for r in range(7):
        before = pltpu.roll(goal[r], 1, 1)
        carry = pltpu.roll(goal[r - 1], 1, 1) if r else jnp.full((1, BLOCK), -1.0, F32)
        before = jnp.where(first, carry, before)
        fresh.append(jnp.where(goal[r] == before, 0.0, 1.0))
    some = [jnp.where(last >= 0.0, 1.0, 0.0)]
    return jnp.concatenate(pair + [jnp.maximum(last, 0.0)] + fresh + some, axis=0).astype(jnp.int32)


def conv_kernel(
    send_ref,
    map_ref,
    feat_ref,
    occ_ref,
    w_ref,
    conv_ref,
    sum_ref,
    ext_to,
    parts_ref,
    meta_ref,
    ext,
    own,
    from_dn,
    from_up,
    opp,
    fout,
    fin,
    prod,
    ysend,
    yrecv,
    fsend,
    frecv,
    esem,
):
    q = lax.axis_index("ch")
    b = lax.axis_index("box")
    above = {"box": lax.rem(b + 1, NBOX)}
    below = {"box": lax.rem(b + NBOX - 1, NBOX)}
    gather = YGather(own, from_dn, from_up, opp, ysend, yrecv)
    quarters = ((q, own), (lax.rem(q + 3, 4), from_dn), (lax.rem(q + 1, 4), from_up), (lax.rem(q + 2, 4), opp))

    def mask(e, _):
        x = feat_ref[:, pl.ds(pl.multiple_of(e * BLOCK, BLOCK), BLOCK)].astype(F32)
        own[e] = (x * occ_of(occ_ref, e)).astype(BF16)
        return 0

    lax.fori_loop(0, BLOCKS, mask, 0)
    greet([gather.up, gather.dn, above, below])
    gather.start_near()

    def pack(r, src):
        for d in range(2):
            for s in range(SLOTS):
                pick = send_ref[0, d, s]
                blk = src[jnp.minimum(pick, BLOCKS - 1)].astype(F32)
                fout[r, d, s] = jnp.where(pick < BLOCKS, blk, 0.0).astype(BF16)
        for c in face_copies(r):
            c.start()

    def face_copies(r):
        return (
            rcopy(fout.at[r, 1], fin.at[r, 0], fsend.at[r, 1], frecv.at[r, 0], above),
            rcopy(fout.at[r, 0], fin.at[r, 1], fsend.at[r, 0], frecv.at[r, 1], below),
        )

    def tile(t):
        rhs = jnp.concatenate([ext[2 * t], ext[2 * t + 1]], axis=1)
        res = jnp.dot(w_ref[...], rhs, preferred_element_type=F32)
        prod[2 * t] = res[:, :BLOCK]
        prod[2 * t + 1] = res[:, BLOCK:]

    def face_rows():
        keep = jnp.where(b > 0, 1.0, 0.0), jnp.where(b < NBOX - 1, 1.0, 0.0)
        for r, (r_abs, _) in enumerate(quarters):
            for c in face_copies(r):
                c.wait_recv()
            rows = rows_of(r_abs)
            for d in range(2):
                for s in range(SLOTS):
                    ext[BLOCKS + d * SLOTS + s, rows, :] = (fin[r, d, s].astype(F32) * keep[d]).astype(BF16)

    def two_tiles(p, _):
        first = jnp.where(p < NCHUNK, 2 * (p // 2) + NCHUNK * lax.rem(p, 2), 2 * p)

        @pl.when((p < NCHUNK) & (lax.rem(p, 2) == 0))
        def _():
            gather.wait_far(p // 2)

        @pl.when(p == NCHUNK - 2)
        def _():
            pack(3, opp)

        @pl.when(p < NCHUNK)
        def _():
            for r_abs, src in quarters:
                rows = rows_of(r_abs)
                for e in range(CHUNK):
                    ext[2 * first + e, rows, :] = src[2 * first + e]

        @pl.when(p == NCHUNK)
        def _():
            face_rows()

        tile(first)
        tile(first + 1)
        return 0

    pack(0, own)
    prod[EXT] = jnp.zeros((OFFSETS * LOC, BLOCK), F32)
    ext[EXT] = jnp.zeros((CH, BLOCK), BF16)
    low = lax.broadcasted_iota(jnp.int32, (LOC, BLOCK), 1) < LOC

    def columns(p, _):
        for h in range(2):
            cols = pl.ds(h * BLOCK, BLOCK)
            first = w_ref[pl.ds(pl.multiple_of(2 * p * LOC, LOC), LOC), cols].astype(F32)
            row = jnp.minimum(2 * p + 1, OFFSETS - 1) * LOC
            second = w_ref[pl.ds(pl.multiple_of(row, LOC), LOC), cols].astype(F32)
            second = jnp.where(2 * p + 1 < OFFSETS, second, 0.0)
            put = pl.ds(pl.multiple_of(p * BLOCK, BLOCK), BLOCK)
            parts_ref[2 * h, :, put] = jnp.where(low, first, pltpu.roll(second, LOC, 1)).astype(BF16)
            parts_ref[2 * h + 1, :, put] = jnp.where(low, pltpu.roll(first, LOC, 1), second).astype(BF16)
        return 0

    lax.fori_loop(0, WPAD // BLOCK, columns, 0)
    gather.advance(0)
    target = pair_targets(map_ref)
    gather.advance(1)
    rank = pair_ranks(map_ref, target)
    gather.advance(2)
    meta_ref[...] = sort_pairs(target, rank)
    gather.advance(3)
    gather.start_far()
    gather.wait_near()
    pack(1, from_dn)
    pack(2, from_up)
    lax.fori_loop(0, EXT // 4, two_tiles, 0)
    leave = pltpu.make_async_copy(ext, ext_to, esem)
    leave.start()

    def out(j, carry):
        a, s = carry
        acc = prod[map_ref[0, 0, j], pl.ds(0, LOC), :]
        for k in range(1, OFFSETS):
            acc = acc + prod[map_ref[k, 0, j], pl.ds(LOC * k, LOC), :]
        conv_ref[j] = acc
        o = occ_of(occ_ref, j) * acc
        return a + o, s + o * acc

    zero = jnp.zeros((LOC, BLOCK), F32)
    a, s = lax.fori_loop(0, BLOCKS, out, (zero, zero), unroll=2)
    sum_ref[0] = a
    sum_ref[1] = s
    leave.wait()
    gather.wait_sends()
    for r in range(4):
        for c in face_copies(r):
            c.wait_send()


def conv_call(send, kmap, features, occ, w):
    quarter = pltpu.VMEM((BLOCKS, LOC, BLOCK), BF16)
    faces = pltpu.VMEM((4, 2, SLOTS, LOC, BLOCK), BF16)
    dma = pltpu.SemaphoreType.DMA
    return pl.pallas_call(
        conv_kernel,
        out_shape=(
            jax.ShapeDtypeStruct((BLOCKS, LOC, BLOCK), F32),
            jax.ShapeDtypeStruct((2, LOC, BLOCK), F32),
            jax.ShapeDtypeStruct((EXT + 1, CH, BLOCK), BF16),
            jax.ShapeDtypeStruct((4, LOC, WPAD), BF16),
            jax.ShapeDtypeStruct((16, BLOCK), jnp.int32),
        ),
        in_specs=[SMEM, SMEM, VMEM, VMEM, VMEM],
        out_specs=(VMEM, VMEM, ANY, VMEM, VMEM),
        scratch_shapes=[
            pltpu.VMEM((EXT + 1, CH, BLOCK), BF16),
            quarter,
            quarter,
            quarter,
            quarter,
            faces,
            faces,
            pltpu.VMEM((EXT + 1, OFFSETS * LOC, BLOCK), F32),
            dma((3 * NCHUNK,)),
            dma((3 * NCHUNK,)),
            dma((4, 2)),
            dma((4, 2)),
            dma,
        ],
        compiler_params=params(1),
        name="conv",
    )(send, kmap, features, occ, w)


def lane_masks():
    ch = lax.broadcasted_iota(jnp.int32, (LOC, BLOCK), 0)
    lane = lax.broadcasted_iota(jnp.int32, (LOC, BLOCK), 1)
    return lane == ch, lane == ch + LOC


def to_row(first, second):
    m0, m1 = lane_masks()
    c0 = jnp.sum(first, axis=1, keepdims=True)
    c1 = jnp.sum(second, axis=1, keepdims=True)
    return jnp.sum(jnp.where(m0, c0, 0.0) + jnp.where(m1, c1, 0.0), axis=0, keepdims=True)


def to_cols(row):
    m0, m1 = lane_masks()
    return (
        jnp.sum(jnp.where(m0, row, 0.0), axis=1, keepdims=True),
        jnp.sum(jnp.where(m1, row, 0.0), axis=1, keepdims=True),
    )


def at_box(x, z, core):
    return {"box": x * 16 + z * 2 + core}


def to_col(row):
    ch = lax.broadcasted_iota(jnp.int32, (LOC, LOC), 0)
    lane = lax.broadcasted_iota(jnp.int32, (LOC, LOC), 1)
    return jnp.sum(jnp.where(ch == lane, row, 0.0), axis=1, keepdims=True)


def box_groups():
    b = lax.axis_index("box")
    x, z, core = b // 16, lax.rem(b // 2, 8), lax.rem(b, 2)
    first = [at_box(lax.rem(x + d // 2, 4), z, lax.rem(core + d % 2, 2)) for d in range(1, 8)]
    second = [at_box(x, lax.rem(z + d, 8), core) for d in range(1, 8)]
    return (x * 2 + core, first), (z, second)


def box_sum(mine, buf, ssem, rsem, idle):
    sent = []
    for step, (me, peers) in enumerate(box_groups()):
        buf[step, me] = mine
        copies = []
        for d, dev in enumerate(peers):
            c = rcopy(buf.at[step, me], buf.at[step, me], ssem.at[step, d], rsem.at[step, d], dev)
            c.start()
            copies.append(c)
        idle(step)
        for c in copies:
            c.wait_recv()
        mine = buf[step, 0]
        for d in range(1, 8):
            mine = mine + buf[step, d]
        sent += copies
    return mine, sent


def norm_kernel(
    send_ref,
    map_ref,
    meta_ref,
    conv_ref,
    sum_ref,
    grad_from,
    occ_ref,
    gain_ref,
    shift_ref,
    ext_from,
    parts_ref,
    out_ref,
    eg,
    fin,
    res,
    stat_ref,
    grad_ref,
    ext_ref,
    relay,
    extt,
    wg,
    wrecv,
    win,
    prod,
    run,
    own,
    from_dn,
    from_up,
    opp,
    sbuf,
    sbuf2,
    fout,
    give,
    given,
    xbuf,
    xin,
    zbuf,
    zin,
    ysend,
    yrecv,
    ssend,
    srecv,
    wsend,
    wrecvs,
    fsend,
    frecv,
    gsend,
    grecv,
    lsem,
):
    q = lax.axis_index("ch")
    b = lax.axis_index("box")
    x, z, core = b // 16, lax.rem(b // 2, 8), lax.rem(b, 2)
    gather = YGather(own, from_dn, from_up, opp, ysend, yrecv)
    (_, near), (_, far) = box_groups()
    above = {"box": lax.rem(b + 1, NBOX)}
    below = {"box": lax.rem(b + NBOX - 1, NBOX)}
    mate = at_box(x, z, 1 - core)
    xpeers = [at_box(lax.rem(x + d, 4), z, core) for d in range(1, 4)]
    zpeers = far
    sent = []
    loads = [pltpu.make_async_copy(ext_from, ext_ref, lsem.at[0]), pltpu.make_async_copy(grad_from, grad_ref, lsem.at[1])]
    for c in loads:
        c.start()

    count = jnp.sum(occ_ref[...].astype(F32), axis=0)
    count = jnp.broadcast_to(jnp.sum(count, axis=1, keepdims=True), (1, BLOCK))
    row = to_row(sum_ref[0], sum_ref[1])
    sub = lax.broadcasted_iota(jnp.int32, (2, BLOCK), 0)
    pay = jnp.where(sub == 0, row, count)
    greet([gather.up, gather.dn] + near + far + [above, below])
    wcopies = []

    def wcopy(src, dst, i, dev):
        c = rcopy(src, dst, wsend.at[i], wrecvs.at[i], dev)
        wcopies.append(c)
        return c

    far_part = parts_ref.at[lax.rem(q + 2, 4)]
    near_rows, far_rows = pl.ds(0, LOC // 2), pl.ds(LOC // 2, LOC // 2)
    lead = [
        wcopy(far_part.at[near_rows], relay.at[0], 0, gather.up),
        wcopy(far_part.at[far_rows], relay.at[1], 1, gather.dn),
    ]
    tail = [
        wcopy(parts_ref.at[lax.rem(q + 1, 4)], wrecv.at[pl.ds(LOC, LOC)], 2, gather.up),
        wcopy(parts_ref.at[lax.rem(q + 3, 4)], wrecv.at[pl.ds(2 * LOC, LOC)], 3, gather.dn),
    ]
    tail_far = [
        wcopy(relay.at[0], wrecv.at[pl.ds(3 * LOC, LOC // 2)], 4, gather.up),
        wcopy(relay.at[1], wrecv.at[pl.ds(3 * LOC + LOC // 2, LOC // 2)], 5, gather.dn),
    ]
    for c in lead + tail:
        c.start()
    wrecv[pl.ds(0, LOC), :] = parts_ref[q]
    loads[0].wait()

    def flip(step):
        if step == 1:
            for c, d in zip(lead, tail_far):
                c.wait_recv()
                d.start()

        def one(e, _):
            extt[e] = ext_ref[e].T
            return 0

        lax.fori_loop(*((0, EXT // 2) if step == 0 else (EXT // 2, EXT + 1)), one, 0)

    tot, more = box_sum(pay, sbuf, ssend.at[0], srecv.at[0], flip)
    sent += wcopies + more
    loads[1].wait()
    n_vox = tot[1:2, 0:1]
    s1, s2 = to_cols(tot[0:1, :])
    mean = s1 / n_vox
    var = s2 / n_vox - mean * mean
    inv = 1.0 / jnp.sqrt(var + 1e-05)
    gain, shift = to_col(gain_ref[...]), to_col(shift_ref[...])

    def fwd(j, carry):
        a, s = carry
        cols = pl.ds(pl.multiple_of(j * BLOCK, BLOCK), BLOCK)
        occ = occ_of(occ_ref, j)
        nd = (conv_ref[j] - mean) * inv
        sh = nd * gain + shift
        out_ref[:, cols] = (occ * jnp.maximum(sh, 0.0)).astype(BF16)
        rg = jnp.where(sh > 0.0, occ * grad_ref[:, cols].astype(F32), 0.0)
        run[2 * j] = nd
        run[2 * j + 1] = rg
        return a + rg, s + rg * nd

    zero = jnp.zeros((LOC, BLOCK), F32)
    a, s = lax.fori_loop(0, BLOCKS, fwd, (zero, zero))
    row = to_row(a, s)

    def turn(step):
        if step == 0:
            return
        for c in tail + tail_far:
            c.wait_recv()
        for p in range(WPAD // BLOCK):
            win[pl.ds(p * BLOCK, BLOCK), :] = wrecv[:, pl.ds(p * BLOCK, BLOCK)].T

    tot, more = box_sum(row, sbuf2, ssend.at[1], srecv.at[1], turn)
    sent += more
    stat_ref[...] = tot
    sg, gg = to_cols(tot)
    scale = inv * gain
    sgm = sg / n_vox

    def bwd(j, _):
        nd, rg = run[2 * j], run[2 * j + 1]
        own[j] = (occ_of(occ_ref, j) * scale * (rg - sgm - nd * gg / n_vox)).astype(BF16)
        return 0

    lax.fori_loop(0, BLOCKS, bwd, 0)
    gather.start()

    def kterm(k, _):
        lhs = jnp.concatenate([own[j] for j in range(BLOCKS)], axis=1)
        rhs = jnp.concatenate([extt[map_ref[k, 0, j]] for j in range(BLOCKS)], axis=0)
        wg[k] = jnp.dot(lhs, rhs, preferred_element_type=F32)
        return 0

    def send(src, dst, h, i, dev):
        c = rcopy(src, dst, gsend.at[h, i], grecv.at[h, i], dev)
        c.start()
        sent.append(c)
        return c

    flight = [None] * PARTS
    xpart = lambda i: pl.ds(pl.multiple_of(i * XROWS, XROWS), XROWS)
    zpart = lambda i: pl.ds(pl.multiple_of(i * ZROWS, ZROWS), ZROWS)
    mine = pl.ds(pl.multiple_of(x * XROWS + z * ZROWS, ZROWS), ZROWS)

    def arrive(h):
        for c in flight[h]:
            c.wait_recv()

    def each_k(h, body):
        def one(k, _):
            body(k + KFIRST[h], pl.ds(pl.multiple_of(k * LOC, LOC), LOC))
            return 0

        lax.fori_loop(0, KCOUNT[h], one, 0)

    def step0(h):
        def cut(k, rows):
            give[h, rows, :] = jnp.where(core == 0, wg[k, :, BLOCK:], wg[k, :, :BLOCK]).astype(BF16)

        each_k(h, cut)
        rows = pl.ds(0, KCOUNT[h] * LOC)
        flight[h] = [send(give.at[h, rows], given.at[h, rows], h, 0, mate)]

    def step1(h):
        arrive(h)

        def add(k, rows):
            keep = jnp.where(core == 0, wg[k, :, :BLOCK], wg[k, :, BLOCK:])
            xbuf[h, rows, :] = (keep + given[h, rows, :].astype(F32)).astype(BF16)

        each_k(h, add)
        rest = WROWS - KCOUNT[h] * LOC
        if rest:
            xbuf[h, pl.ds(KCOUNT[h] * LOC, rest), :] = jnp.zeros((rest, BLOCK), BF16)
        flight[h] = [
            send(xbuf.at[h, xpart(lax.rem(x + d, 4))], xin.at[h, d - 1], h, d, xpeers[d - 1]) for d in range(1, 4)
        ]

    def step2(h):
        arrive(h)
        t = xbuf[h, xpart(x), :].astype(F32)
        for d in range(3):
            t = t + xin[h, d].astype(F32)
        zbuf[h] = t.astype(BF16)
        flight[h] = [
            send(zbuf.at[h, zpart(lax.rem(z + d, 8))], zin.at[h, d - 1], h, 3 + d, zpeers[d - 1]) for d in range(1, 8)
        ]

    def step3(h):
        arrive(h)
        t = zbuf[h, zpart(z), :].astype(F32)
        for d in range(7):
            t = t + zin[h, d].astype(F32)
        res[h, 0, mine, :] = t.astype(BF16)
        flight[h] = [
            send(res.at[h, 0, mine], res.at[h, 0, mine], h, 10 + d, zpeers[d - 1]) for d in range(1, 8)
        ]

    def step4(h):
        arrive(h)
        part = xpart(x)
        flight[h] = [
            send(res.at[h, 0, part], res.at[h, 0, part], h, 17 + d, xpeers[d - 1]) for d in range(1, 4)
        ]

    def step5(h):
        arrive(h)
        rows = pl.ds(0, KCOUNT[h] * LOC)
        flight[h] = [send(res.at[h, 0, rows], res.at[h, 1, rows], h, 21, mate)]

    def kterms(first, last):
        lax.fori_loop(first, last, kterm, 0)

    kterms(0, 8)
    step0(0)
    gather.forward(0)
    kterms(8, 12)
    step1(0)
    kterms(12, 14)
    gather.forward(1)
    kterms(14, 16)
    step0(1)
    kterms(16, 20)
    gather.forward(2)
    step2(0)
    step1(1)
    kterms(20, 24)
    step0(2)
    kterms(24, 25)
    gather.forward(3)
    kterms(25, 27)
    step0(3)
    step2(1)
    step1(2)

    def tile(t, _):
        halves = []
        for e in (2 * t, 2 * t + 1):
            halves.append(jnp.concatenate([own[e], from_dn[e], from_up[e], opp[e]], axis=0))
        rhs = jnp.concatenate(halves, axis=1)
        r = jnp.dot(win[pl.ds(0, OFFSETS * LOC), :], rhs, preferred_element_type=F32)
        r = r.astype(BF16)
        place = 2 * OFFSETS * t
        prod[pl.ds(place, OFFSETS)] = r[:, :BLOCK].reshape(OFFSETS, LOC, BLOCK)
        prod[pl.ds(place + OFFSETS, OFFSETS)] = r[:, BLOCK:].reshape(OFFSETS, LOC, BLOCK)
        return 0

    def tiles(i):
        gather.wait_part(i)
        lax.fori_loop(2 * i, 2 * i + 2, tile, 0)
        lax.fori_loop(2 * i + 8, 2 * i + 10, tile, 0)

    tiles(0)
    step1(3)
    step3(0)
    tiles(1)
    step2(2)
    tiles(2)
    step2(3)
    step3(1)
    tiles(3)
    step4(0)

    def walk(g, acc):
        for u in range(WALK):
            row, col = g // (BLOCK // WALK), lax.rem(g, BLOCK // WALK) * WALK + u
            term = prod[meta_ref[row, col]].astype(F32)
            acc = jnp.where(meta_ref[8 + row, col] > 0, 0.0, acc) + term
            run[g * WALK + u] = acc
        return acc

    third = OFFSETS * BLOCKS // WALK // 3
    acc = lax.fori_loop(0, third, walk, jnp.zeros((LOC, BLOCK), F32))
    step3(2)
    acc = lax.fori_loop(third, 2 * third, walk, acc)
    step3(3)
    step4(1)
    lax.fori_loop(2 * third, 3 * third, walk, acc)
    step5(0)

    def total(d):
        return jnp.where(meta_ref[15, d] > 0, run[meta_ref[7, d]], 0.0)

    for s in range(2 * SLOTS):
        fout[s // SLOTS, s % SLOTS] = total(BLOCKS + s).astype(BF16)
    fcopies = []
    for d, dev in enumerate((below, above)):
        c = rcopy(fout.at[d], fin.at[d], fsend.at[d], frecv.at[d], dev)
        c.start()
        fcopies.append(c)
    sent += fcopies

    def keep(d, _):
        eg[d] = total(d)
        return 0

    lax.fori_loop(0, BLOCKS, keep, 0)
    step4(2)
    step4(3)
    step5(1)
    for c in fcopies:
        c.wait_recv()
    step5(2)
    step5(3)
    for h in range(PARTS):
        arrive(h)
    gather.wait_sends()
    for c in sent:
        c.wait_send()


def norm_call(send, kmap, meta, conv, sums, out_grad, occ, gain, shift, ext, parts):
    quarter = pltpu.VMEM((BLOCKS, LOC, BLOCK), BF16)
    dma = pltpu.SemaphoreType.DMA
    return pl.pallas_call(
        norm_kernel,
        out_shape=(
            jax.ShapeDtypeStruct((LOC, BLOCKS * BLOCK), BF16),
            jax.ShapeDtypeStruct((BLOCKS, LOC, BLOCK), F32),
            jax.ShapeDtypeStruct((2, SLOTS, LOC, BLOCK), BF16),
            jax.ShapeDtypeStruct((PARTS, 2, WROWS, BLOCK), BF16),
            jax.ShapeDtypeStruct((1, BLOCK), F32),
        ),
        in_specs=[SMEM] * 3 + [VMEM, VMEM, ANY, VMEM, VMEM, VMEM, ANY, VMEM],
        out_specs=(VMEM,) * 5,
        scratch_shapes=[
            pltpu.VMEM((LOC, BLOCKS * BLOCK), BF16),
            pltpu.VMEM((EXT + 1, CH, BLOCK), BF16),
            pltpu.VMEM((2, LOC // 2, WPAD), BF16),
            pltpu.VMEM((EXT + 1, BLOCK, CH), BF16),
            pltpu.VMEM((OFFSETS, LOC, CH), F32),
            pltpu.VMEM((CH, WPAD), BF16),
            pltpu.VMEM((WPAD, CH), BF16),
            pltpu.VMEM((OFFSETS * BLOCKS, LOC, BLOCK), BF16),
            pltpu.VMEM((OFFSETS * BLOCKS, LOC, BLOCK), F32),
            quarter,
            quarter,
            quarter,
            quarter,
            pltpu.VMEM((2, 8, 2, BLOCK), F32),
            pltpu.VMEM((2, 8, 1, BLOCK), F32),
            pltpu.VMEM((2, SLOTS, LOC, BLOCK), BF16),
            pltpu.VMEM((PARTS, WROWS, BLOCK), BF16),
            pltpu.VMEM((PARTS, WROWS, BLOCK), BF16),
            pltpu.VMEM((PARTS, WROWS, BLOCK), BF16),
            pltpu.VMEM((PARTS, 3, XROWS, BLOCK), BF16),
            pltpu.VMEM((PARTS, XROWS, BLOCK), BF16),
            pltpu.VMEM((PARTS, 7, ZROWS, BLOCK), BF16),
            dma((3 * NCHUNK,)),
            dma((3 * NCHUNK,)),
            dma((2, 2, 7)),
            dma((2, 2, 7)),
            dma((6,)),
            dma((6,)),
            dma((2,)),
            dma((2,)),
            dma((PARTS, 22)),
            dma((PARTS, 22)),
            dma((2,)),
        ],
        compiler_params=params(2),
        name="norm",
    )(send, kmap, meta, conv, sums, out_grad, occ, gain, shift, ext, parts)


def emit_kernel(
    send_ref, out_ref, eg_ref, fin_ref, res_ref, stat_ref, occ_ref, out_to, in_to, wg_to, gain_to, shift_to, acc
):
    out_to[...] = out_ref[...]
    b = lax.axis_index("box")
    core = lax.rem(b, 2)
    for h in range(PARTS):

        def put(k, _):
            rows = pl.ds(pl.multiple_of(k * LOC, LOC), LOC)
            m, o = res_ref[h, 0, rows, :].astype(F32), res_ref[h, 1, rows, :].astype(F32)
            wg_to[k + KFIRST[h], :, :BLOCK] = jnp.where(core == 0, m, o)
            wg_to[k + KFIRST[h], :, BLOCK:] = jnp.where(core == 0, o, m)
            return 0

        lax.fori_loop(0, KCOUNT[h], put, 0)
    shift_to[...] = stat_ref[:, :LOC]
    gain_to[...] = stat_ref[:, LOC:]
    acc[pl.ds(0, BLOCKS)] = eg_ref[...]
    acc[BLOCKS] = jnp.zeros((LOC, BLOCK), F32)
    for d, ok in ((0, b < NBOX - 1), (1, b > 0)):
        for s in range(SLOTS):
            at = send_ref[0, 1 - d, s]
            acc[at] = acc[at] + jnp.where(ok, fin_ref[d, s].astype(F32), 0.0)

    def settle(d, _):
        in_to[:, pl.ds(pl.multiple_of(d * BLOCK, BLOCK), BLOCK)] = (occ_of(occ_ref, d) * acc[d]).astype(BF16)
        return 0

    lax.fori_loop(0, BLOCKS, settle, 0)


def emit_call(send, occ, out_features, eg, fin, res, stat):
    whole = jax.ShapeDtypeStruct((LOC, BLOCKS * BLOCK), BF16)
    line = jax.ShapeDtypeStruct((1, LOC), F32)
    return pl.pallas_call(
        emit_kernel,
        out_shape=(whole, whole, jax.ShapeDtypeStruct((OFFSETS, LOC, CH), F32), line, line),
        in_specs=[SMEM] + [VMEM] * 6,
        out_specs=(VMEM,) * 5,
        scratch_shapes=[pltpu.VMEM((BLOCKS + 1, LOC, BLOCK), F32)],
        compiler_params=params(),
        name="emit",
    )(send, out_features, eg, fin, res, stat, occ)


def per_device(
    features, occupied, send_lists, kernel_map, weights, norm_gain, norm_shift, out_grad
):
    occ = occupied.reshape(BLOCKS, 1, BLOCK)
    w = weights.reshape(OFFSETS * LOC, CH)
    kernel_map = kernel_map.transpose(1, 0, 2)
    gain, shift = norm_gain.reshape(1, LOC), norm_shift.reshape(1, LOC)
    conv, sums, ext, parts, meta = conv_call(send_lists, kernel_map, features, occ, w)
    results = norm_call(send_lists, kernel_map, meta, conv, sums, out_grad, occ, gain, shift, ext, parts)
    out_features, in_grad, weight_grad, gain_grad, shift_grad = emit_call(send_lists, occ, *results)
    return (out_features, in_grad, weight_grad, gain_grad.reshape(LOC), shift_grad.reshape(LOC))


def solution(mesh):
    in_specs = (
        P("ch", "box"),
        P("box"),
        P("box", None, None),
        P("box", None, None),
        P(None, "ch", None),
        P("ch"),
        P("ch"),
        P("ch", "box"),
    )
    out_specs = (P("ch", "box"), P("ch", "box"), P(None, "ch", None), P("ch"), P("ch"))
    return jax.shard_map(
        per_device, mesh=mesh, in_specs=in_specs, out_specs=out_specs, check_vma=False
    )
```

```python
import functools

import jax
import jax.numpy as jnp
from jax import lax
from jax.experimental import pallas as pl
from jax.experimental.pallas import tpu as pltpu
from jax.sharding import PartitionSpec as P

F32 = jnp.float32
BF16 = jnp.bfloat16
MESH = pl.DeviceIdType.MESH
VMEM = pl.BlockSpec(memory_space=pltpu.VMEM)
SMEM = pl.BlockSpec(memory_space=pltpu.SMEM)
ANY = pl.BlockSpec(memory_space=pl.ANY)
VMEM_LIMIT = 62 * 2**20

BLOCK = 128
BLOCKS = 32
CHUNK = 4
NCHUNK = 8
NFWD = 4
SLOTS = 8
EXT = BLOCKS + 2 * SLOTS
OFFSETS = 27
CH = 256
LOC = 64
WPAD = 1792
PARTS = 4
KFIRST = (0, 8, 16, 24)
KCOUNT = (8, 8, 8, 3)
WROWS = 512
XROWS = WROWS // 4
ZROWS = XROWS // 8
NBOX = 64
WALK = 16


def params(cid=None):
    if cid is None:
        return pltpu.CompilerParams(vmem_limit_bytes=VMEM_LIMIT)
    return pltpu.CompilerParams(
        vmem_limit_bytes=VMEM_LIMIT, collective_id=cid, has_side_effects=True
    )


def rcopy(src, dst, ssem, rsem, dev):
    return pltpu.make_async_remote_copy(
        src_ref=src, dst_ref=dst, send_sem=ssem, recv_sem=rsem, device_id=dev, device_id_type=MESH
    )


def greet(devs):
    barrier = pltpu.get_barrier_semaphore()
    for dev in devs:
        pl.semaphore_signal(barrier, inc=1, device_id=dev, device_id_type=MESH)
    return lambda: pl.semaphore_wait(barrier, len(devs))


def occ_of(occ_ref, j):
    return occ_ref[j].astype(F32)


def rows_of(q):
    return pl.ds(pl.multiple_of(q * LOC, LOC), LOC)


class YGather:
    def __init__(self, own, from_dn, from_up, opp, ssem, rsem):
        q = lax.axis_index("ch")
        self.up = {"ch": lax.rem(q + 1, 4)}
        self.dn = {"ch": lax.rem(q + 3, 4)}
        self.refs = own, from_dn, from_up, opp
        self.sems = ssem, rsem

    def copy(self, src, dst, chunk, i, dev):
        part = pl.ds(chunk * CHUNK, CHUNK)
        return rcopy(src.at[part], dst.at[part], self.sems[0].at[i], self.sems[1].at[i], dev)

    def own_up(self, c):
        return self.copy(self.refs[0], self.refs[1], c, c, self.up)

    def own_dn(self, c):
        return self.copy(self.refs[0], self.refs[2], c, NCHUNK + c, self.dn)

    def far_up(self, c):
        return self.copy(self.refs[1], self.refs[3], c, 2 * NCHUNK + c, self.up)

    def far_dn(self, c):
        return self.copy(self.refs[2], self.refs[3], c, 2 * NCHUNK + c, self.dn)

    def start(self):
        for c in range(2):
            self.own_up(c).start()
            self.own_dn(NFWD + c).start()

    def start_near(self):
        for c in range(NFWD):
            self.own_up(c).start()
            self.own_dn(NFWD + c).start()

    def advance(self, i):
        self.own_up(i).wait_recv()
        self.own_up(NFWD + i).start()
        self.own_dn(NFWD + i).wait_recv()
        self.own_dn(i).start()

    def start_far(self):
        for c in range(NFWD):
            self.far_up(c).start()
            self.far_dn(NFWD + c).start()

    def wait_near(self):
        for c in range(NFWD):
            self.own_up(NFWD + c).wait_recv()
            self.own_dn(c).wait_recv()

    def wait_far(self, i):
        self.far_up(i).wait_recv()
        self.far_dn(NFWD + i).wait_recv()

    def forward(self, i):
        self.own_up(i).wait_recv()
        self.far_up(i).start()
        self.own_up(NFWD + i).start()
        self.own_dn(NFWD + i).wait_recv()
        self.far_dn(NFWD + i).start()
        self.own_dn(i).start()
        if i + 2 < NFWD:
            self.own_up(i + 2).start()
            self.own_dn(NFWD + i + 2).start()

    def wait_part(self, i):
        self.own_up(NFWD + i).wait_recv()
        self.own_dn(i).wait_recv()
        self.far_up(i).wait_recv()
        self.far_dn(NFWD + i).wait_recv()

    def wait_sends(self):
        for c in range(NCHUNK):
            self.own_up(c).wait_send()
            self.own_dn(c).wait_send()
        for c in range(NFWD):
            self.far_up(c).wait_send()
            self.far_dn(NFWD + c).wait_send()


def pair_places():
    return lax.broadcasted_iota(jnp.int32, (8, BLOCK), 0) * BLOCK + lax.broadcasted_iota(jnp.int32, (8, BLOCK), 1)


def pair_targets(map_ref):
    at = pair_places()

    def fill(k, target):
        for j in range(BLOCKS):
            target = jnp.where(at == k * BLOCKS + j, map_ref[k, 0, j], target)
        return target

    return lax.fori_loop(0, OFFSETS, fill, jnp.full((8, BLOCK), 63, jnp.int32))


def pair_ranks(map_ref, target):
    keys = target * 1024 + pair_places()

    def count(k, rank):
        for j in range(BLOCKS):
            rank = rank + (keys > map_ref[k, 0, j] * 1024 + (k * BLOCKS + j)).astype(jnp.int32)
        return rank

    return lax.fori_loop(0, OFFSETS, count, jnp.zeros((8, BLOCK), jnp.int32))


def sort_pairs(target, rank):
    lane = lax.broadcasted_iota(jnp.int32, (BLOCK, BLOCK), 1)
    sub = lax.broadcasted_iota(jnp.int32, (BLOCK, BLOCK), 0)
    pair = [jnp.zeros((1, BLOCK), F32) for _ in range(7)]
    goal = [jnp.zeros((1, BLOCK), F32) for _ in range(7)]
    last = jnp.full((1, BLOCK), -1.0, F32)
    for s in range(7):
        rcol = jnp.broadcast_to(rank[s : s + 1, :].astype(F32), (BLOCK, BLOCK)).T
        tcol = jnp.broadcast_to(target[s : s + 1, :].astype(F32), (BLOCK, BLOCK)).T
        i = sub + s * BLOCK
        number = (lax.rem(i, BLOCKS) * OFFSETS + i // BLOCKS).astype(F32)
        for r in range(7):
            hit = rcol == (lane + r * BLOCK).astype(F32)
            pair[r] = pair[r] + jnp.sum(jnp.where(hit, number, 0.0), axis=0, keepdims=True)
            goal[r] = goal[r] + jnp.sum(jnp.where(hit, tcol, 0.0), axis=0, keepdims=True)
        mine = tcol == lane.astype(F32)
        last = jnp.maximum(last, jnp.max(jnp.where(mine, rcol, -1.0), axis=0, keepdims=True))
    fresh = []
    first = lax.broadcasted_iota(jnp.int32, (1, BLOCK), 1) == 0
    for r in range(7):
        before = pltpu.roll(goal[r], 1, 1)
        carry = pltpu.roll(goal[r - 1], 1, 1) if r else jnp.full((1, BLOCK), -1.0, F32)
        before = jnp.where(first, carry, before)
        fresh.append(jnp.where(goal[r] == before, 0.0, 1.0))
    some = [jnp.where(last >= 0.0, 1.0, 0.0)]
    return jnp.concatenate(pair + [jnp.maximum(last, 0.0)] + fresh + some, axis=0).astype(jnp.int32)


def conv_kernel(
    send_ref,
    map_ref,
    feat_ref,
    occ_ref,
    w_ref,
    conv_ref,
    sum_ref,
    ext_to,
    parts_ref,
    meta_ref,
    ext,
    own,
    from_dn,
    from_up,
    opp,
    fout,
    fin,
    prod,
    ysend,
    yrecv,
    fsend,
    frecv,
    esem,
):
    q = lax.axis_index("ch")
    b = lax.axis_index("box")
    above = {"box": lax.rem(b + 1, NBOX)}
    below = {"box": lax.rem(b + NBOX - 1, NBOX)}
    gather = YGather(own, from_dn, from_up, opp, ysend, yrecv)
    quarters = ((q, own), (lax.rem(q + 3, 4), from_dn), (lax.rem(q + 1, 4), from_up), (lax.rem(q + 2, 4), opp))

    all_here = greet([gather.up, gather.dn, above, below])

    def mask(e, _):
        x = feat_ref[:, pl.ds(pl.multiple_of(e * BLOCK, BLOCK), BLOCK)].astype(F32)
        own[e] = (x * occ_of(occ_ref, e)).astype(BF16)
        return 0

    lax.fori_loop(0, BLOCKS, mask, 0)
    all_here()
    gather.start_near()

    def pack(r, src):
        for d in range(2):
            for s in range(SLOTS):
                pick = send_ref[0, d, s]
                blk = src[jnp.minimum(pick, BLOCKS - 1)].astype(F32)
                fout[r, d, s] = jnp.where(pick < BLOCKS, blk, 0.0).astype(BF16)
        for c in face_copies(r):
            c.start()

    def face_copies(r):
        return (
            rcopy(fout.at[r, 1], fin.at[r, 0], fsend.at[r, 1], frecv.at[r, 0], above),
            rcopy(fout.at[r, 0], fin.at[r, 1], fsend.at[r, 0], frecv.at[r, 1], below),
        )

    def tile(t):
        rhs = jnp.concatenate([ext[2 * t], ext[2 * t + 1]], axis=1)
        res = jnp.dot(w_ref[...], rhs, preferred_element_type=F32)
        prod[2 * t] = res[:, :BLOCK]
        prod[2 * t + 1] = res[:, BLOCK:]

    def face_rows():
        keep = jnp.where(b > 0, 1.0, 0.0), jnp.where(b < NBOX - 1, 1.0, 0.0)
        for r, (r_abs, _) in enumerate(quarters):
            for c in face_copies(r):
                c.wait_recv()
            rows = rows_of(r_abs)
            for d in range(2):
                for s in range(SLOTS):
                    ext[BLOCKS + d * SLOTS + s, rows, :] = (fin[r, d, s].astype(F32) * keep[d]).astype(BF16)

    def two_tiles(p, _):
        first = jnp.where(p < NCHUNK, 2 * (p // 2) + NCHUNK * lax.rem(p, 2), 2 * p)

        @pl.when((p < NCHUNK) & (lax.rem(p, 2) == 0))
        def _():
            gather.wait_far(p // 2)

        @pl.when(p == NCHUNK - 2)
        def _():
            pack(3, opp)

        @pl.when(p < NCHUNK)
        def _():
            for r_abs, src in quarters:
                rows = rows_of(r_abs)
                for e in range(CHUNK):
                    ext[2 * first + e, rows, :] = src[2 * first + e]

        @pl.when(p == NCHUNK)
        def _():
            face_rows()

        tile(first)
        tile(first + 1)
        return 0

    pack(0, own)
    prod[EXT] = jnp.zeros((OFFSETS * LOC, BLOCK), F32)
    ext[EXT] = jnp.zeros((CH, BLOCK), BF16)
    low = lax.broadcasted_iota(jnp.int32, (LOC, BLOCK), 1) < LOC

    def columns(p, _):
        for h in range(2):
            cols = pl.ds(h * BLOCK, BLOCK)
            first = w_ref[pl.ds(pl.multiple_of(2 * p * LOC, LOC), LOC), cols].astype(F32)
            row = jnp.minimum(2 * p + 1, OFFSETS - 1) * LOC
            second = w_ref[pl.ds(pl.multiple_of(row, LOC), LOC), cols].astype(F32)
            second = jnp.where(2 * p + 1 < OFFSETS, second, 0.0)
            put = pl.ds(pl.multiple_of(p * BLOCK, BLOCK), BLOCK)
            parts_ref[2 * h, :, put] = jnp.where(low, first, pltpu.roll(second, LOC, 1)).astype(BF16)
            parts_ref[2 * h + 1, :, put] = jnp.where(low, pltpu.roll(first, LOC, 1), second).astype(BF16)
        return 0

    lax.fori_loop(0, WPAD // BLOCK, columns, 0)
    gather.advance(0)
    target = pair_targets(map_ref)
    gather.advance(1)
    rank = pair_ranks(map_ref, target)
    gather.advance(2)
    meta_ref[...] = sort_pairs(target, rank)
    gather.advance(3)
    gather.start_far()
    gather.wait_near()
    pack(1, from_dn)
    pack(2, from_up)
    lax.fori_loop(0, EXT // 4, two_tiles, 0)
    leave = pltpu.make_async_copy(ext, ext_to, esem)
    leave.start()

    def out(j, carry):
        a, s = carry
        acc = prod[map_ref[0, 0, j], pl.ds(0, LOC), :]
        for k in range(1, OFFSETS):
            acc = acc + prod[map_ref[k, 0, j], pl.ds(LOC * k, LOC), :]
        conv_ref[j] = acc
        o = occ_of(occ_ref, j) * acc
        return a + o, s + o * acc

    zero = jnp.zeros((LOC, BLOCK), F32)
    a, s = lax.fori_loop(0, BLOCKS, out, (zero, zero), unroll=2)
    sum_ref[0] = a
    sum_ref[1] = s
    leave.wait()
    gather.wait_sends()
    for r in range(4):
        for c in face_copies(r):
            c.wait_send()


def conv_call(send, kmap, features, occ, w):
    quarter = pltpu.VMEM((BLOCKS, LOC, BLOCK), BF16)
    faces = pltpu.VMEM((4, 2, SLOTS, LOC, BLOCK), BF16)
    dma = pltpu.SemaphoreType.DMA
    return pl.pallas_call(
        conv_kernel,
        out_shape=(
            jax.ShapeDtypeStruct((BLOCKS, LOC, BLOCK), F32),
            jax.ShapeDtypeStruct((2, LOC, BLOCK), F32),
            jax.ShapeDtypeStruct((EXT + 1, CH, BLOCK), BF16),
            jax.ShapeDtypeStruct((4, LOC, WPAD), BF16),
            jax.ShapeDtypeStruct((16, BLOCK), jnp.int32),
        ),
        in_specs=[SMEM, SMEM, VMEM, VMEM, VMEM],
        out_specs=(VMEM, VMEM, ANY, VMEM, VMEM),
        scratch_shapes=[
            pltpu.VMEM((EXT + 1, CH, BLOCK), BF16),
            quarter,
            quarter,
            quarter,
            quarter,
            faces,
            faces,
            pltpu.VMEM((EXT + 1, OFFSETS * LOC, BLOCK), F32),
            dma((3 * NCHUNK,)),
            dma((3 * NCHUNK,)),
            dma((4, 2)),
            dma((4, 2)),
            dma,
        ],
        compiler_params=params(1),
        name="conv",
    )(send, kmap, features, occ, w)


def lane_masks():
    ch = lax.broadcasted_iota(jnp.int32, (LOC, BLOCK), 0)
    lane = lax.broadcasted_iota(jnp.int32, (LOC, BLOCK), 1)
    return lane == ch, lane == ch + LOC


def to_row(first, second):
    m0, m1 = lane_masks()
    c0 = jnp.sum(first, axis=1, keepdims=True)
    c1 = jnp.sum(second, axis=1, keepdims=True)
    return jnp.sum(jnp.where(m0, c0, 0.0) + jnp.where(m1, c1, 0.0), axis=0, keepdims=True)


def to_cols(row):
    m0, m1 = lane_masks()
    return (
        jnp.sum(jnp.where(m0, row, 0.0), axis=1, keepdims=True),
        jnp.sum(jnp.where(m1, row, 0.0), axis=1, keepdims=True),
    )


def at_box(x, z, core):
    return {"box": x * 16 + z * 2 + core}


def to_col(row):
    ch = lax.broadcasted_iota(jnp.int32, (LOC, LOC), 0)
    lane = lax.broadcasted_iota(jnp.int32, (LOC, LOC), 1)
    return jnp.sum(jnp.where(ch == lane, row, 0.0), axis=1, keepdims=True)


def box_groups():
    b = lax.axis_index("box")
    x, z, core = b // 16, lax.rem(b // 2, 8), lax.rem(b, 2)
    first = [at_box(lax.rem(x + d // 2, 4), z, lax.rem(core + d % 2, 2)) for d in range(1, 8)]
    second = [at_box(x, lax.rem(z + d, 8), core) for d in range(1, 8)]
    return (x * 2 + core, first), (z, second)


def box_sum(mine, buf, ssem, rsem, idle):
    sent = []
    for step, (me, peers) in enumerate(box_groups()):
        buf[step, me] = mine
        copies = []
        for d, dev in enumerate(peers):
            c = rcopy(buf.at[step, me], buf.at[step, me], ssem.at[step, d], rsem.at[step, d], dev)
            c.start()
            copies.append(c)
        idle(step)
        for c in copies:
            c.wait_recv()
        mine = buf[step, 0]
        for d in range(1, 8):
            mine = mine + buf[step, d]
        sent += copies
    return mine, sent


def norm_kernel(
    send_ref,
    map_ref,
    meta_ref,
    conv_ref,
    sum_ref,
    grad_from,
    occ_ref,
    gain_ref,
    shift_ref,
    ext_from,
    parts_ref,
    out_to,
    eg_to,
    fin,
    res,
    stat_ref,
    out_ref,
    eg,
    grad_ref,
    ext_ref,
    relay,
    extt,
    wg,
    wrecv,
    win,
    prod,
    run,
    own,
    from_dn,
    from_up,
    opp,
    sbuf,
    sbuf2,
    fout,
    give,
    given,
    xbuf,
    xin,
    zbuf,
    zin,
    ysend,
    yrecv,
    ssend,
    srecv,
    wsend,
    wrecvs,
    fsend,
    frecv,
    gsend,
    grecv,
    lsem,
):
    q = lax.axis_index("ch")
    b = lax.axis_index("box")
    x, z, core = b // 16, lax.rem(b // 2, 8), lax.rem(b, 2)
    gather = YGather(own, from_dn, from_up, opp, ysend, yrecv)
    (_, near), (_, far) = box_groups()
    above = {"box": lax.rem(b + 1, NBOX)}
    below = {"box": lax.rem(b + NBOX - 1, NBOX)}
    mate = at_box(x, z, 1 - core)
    xpeers = [at_box(lax.rem(x + d, 4), z, core) for d in range(1, 4)]
    zpeers = far
    sent = []
    loads = [pltpu.make_async_copy(ext_from, ext_ref, lsem.at[0]), pltpu.make_async_copy(grad_from, grad_ref, lsem.at[1])]
    for c in loads:
        c.start()

    all_here = greet([gather.up, gather.dn] + near + far + [above, below])
    count = jnp.sum(occ_ref[...].astype(F32), axis=0)
    count = jnp.broadcast_to(jnp.sum(count, axis=1, keepdims=True), (1, BLOCK))
    row = to_row(sum_ref[0], sum_ref[1])
    sub = lax.broadcasted_iota(jnp.int32, (2, BLOCK), 0)
    pay = jnp.where(sub == 0, row, count)
    all_here()
    wcopies = []

    def wcopy(src, dst, i, dev):
        c = rcopy(src, dst, wsend.at[i], wrecvs.at[i], dev)
        wcopies.append(c)
        return c

    far_part = parts_ref.at[lax.rem(q + 2, 4)]
    near_rows, far_rows = pl.ds(0, LOC // 2), pl.ds(LOC // 2, LOC // 2)
    lead = [
        wcopy(far_part.at[near_rows], relay.at[0], 0, gather.up),
        wcopy(far_part.at[far_rows], relay.at[1], 1, gather.dn),
    ]
    tail = [
        wcopy(parts_ref.at[lax.rem(q + 1, 4)], wrecv.at[pl.ds(LOC, LOC)], 2, gather.up),
        wcopy(parts_ref.at[lax.rem(q + 3, 4)], wrecv.at[pl.ds(2 * LOC, LOC)], 3, gather.dn),
    ]
    tail_far = [
        wcopy(relay.at[0], wrecv.at[pl.ds(3 * LOC, LOC // 2)], 4, gather.up),
        wcopy(relay.at[1], wrecv.at[pl.ds(3 * LOC + LOC // 2, LOC // 2)], 5, gather.dn),
    ]
    for c in lead + tail:
        c.start()
    wrecv[pl.ds(0, LOC), :] = parts_ref[q]
    loads[0].wait()

    def flip(step):
        if step == 1:
            for c, d in zip(lead, tail_far):
                c.wait_recv()
                d.start()

        def one(e, _):
            extt[e] = ext_ref[e].T
            return 0

        lax.fori_loop(*((0, EXT // 2) if step == 0 else (EXT // 2, EXT + 1)), one, 0)

    tot, more = box_sum(pay, sbuf, ssend.at[0], srecv.at[0], flip)
    sent += wcopies + more
    loads[1].wait()
    n_vox = tot[1:2, 0:1]
    s1, s2 = to_cols(tot[0:1, :])
    mean = s1 / n_vox
    var = s2 / n_vox - mean * mean
    inv = 1.0 / jnp.sqrt(var + 1e-05)
    gain, shift = to_col(gain_ref[...]), to_col(shift_ref[...])

    def fwd(j, carry):
        a, s = carry
        cols = pl.ds(pl.multiple_of(j * BLOCK, BLOCK), BLOCK)
        occ = occ_of(occ_ref, j)
        nd = (conv_ref[j] - mean) * inv
        sh = nd * gain + shift
        out_ref[:, cols] = (occ * jnp.maximum(sh, 0.0)).astype(BF16)
        rg = jnp.where(sh > 0.0, occ * grad_ref[:, cols].astype(F32), 0.0)
        run[2 * j] = nd
        run[2 * j + 1] = rg
        return a + rg, s + rg * nd

    zero = jnp.zeros((LOC, BLOCK), F32)
    a, s = lax.fori_loop(0, BLOCKS, fwd, (zero, zero))
    leave = [pltpu.make_async_copy(out_ref, out_to, lsem.at[2]), pltpu.make_async_copy(eg, eg_to, lsem.at[3])]
    leave[0].start()
    row = to_row(a, s)

    def turn(step):
        if step == 0:
            return
        for c in tail + tail_far:
            c.wait_recv()
        for p in range(WPAD // BLOCK):
            win[pl.ds(p * BLOCK, BLOCK), :] = wrecv[:, pl.ds(p * BLOCK, BLOCK)].T

    tot, more = box_sum(row, sbuf2, ssend.at[1], srecv.at[1], turn)
    sent += more
    stat_ref[...] = tot
    sg, gg = to_cols(tot)
    scale = inv * gain
    sgm = sg / n_vox

    def bwd(j, _):
        nd, rg = run[2 * j], run[2 * j + 1]
        own[j] = (occ_of(occ_ref, j) * scale * (rg - sgm - nd * gg / n_vox)).astype(BF16)
        return 0

    lax.fori_loop(0, BLOCKS, bwd, 0)
    gather.start()

    def kterm(k, _):
        lhs = jnp.concatenate([own[j] for j in range(BLOCKS)], axis=1)
        rhs = jnp.concatenate([extt[map_ref[k, 0, j]] for j in range(BLOCKS)], axis=0)
        wg[k] = jnp.dot(lhs, rhs, preferred_element_type=F32)
        return 0

    def send(src, dst, h, i, dev):
        c = rcopy(src, dst, gsend.at[h, i], grecv.at[h, i], dev)
        c.start()
        sent.append(c)
        return c

    flight = [None] * PARTS
    xpart = lambda i: pl.ds(pl.multiple_of(i * XROWS, XROWS), XROWS)
    zpart = lambda i: pl.ds(pl.multiple_of(i * ZROWS, ZROWS), ZROWS)
    mine = pl.ds(pl.multiple_of(x * XROWS + z * ZROWS, ZROWS), ZROWS)

    def arrive(h):
        for c in flight[h]:
            c.wait_recv()

    def each_k(h, body):
        def one(k, _):
            body(k + KFIRST[h], pl.ds(pl.multiple_of(k * LOC, LOC), LOC))
            return 0

        lax.fori_loop(0, KCOUNT[h], one, 0)

    def step0(h):
        def cut(k, rows):
            give[h, rows, :] = jnp.where(core == 0, wg[k, :, BLOCK:], wg[k, :, :BLOCK]).astype(BF16)

        each_k(h, cut)
        rows = pl.ds(0, KCOUNT[h] * LOC)
        flight[h] = [send(give.at[h, rows], given.at[h, rows], h, 0, mate)]

    def step1(h):
        arrive(h)

        def add(k, rows):
            keep = jnp.where(core == 0, wg[k, :, :BLOCK], wg[k, :, BLOCK:])
            xbuf[h, rows, :] = (keep + given[h, rows, :].astype(F32)).astype(BF16)

        each_k(h, add)
        rest = WROWS - KCOUNT[h] * LOC
        if rest:
            xbuf[h, pl.ds(KCOUNT[h] * LOC, rest), :] = jnp.zeros((rest, BLOCK), BF16)
        flight[h] = [
            send(xbuf.at[h, xpart(lax.rem(x + d, 4))], xin.at[h, d - 1], h, d, xpeers[d - 1]) for d in range(1, 4)
        ]

    def step2(h):
        arrive(h)
        t = xbuf[h, xpart(x), :].astype(F32)
        for d in range(3):
            t = t + xin[h, d].astype(F32)
        zbuf[h] = t.astype(BF16)
        flight[h] = [
            send(zbuf.at[h, zpart(lax.rem(z + d, 8))], zin.at[h, d - 1], h, 3 + d, zpeers[d - 1]) for d in range(1, 8)
        ]

    def step3(h):
        arrive(h)
        t = zbuf[h, zpart(z), :].astype(F32)
        for d in range(7):
            t = t + zin[h, d].astype(F32)
        res[h, 0, mine, :] = t.astype(BF16)
        flight[h] = [
            send(res.at[h, 0, mine], res.at[h, 0, mine], h, 10 + d, zpeers[d - 1]) for d in range(1, 8)
        ]

    def step4(h):
        arrive(h)
        part = xpart(x)
        flight[h] = [
            send(res.at[h, 0, part], res.at[h, 0, part], h, 17 + d, xpeers[d - 1]) for d in range(1, 4)
        ]

    def step5(h):
        arrive(h)
        rows = pl.ds(0, KCOUNT[h] * LOC)
        flight[h] = [send(res.at[h, 0, rows], res.at[h, 1, rows], h, 21, mate)]

    def kterms(first, last):
        lax.fori_loop(first, last, kterm, 0)

    kterms(0, 8)
    step0(0)
    gather.forward(0)
    kterms(8, 12)
    step1(0)
    kterms(12, 14)
    gather.forward(1)
    kterms(14, 16)
    step0(1)
    kterms(16, 20)
    gather.forward(2)
    step2(0)
    step1(1)
    kterms(20, 24)
    step0(2)
    kterms(24, 25)
    gather.forward(3)
    kterms(25, 27)
    step0(3)
    step2(1)
    step1(2)

    def tile(t, _):
        halves = []
        for e in (2 * t, 2 * t + 1):
            halves.append(jnp.concatenate([own[e], from_dn[e], from_up[e], opp[e]], axis=0))
        rhs = jnp.concatenate(halves, axis=1)
        r = jnp.dot(win[pl.ds(0, OFFSETS * LOC), :], rhs, preferred_element_type=F32)
        r = r.astype(BF16)
        place = 2 * OFFSETS * t
        prod[pl.ds(place, OFFSETS)] = r[:, :BLOCK].reshape(OFFSETS, LOC, BLOCK)
        prod[pl.ds(place + OFFSETS, OFFSETS)] = r[:, BLOCK:].reshape(OFFSETS, LOC, BLOCK)
        return 0

    def tiles(i):
        gather.wait_part(i)
        lax.fori_loop(2 * i, 2 * i + 2, tile, 0)
        lax.fori_loop(2 * i + 8, 2 * i + 10, tile, 0)

    tiles(0)
    step1(3)
    step3(0)
    tiles(1)
    step2(2)
    tiles(2)
    step2(3)
    step3(1)
    tiles(3)
    step4(0)

    def walk(g, acc):
        for u in range(WALK):
            row, col = g // (BLOCK // WALK), lax.rem(g, BLOCK // WALK) * WALK + u
            term = prod[meta_ref[row, col]].astype(F32)
            acc = jnp.where(meta_ref[8 + row, col] > 0, 0.0, acc) + term
            run[g * WALK + u] = acc
        return acc

    third = OFFSETS * BLOCKS // WALK // 3
    acc = lax.fori_loop(0, third, walk, jnp.zeros((LOC, BLOCK), F32))
    step3(2)
    acc = lax.fori_loop(third, 2 * third, walk, acc)
    step3(3)
    step4(1)
    lax.fori_loop(2 * third, 3 * third, walk, acc)
    step5(0)

    def total(d):
        return jnp.where(meta_ref[15, d] > 0, run[meta_ref[7, d]], 0.0)

    for s in range(2 * SLOTS):
        fout[s // SLOTS, s % SLOTS] = total(BLOCKS + s).astype(BF16)
    fcopies = []
    for d, dev in enumerate((below, above)):
        c = rcopy(fout.at[d], fin.at[d], fsend.at[d], frecv.at[d], dev)
        c.start()
        fcopies.append(c)
    sent += fcopies

    def keep(d, _):
        eg[d] = total(d)
        return 0

    lax.fori_loop(0, BLOCKS, keep, 0)
    leave[1].start()
    step4(2)
    step4(3)
    step5(1)
    for c in fcopies:
        c.wait_recv()
    step5(2)
    step5(3)
    for h in range(PARTS):
        arrive(h)
    for c in leave:
        c.wait()
    gather.wait_sends()
    for c in sent:
        c.wait_send()


def norm_call(send, kmap, meta, conv, sums, out_grad, occ, gain, shift, ext, parts):
    quarter = pltpu.VMEM((BLOCKS, LOC, BLOCK), BF16)
    dma = pltpu.SemaphoreType.DMA
    return pl.pallas_call(
        norm_kernel,
        out_shape=(
            jax.ShapeDtypeStruct((LOC, BLOCKS * BLOCK), BF16),
            jax.ShapeDtypeStruct((BLOCKS, LOC, BLOCK), F32),
            jax.ShapeDtypeStruct((2, SLOTS, LOC, BLOCK), BF16),
            jax.ShapeDtypeStruct((PARTS, 2, WROWS, BLOCK), BF16),
            jax.ShapeDtypeStruct((1, BLOCK), F32),
        ),
        in_specs=[SMEM] * 3 + [VMEM, VMEM, ANY, VMEM, VMEM, VMEM, ANY, VMEM],
        out_specs=(ANY, ANY, VMEM, VMEM, VMEM),
        scratch_shapes=[
            pltpu.VMEM((LOC, BLOCKS * BLOCK), BF16),
            pltpu.VMEM((BLOCKS, LOC, BLOCK), F32),
            pltpu.VMEM((LOC, BLOCKS * BLOCK), BF16),
            pltpu.VMEM((EXT + 1, CH, BLOCK), BF16),
            pltpu.VMEM((2, LOC // 2, WPAD), BF16),
            pltpu.VMEM((EXT + 1, BLOCK, CH), BF16),
            pltpu.VMEM((OFFSETS, LOC, CH), F32),
            pltpu.VMEM((CH, WPAD), BF16),
            pltpu.VMEM((WPAD, CH), BF16),
            pltpu.VMEM((OFFSETS * BLOCKS, LOC, BLOCK), BF16),
            pltpu.VMEM((OFFSETS * BLOCKS, LOC, BLOCK), F32),
            quarter,
            quarter,
            quarter,
            quarter,
            pltpu.VMEM((2, 8, 2, BLOCK), F32),
            pltpu.VMEM((2, 8, 1, BLOCK), F32),
            pltpu.VMEM((2, SLOTS, LOC, BLOCK), BF16),
            pltpu.VMEM((PARTS, WROWS, BLOCK), BF16),
            pltpu.VMEM((PARTS, WROWS, BLOCK), BF16),
            pltpu.VMEM((PARTS, WROWS, BLOCK), BF16),
            pltpu.VMEM((PARTS, 3, XROWS, BLOCK), BF16),
            pltpu.VMEM((PARTS, XROWS, BLOCK), BF16),
            pltpu.VMEM((PARTS, 7, ZROWS, BLOCK), BF16),
            dma((3 * NCHUNK,)),
            dma((3 * NCHUNK,)),
            dma((2, 2, 7)),
            dma((2, 2, 7)),
            dma((6,)),
            dma((6,)),
            dma((2,)),
            dma((2,)),
            dma((PARTS, 22)),
            dma((PARTS, 22)),
            dma((4,)),
        ],
        compiler_params=params(2),
        name="norm",
    )(send, kmap, meta, conv, sums, out_grad, occ, gain, shift, ext, parts)


def emit_kernel(
    send_ref, out_ref, eg_ref, fin_ref, res_ref, stat_ref, occ_ref, out_to, in_to, wg_to, gain_to, shift_to, acc
):
    out_to[...] = out_ref[...]
    b = lax.axis_index("box")
    core = lax.rem(b, 2)
    for h in range(PARTS):

        def put(k, _):
            rows = pl.ds(pl.multiple_of(k * LOC, LOC), LOC)
            m, o = res_ref[h, 0, rows, :].astype(F32), res_ref[h, 1, rows, :].astype(F32)
            wg_to[k + KFIRST[h], :, :BLOCK] = jnp.where(core == 0, m, o)
            wg_to[k + KFIRST[h], :, BLOCK:] = jnp.where(core == 0, o, m)
            return 0

        lax.fori_loop(0, KCOUNT[h], put, 0)
    shift_to[...] = stat_ref[:, :LOC]
    gain_to[...] = stat_ref[:, LOC:]
    acc[pl.ds(0, BLOCKS)] = eg_ref[...]
    acc[BLOCKS] = jnp.zeros((LOC, BLOCK), F32)
    for d, ok in ((0, b < NBOX - 1), (1, b > 0)):
        for s in range(SLOTS):
            at = send_ref[0, 1 - d, s]
            acc[at] = acc[at] + jnp.where(ok, fin_ref[d, s].astype(F32), 0.0)

    def settle(d, _):
        in_to[:, pl.ds(pl.multiple_of(d * BLOCK, BLOCK), BLOCK)] = (occ_of(occ_ref, d) * acc[d]).astype(BF16)
        return 0

    lax.fori_loop(0, BLOCKS, settle, 0)


def emit_call(send, occ, out_features, eg, fin, res, stat):
    whole = jax.ShapeDtypeStruct((LOC, BLOCKS * BLOCK), BF16)
    line = jax.ShapeDtypeStruct((1, LOC), F32)
    return pl.pallas_call(
        emit_kernel,
        out_shape=(whole, whole, jax.ShapeDtypeStruct((OFFSETS, LOC, CH), F32), line, line),
        in_specs=[SMEM] + [VMEM] * 6,
        out_specs=(VMEM,) * 5,
        scratch_shapes=[pltpu.VMEM((BLOCKS + 1, LOC, BLOCK), F32)],
        compiler_params=params(),
        name="emit",
    )(send, out_features, eg, fin, res, stat, occ)


def per_device(
    features, occupied, send_lists, kernel_map, weights, norm_gain, norm_shift, out_grad
):
    occ = occupied.reshape(BLOCKS, 1, BLOCK)
    w = weights.reshape(OFFSETS * LOC, CH)
    kernel_map = kernel_map.transpose(1, 0, 2)
    gain, shift = norm_gain.reshape(1, LOC), norm_shift.reshape(1, LOC)
    conv, sums, ext, parts, meta = conv_call(send_lists, kernel_map, features, occ, w)
    results = norm_call(send_lists, kernel_map, meta, conv, sums, out_grad, occ, gain, shift, ext, parts)
    out_features, in_grad, weight_grad, gain_grad, shift_grad = emit_call(send_lists, occ, *results)
    return (out_features, in_grad, weight_grad, gain_grad.reshape(LOC), shift_grad.reshape(LOC))


def solution(mesh):
    in_specs = (
        P("ch", "box"),
        P("box"),
        P("box", None, None),
        P("box", None, None),
        P(None, "ch", None),
        P("ch"),
        P("ch"),
        P("ch", "box"),
    )
    out_specs = (P("ch", "box"), P("ch", "box"), P(None, "ch", None), P("ch"), P("ch"))
    return jax.shard_map(
        per_device, mesh=mesh, in_specs=in_specs, out_specs=out_specs, check_vma=False
    )
```

```python
import functools

import jax
import jax.numpy as jnp
from jax import lax
from jax.experimental import pallas as pl
from jax.experimental.pallas import tpu as pltpu
from jax.sharding import PartitionSpec as P

F32 = jnp.float32
BF16 = jnp.bfloat16
MESH = pl.DeviceIdType.MESH
VMEM = pl.BlockSpec(memory_space=pltpu.VMEM)
SMEM = pl.BlockSpec(memory_space=pltpu.SMEM)
ANY = pl.BlockSpec(memory_space=pl.ANY)
VMEM_LIMIT = 62 * 2**20

BLOCK = 128
BLOCKS = 32
CHUNK = 4
NCHUNK = 8
NFWD = 4
SLOTS = 8
EXT = BLOCKS + 2 * SLOTS
OFFSETS = 27
CH = 256
LOC = 64
WPAD = 1792
PARTS = 4
KFIRST = (0, 8, 16, 24)
KCOUNT = (8, 8, 8, 3)
WROWS = 512
XROWS = WROWS // 4
ZROWS = XROWS // 8
NBOX = 64
WALK = 16


def params(cid=None):
    if cid is None:
        return pltpu.CompilerParams(vmem_limit_bytes=VMEM_LIMIT)
    return pltpu.CompilerParams(
        vmem_limit_bytes=VMEM_LIMIT, collective_id=cid, has_side_effects=True
    )


def rcopy(src, dst, ssem, rsem, dev):
    return pltpu.make_async_remote_copy(
        src_ref=src, dst_ref=dst, send_sem=ssem, recv_sem=rsem, device_id=dev, device_id_type=MESH
    )


def greet(devs):
    barrier = pltpu.get_barrier_semaphore()
    for dev in devs:
        pl.semaphore_signal(barrier, inc=1, device_id=dev, device_id_type=MESH)
    return lambda: pl.semaphore_wait(barrier, len(devs))


def occ_of(occ_ref, j):
    return occ_ref[j].astype(F32)


def rows_of(q):
    return pl.ds(pl.multiple_of(q * LOC, LOC), LOC)


class YGather:
    def __init__(self, own, from_dn, from_up, opp, ssem, rsem):
        q = lax.axis_index("ch")
        self.up = {"ch": lax.rem(q + 1, 4)}
        self.dn = {"ch": lax.rem(q + 3, 4)}
        self.refs = own, from_dn, from_up, opp
        self.sems = ssem, rsem

    def copy(self, src, dst, chunk, i, dev):
        part = pl.ds(chunk * CHUNK, CHUNK)
        return rcopy(src.at[part], dst.at[part], self.sems[0].at[i], self.sems[1].at[i], dev)

    def own_up(self, c):
        return self.copy(self.refs[0], self.refs[1], c, c, self.up)

    def own_dn(self, c):
        return self.copy(self.refs[0], self.refs[2], c, NCHUNK + c, self.dn)

    def far_up(self, c):
        return self.copy(self.refs[1], self.refs[3], c, 2 * NCHUNK + c, self.up)

    def far_dn(self, c):
        return self.copy(self.refs[2], self.refs[3], c, 2 * NCHUNK + c, self.dn)

    def start(self):
        for c in range(2):
            self.own_up(c).start()
            self.own_dn(NFWD + c).start()

    def start_near(self):
        for c in range(NFWD):
            self.own_up(c).start()
            self.own_dn(NFWD + c).start()

    def advance(self, i):
        self.own_up(i).wait_recv()
        self.own_up(NFWD + i).start()
        self.own_dn(NFWD + i).wait_recv()
        self.own_dn(i).start()

    def start_far(self):
        for c in range(NFWD):
            self.far_up(c).start()
            self.far_dn(NFWD + c).start()

    def wait_near(self):
        for c in range(NFWD):
            self.own_up(NFWD + c).wait_recv()
            self.own_dn(c).wait_recv()

    def wait_far(self, i):
        self.far_up(i).wait_recv()
        self.far_dn(NFWD + i).wait_recv()

    def forward(self, i):
        self.own_up(i).wait_recv()
        self.far_up(i).start()
        self.own_up(NFWD + i).start()
        self.own_dn(NFWD + i).wait_recv()
        self.far_dn(NFWD + i).start()
        self.own_dn(i).start()
        if i + 2 < NFWD:
            self.own_up(i + 2).start()
            self.own_dn(NFWD + i + 2).start()

    def wait_part(self, i):
        self.own_up(NFWD + i).wait_recv()
        self.own_dn(i).wait_recv()
        self.far_up(i).wait_recv()
        self.far_dn(NFWD + i).wait_recv()

    def wait_sends(self):
        for c in range(NCHUNK):
            self.own_up(c).wait_send()
            self.own_dn(c).wait_send()
        for c in range(NFWD):
            self.far_up(c).wait_send()
            self.far_dn(NFWD + c).wait_send()


def pair_places():
    return lax.broadcasted_iota(jnp.int32, (8, BLOCK), 0) * BLOCK + lax.broadcasted_iota(jnp.int32, (8, BLOCK), 1)


def pair_targets(map_ref):
    at = pair_places()

    def fill(k, target):
        for j in range(BLOCKS):
            target = jnp.where(at == k * BLOCKS + j, map_ref[k, 0, j], target)
        return target

    return lax.fori_loop(0, OFFSETS, fill, jnp.full((8, BLOCK), 63, jnp.int32))


def pair_ranks(map_ref, target):
    keys = target * 1024 + pair_places()

    def count(k, rank):
        for j in range(BLOCKS):
            rank = rank + (keys > map_ref[k, 0, j] * 1024 + (k * BLOCKS + j)).astype(jnp.int32)
        return rank

    return lax.fori_loop(0, OFFSETS, count, jnp.zeros((8, BLOCK), jnp.int32))


def sort_pairs(target, rank):
    lane = lax.broadcasted_iota(jnp.int32, (BLOCK, BLOCK), 1)
    sub = lax.broadcasted_iota(jnp.int32, (BLOCK, BLOCK), 0)
    pair = [jnp.zeros((1, BLOCK), F32) for _ in range(7)]
    goal = [jnp.zeros((1, BLOCK), F32) for _ in range(7)]
    last = jnp.full((1, BLOCK), -1.0, F32)
    for s in range(7):
        rcol = jnp.broadcast_to(rank[s : s + 1, :].astype(F32), (BLOCK, BLOCK)).T
        tcol = jnp.broadcast_to(target[s : s + 1, :].astype(F32), (BLOCK, BLOCK)).T
        i = sub + s * BLOCK
        number = (lax.rem(i, BLOCKS) * OFFSETS + i // BLOCKS).astype(F32)
        for r in range(7):
            hit = rcol == (lane + r * BLOCK).astype(F32)
            pair[r] = pair[r] + jnp.sum(jnp.where(hit, number, 0.0), axis=0, keepdims=True)
            goal[r] = goal[r] + jnp.sum(jnp.where(hit, tcol, 0.0), axis=0, keepdims=True)
        mine = tcol == lane.astype(F32)
        last = jnp.maximum(last, jnp.max(jnp.where(mine, rcol, -1.0), axis=0, keepdims=True))
    fresh = []
    first = lax.broadcasted_iota(jnp.int32, (1, BLOCK), 1) == 0
    for r in range(7):
        before = pltpu.roll(goal[r], 1, 1)
        carry = pltpu.roll(goal[r - 1], 1, 1) if r else jnp.full((1, BLOCK), -1.0, F32)
        before = jnp.where(first, carry, before)
        fresh.append(jnp.where(goal[r] == before, 0.0, 1.0))
    some = [jnp.where(last >= 0.0, 1.0, 0.0)]
    return jnp.concatenate(pair + [jnp.maximum(last, 0.0)] + fresh + some, axis=0).astype(jnp.int32)


def conv_kernel(
    send_ref,
    map_ref,
    feat_ref,
    occ_ref,
    w_ref,
    conv_ref,
    sum_ref,
    ext_to,
    parts_ref,
    meta_ref,
    ext,
    own,
    from_dn,
    from_up,
    opp,
    fout,
    fin,
    prod,
    ysend,
    yrecv,
    fsend,
    frecv,
    esem,
):
    q = lax.axis_index("ch")
    b = lax.axis_index("box")
    above = {"box": lax.rem(b + 1, NBOX)}
    below = {"box": lax.rem(b + NBOX - 1, NBOX)}
    gather = YGather(own, from_dn, from_up, opp, ysend, yrecv)
    quarters = ((q, own), (lax.rem(q + 3, 4), from_dn), (lax.rem(q + 1, 4), from_up), (lax.rem(q + 2, 4), opp))

    all_here = greet([gather.up, gather.dn, above, below])

    def mask(e, _):
        x = feat_ref[:, pl.ds(pl.multiple_of(e * BLOCK, BLOCK), BLOCK)].astype(F32)
        own[e] = (x * occ_of(occ_ref, e)).astype(BF16)
        return 0

    lax.fori_loop(0, BLOCKS, mask, 0)
    all_here()
    gather.start_near()

    def pack(r, src):
        for d in range(2):
            for s in range(SLOTS):
                pick = send_ref[0, d, s]
                blk = src[jnp.minimum(pick, BLOCKS - 1)].astype(F32)
                fout[r, d, s] = jnp.where(pick < BLOCKS, blk, 0.0).astype(BF16)
        for c in face_copies(r):
            c.start()

    def face_copies(r):
        return (
            rcopy(fout.at[r, 1], fin.at[r, 0], fsend.at[r, 1], frecv.at[r, 0], above),
            rcopy(fout.at[r, 0], fin.at[r, 1], fsend.at[r, 0], frecv.at[r, 1], below),
        )

    def tile(t):
        rhs = jnp.concatenate([ext[2 * t], ext[2 * t + 1]], axis=1)
        res = jnp.dot(w_ref[...], rhs, preferred_element_type=F32)
        prod[2 * t] = res[:, :BLOCK]
        prod[2 * t + 1] = res[:, BLOCK:]

    def face_rows():
        keep = jnp.where(b > 0, 1.0, 0.0), jnp.where(b < NBOX - 1, 1.0, 0.0)
        for r, (r_abs, _) in enumerate(quarters):
            for c in face_copies(r):
                c.wait_recv()
            rows = rows_of(r_abs)
            for d in range(2):
                for s in range(SLOTS):
                    ext[BLOCKS + d * SLOTS + s, rows, :] = (fin[r, d, s].astype(F32) * keep[d]).astype(BF16)

    def two_tiles(p, _):
        first = jnp.where(p < NCHUNK, 2 * (p // 2) + NCHUNK * lax.rem(p, 2), 2 * p)

        @pl.when((p < NCHUNK) & (lax.rem(p, 2) == 0))
        def _():
            gather.wait_far(p // 2)

        @pl.when(p == NCHUNK - 2)
        def _():
            pack(3, opp)

        @pl.when(p < NCHUNK)
        def _():
            for r_abs, src in quarters:
                rows = rows_of(r_abs)
                for e in range(CHUNK):
                    ext[2 * first + e, rows, :] = src[2 * first + e]

        @pl.when(p == NCHUNK)
        def _():
            face_rows()

        tile(first)
        tile(first + 1)
        return 0

    pack(0, own)
    prod[EXT] = jnp.zeros((OFFSETS * LOC, BLOCK), F32)
    ext[EXT] = jnp.zeros((CH, BLOCK), BF16)
    low = lax.broadcasted_iota(jnp.int32, (LOC, BLOCK), 1) < LOC

    def columns(p, _):
        for h in range(2):
            cols = pl.ds(h * BLOCK, BLOCK)
            first = w_ref[pl.ds(pl.multiple_of(2 * p * LOC, LOC), LOC), cols].astype(F32)
            row = jnp.minimum(2 * p + 1, OFFSETS - 1) * LOC
            second = w_ref[pl.ds(pl.multiple_of(row, LOC), LOC), cols].astype(F32)
            second = jnp.where(2 * p + 1 < OFFSETS, second, 0.0)
            put = pl.ds(pl.multiple_of(p * BLOCK, BLOCK), BLOCK)
            parts_ref[2 * h, :, put] = jnp.where(low, first, pltpu.roll(second, LOC, 1)).astype(BF16)
            parts_ref[2 * h + 1, :, put] = jnp.where(low, pltpu.roll(first, LOC, 1), second).astype(BF16)
        return 0

    lax.fori_loop(0, WPAD // BLOCK, columns, 0)
    gather.advance(0)
    target = pair_targets(map_ref)
    gather.advance(1)
    rank = pair_ranks(map_ref, target)
    gather.advance(2)
    meta_ref[...] = sort_pairs(target, rank)
    gather.advance(3)
    gather.start_far()
    gather.wait_near()
    pack(1, from_dn)
    pack(2, from_up)
    lax.fori_loop(0, EXT // 4, two_tiles, 0)
    leave = pltpu.make_async_copy(ext, ext_to, esem)
    leave.start()

    def out(j, carry):
        a, s = carry
        acc = prod[map_ref[0, 0, j], pl.ds(0, LOC), :]
        for k in range(1, OFFSETS):
            acc = acc + prod[map_ref[k, 0, j], pl.ds(LOC * k, LOC), :]
        conv_ref[j] = acc
        o = occ_of(occ_ref, j) * acc
        return a + o, s + o * acc

    zero = jnp.zeros((LOC, BLOCK), F32)
    a, s = lax.fori_loop(0, BLOCKS, out, (zero, zero), unroll=4)
    sum_ref[0] = a
    sum_ref[1] = s
    leave.wait()
    gather.wait_sends()
    for r in range(4):
        for c in face_copies(r):
            c.wait_send()


def conv_call(send, kmap, features, occ, w):
    quarter = pltpu.VMEM((BLOCKS, LOC, BLOCK), BF16)
    faces = pltpu.VMEM((4, 2, SLOTS, LOC, BLOCK), BF16)
    dma = pltpu.SemaphoreType.DMA
    return pl.pallas_call(
        conv_kernel,
        out_shape=(
            jax.ShapeDtypeStruct((BLOCKS, LOC, BLOCK), F32),
            jax.ShapeDtypeStruct((2, LOC, BLOCK), F32),
            jax.ShapeDtypeStruct((EXT + 1, CH, BLOCK), BF16),
            jax.ShapeDtypeStruct((4, LOC, WPAD), BF16),
            jax.ShapeDtypeStruct((16, BLOCK), jnp.int32),
        ),
        in_specs=[SMEM, SMEM, VMEM, VMEM, VMEM],
        out_specs=(VMEM, VMEM, ANY, VMEM, VMEM),
        scratch_shapes=[
            pltpu.VMEM((EXT + 1, CH, BLOCK), BF16),
            quarter,
            quarter,
            quarter,
            quarter,
            faces,
            faces,
            pltpu.VMEM((EXT + 1, OFFSETS * LOC, BLOCK), F32),
            dma((3 * NCHUNK,)),
            dma((3 * NCHUNK,)),
            dma((4, 2)),
            dma((4, 2)),
            dma,
        ],
        compiler_params=params(1),
        name="conv",
    )(send, kmap, features, occ, w)


def lane_masks():
    ch = lax.broadcasted_iota(jnp.int32, (LOC, BLOCK), 0)
    lane = lax.broadcasted_iota(jnp.int32, (LOC, BLOCK), 1)
    return lane == ch, lane == ch + LOC


def to_row(first, second):
    m0, m1 = lane_masks()
    c0 = jnp.sum(first, axis=1, keepdims=True)
    c1 = jnp.sum(second, axis=1, keepdims=True)
    return jnp.sum(jnp.where(m0, c0, 0.0) + jnp.where(m1, c1, 0.0), axis=0, keepdims=True)


def to_cols(row):
    m0, m1 = lane_masks()
    return (
        jnp.sum(jnp.where(m0, row, 0.0), axis=1, keepdims=True),
        jnp.sum(jnp.where(m1, row, 0.0), axis=1, keepdims=True),
    )


def at_box(x, z, core):
    return {"box": x * 16 + z * 2 + core}


def to_col(row):
    ch = lax.broadcasted_iota(jnp.int32, (LOC, LOC), 0)
    lane = lax.broadcasted_iota(jnp.int32, (LOC, LOC), 1)
    return jnp.sum(jnp.where(ch == lane, row, 0.0), axis=1, keepdims=True)


def box_groups():
    b = lax.axis_index("box")
    x, z, core = b // 16, lax.rem(b // 2, 8), lax.rem(b, 2)
    first = [at_box(lax.rem(x + d // 2, 4), z, lax.rem(core + d % 2, 2)) for d in range(1, 8)]
    second = [at_box(x, lax.rem(z + d, 8), core) for d in range(1, 8)]
    return (x * 2 + core, first), (z, second)


def box_sum(mine, buf, ssem, rsem, idle):
    sent = []
    for step, (me, peers) in enumerate(box_groups()):
        buf[step, me] = mine
        copies = []
        for d, dev in enumerate(peers):
            c = rcopy(buf.at[step, me], buf.at[step, me], ssem.at[step, d], rsem.at[step, d], dev)
            c.start()
            copies.append(c)
        idle(step)
        for c in copies:
            c.wait_recv()
        mine = buf[step, 0]
        for d in range(1, 8):
            mine = mine + buf[step, d]
        sent += copies
    return mine, sent


def norm_kernel(
    send_ref,
    map_ref,
    meta_ref,
    conv_ref,
    sum_ref,
    grad_from,
    occ_ref,
    gain_ref,
    shift_ref,
    ext_from,
    parts_ref,
    out_to,
    eg_to,
    fin,
    res,
    stat_ref,
    out_ref,
    eg,
    grad_ref,
    ext_ref,
    relay,
    extt,
    wg,
    wrecv,
    win,
    prod,
    run,
    own,
    from_dn,
    from_up,
    opp,
    sbuf,
    sbuf2,
    fout,
    give,
    given,
    xbuf,
    xin,
    zbuf,
    zin,
    ysend,
    yrecv,
    ssend,
    srecv,
    wsend,
    wrecvs,
    fsend,
    frecv,
    gsend,
    grecv,
    lsem,
):
    q = lax.axis_index("ch")
    b = lax.axis_index("box")
    x, z, core = b // 16, lax.rem(b // 2, 8), lax.rem(b, 2)
    gather = YGather(own, from_dn, from_up, opp, ysend, yrecv)
    (_, near), (_, far) = box_groups()
    above = {"box": lax.rem(b + 1, NBOX)}
    below = {"box": lax.rem(b + NBOX - 1, NBOX)}
    mate = at_box(x, z, 1 - core)
    xpeers = [at_box(lax.rem(x + d, 4), z, core) for d in range(1, 4)]
    zpeers = far
    sent = []
    loads = [pltpu.make_async_copy(ext_from, ext_ref, lsem.at[0]), pltpu.make_async_copy(grad_from, grad_ref, lsem.at[1])]
    for c in loads:
        c.start()

    all_here = greet([gather.up, gather.dn] + near + far + [above, below])
    count = jnp.sum(occ_ref[...].astype(F32), axis=0)
    count = jnp.broadcast_to(jnp.sum(count, axis=1, keepdims=True), (1, BLOCK))
    row = to_row(sum_ref[0], sum_ref[1])
    sub = lax.broadcasted_iota(jnp.int32, (2, BLOCK), 0)
    pay = jnp.where(sub == 0, row, count)
    all_here()
    wcopies = []

    def wcopy(src, dst, i, dev):
        c = rcopy(src, dst, wsend.at[i], wrecvs.at[i], dev)
        wcopies.append(c)
        return c

    far_part = parts_ref.at[lax.rem(q + 2, 4)]
    near_rows, far_rows = pl.ds(0, LOC // 2), pl.ds(LOC // 2, LOC // 2)
    lead = [
        wcopy(far_part.at[near_rows], relay.at[0], 0, gather.up),
        wcopy(far_part.at[far_rows], relay.at[1], 1, gather.dn),
    ]
    tail = [
        wcopy(parts_ref.at[lax.rem(q + 1, 4)], wrecv.at[pl.ds(LOC, LOC)], 2, gather.up),
        wcopy(parts_ref.at[lax.rem(q + 3, 4)], wrecv.at[pl.ds(2 * LOC, LOC)], 3, gather.dn),
    ]
    tail_far = [
        wcopy(relay.at[0], wrecv.at[pl.ds(3 * LOC, LOC // 2)], 4, gather.up),
        wcopy(relay.at[1], wrecv.at[pl.ds(3 * LOC + LOC // 2, LOC // 2)], 5, gather.dn),
    ]
    for c in lead + tail:
        c.start()
    wrecv[pl.ds(0, LOC), :] = parts_ref[q]
    loads[0].wait()

    def flip(step):
        if step == 1:
            for c, d in zip(lead, tail_far):
                c.wait_recv()
                d.start()

        def one(e, _):
            extt[e] = ext_ref[e].T
            return 0

        lax.fori_loop(*((0, EXT // 2) if step == 0 else (EXT // 2, EXT + 1)), one, 0)

    tot, more = box_sum(pay, sbuf, ssend.at[0], srecv.at[0], flip)
    sent += wcopies + more
    loads[1].wait()
    n_vox = tot[1:2, 0:1]
    s1, s2 = to_cols(tot[0:1, :])
    mean = s1 / n_vox
    var = s2 / n_vox - mean * mean
    inv = 1.0 / jnp.sqrt(var + 1e-05)
    gain, shift = to_col(gain_ref[...]), to_col(shift_ref[...])

    def fwd(j, carry):
        a, s = carry
        cols = pl.ds(pl.multiple_of(j * BLOCK, BLOCK), BLOCK)
        occ = occ_of(occ_ref, j)
        nd = (conv_ref[j] - mean) * inv
        sh = nd * gain + shift
        out_ref[:, cols] = (occ * jnp.maximum(sh, 0.0)).astype(BF16)
        rg = jnp.where(sh > 0.0, occ * grad_ref[:, cols].astype(F32), 0.0)
        run[2 * j] = nd
        run[2 * j + 1] = rg
        return a + rg, s + rg * nd

    zero = jnp.zeros((LOC, BLOCK), F32)
    a, s = lax.fori_loop(0, BLOCKS, fwd, (zero, zero), unroll=2)
    leave = [pltpu.make_async_copy(out_ref, out_to, lsem.at[2]), pltpu.make_async_copy(eg, eg_to, lsem.at[3])]
    leave[0].start()
    row = to_row(a, s)

    def turn(step):
        if step == 0:
            return
        for c in tail + tail_far:
            c.wait_recv()
        for p in range(WPAD // BLOCK):
            win[pl.ds(p * BLOCK, BLOCK), :] = wrecv[:, pl.ds(p * BLOCK, BLOCK)].T

    tot, more = box_sum(row, sbuf2, ssend.at[1], srecv.at[1], turn)
    sent += more
    stat_ref[...] = tot
    sg, gg = to_cols(tot)
    scale = inv * gain
    sgm, ggm = sg / n_vox, gg / n_vox

    def bwd(j, _):
        nd, rg = run[2 * j], run[2 * j + 1]
        own[j] = (occ_of(occ_ref, j) * scale * (rg - sgm - nd * ggm)).astype(BF16)
        return 0

    lax.fori_loop(0, BLOCKS, bwd, 0, unroll=2)
    gather.start()

    def kterm(k, _):
        lhs = jnp.concatenate([own[j] for j in range(BLOCKS)], axis=1)
        rhs = jnp.concatenate([extt[map_ref[k, 0, j]] for j in range(BLOCKS)], axis=0)
        wg[k] = jnp.dot(lhs, rhs, preferred_element_type=F32)
        return 0

    def send(src, dst, h, i, dev):
        c = rcopy(src, dst, gsend.at[h, i], grecv.at[h, i], dev)
        c.start()
        sent.append(c)
        return c

    flight = [None] * PARTS
    xpart = lambda i: pl.ds(pl.multiple_of(i * XROWS, XROWS), XROWS)
    zpart = lambda i: pl.ds(pl.multiple_of(i * ZROWS, ZROWS), ZROWS)
    mine = pl.ds(pl.multiple_of(x * XROWS + z * ZROWS, ZROWS), ZROWS)

    def arrive(h):
        for c in flight[h]:
            c.wait_recv()

    def each_k(h, body):
        def one(k, _):
            body(k + KFIRST[h], pl.ds(pl.multiple_of(k * LOC, LOC), LOC))
            return 0

        lax.fori_loop(0, KCOUNT[h], one, 0)

    def step0(h):
        def cut(k, rows):
            give[h, rows, :] = jnp.where(core == 0, wg[k, :, BLOCK:], wg[k, :, :BLOCK]).astype(BF16)

        each_k(h, cut)
        rows = pl.ds(0, KCOUNT[h] * LOC)
        flight[h] = [send(give.at[h, rows], given.at[h, rows], h, 0, mate)]

    def step1(h):
        arrive(h)

        def add(k, rows):
            keep = jnp.where(core == 0, wg[k, :, :BLOCK], wg[k, :, BLOCK:])
            xbuf[h, rows, :] = (keep + given[h, rows, :].astype(F32)).astype(BF16)

        each_k(h, add)
        rest = WROWS - KCOUNT[h] * LOC
        if rest:
            xbuf[h, pl.ds(KCOUNT[h] * LOC, rest), :] = jnp.zeros((rest, BLOCK), BF16)
        flight[h] = [
            send(xbuf.at[h, xpart(lax.rem(x + d, 4))], xin.at[h, d - 1], h, d, xpeers[d - 1]) for d in range(1, 4)
        ]

    def step2(h):
        arrive(h)
        t = xbuf[h, xpart(x), :].astype(F32)
        for d in range(3):
            t = t + xin[h, d].astype(F32)
        zbuf[h] = t.astype(BF16)
        flight[h] = [
            send(zbuf.at[h, zpart(lax.rem(z + d, 8))], zin.at[h, d - 1], h, 3 + d, zpeers[d - 1]) for d in range(1, 8)
        ]

    def step3(h):
        arrive(h)
        t = zbuf[h, zpart(z), :].astype(F32)
        for d in range(7):
            t = t + zin[h, d].astype(F32)
        res[h, 0, mine, :] = t.astype(BF16)
        flight[h] = [
            send(res.at[h, 0, mine], res.at[h, 0, mine], h, 10 + d, zpeers[d - 1]) for d in range(1, 8)
        ]

    def step4(h):
        arrive(h)
        part = xpart(x)
        flight[h] = [
            send(res.at[h, 0, part], res.at[h, 0, part], h, 17 + d, xpeers[d - 1]) for d in range(1, 4)
        ]

    def step5(h):
        arrive(h)
        rows = pl.ds(0, KCOUNT[h] * LOC)
        flight[h] = [send(res.at[h, 0, rows], res.at[h, 1, rows], h, 21, mate)]

    def kterms(first, last):
        lax.fori_loop(first, last, kterm, 0)

    kterms(0, 8)
    step0(0)
    gather.forward(0)
    kterms(8, 12)
    step1(0)
    kterms(12, 14)
    gather.forward(1)
    kterms(14, 16)
    step0(1)
    kterms(16, 20)
    gather.forward(2)
    step2(0)
    step1(1)
    kterms(20, 24)
    step0(2)
    kterms(24, 25)
    gather.forward(3)
    kterms(25, 27)
    step0(3)
    step2(1)
    step1(2)

    def tile(t, _):
        halves = []
        for e in (2 * t, 2 * t + 1):
            halves.append(jnp.concatenate([own[e], from_dn[e], from_up[e], opp[e]], axis=0))
        rhs = jnp.concatenate(halves, axis=1)
        r = jnp.dot(win[pl.ds(0, OFFSETS * LOC), :], rhs, preferred_element_type=F32)
        r = r.astype(BF16)
        place = 2 * OFFSETS * t
        prod[pl.ds(place, OFFSETS)] = r[:, :BLOCK].reshape(OFFSETS, LOC, BLOCK)
        prod[pl.ds(place + OFFSETS, OFFSETS)] = r[:, BLOCK:].reshape(OFFSETS, LOC, BLOCK)
        return 0

    def tiles(i):
        gather.wait_part(i)
        lax.fori_loop(2 * i, 2 * i + 2, tile, 0)
        lax.fori_loop(2 * i + 8, 2 * i + 10, tile, 0)

    tiles(0)
    step1(3)
    step3(0)
    tiles(1)
    step2(2)
    tiles(2)
    step2(3)
    step3(1)
    tiles(3)
    step4(0)

    def walk(g, acc):
        for u in range(WALK):
            row, col = g // (BLOCK // WALK), lax.rem(g, BLOCK // WALK) * WALK + u
            term = prod[meta_ref[row, col]].astype(F32)
            acc = jnp.where(meta_ref[8 + row, col] > 0, 0.0, acc) + term
            run[g * WALK + u] = acc
        return acc

    third = OFFSETS * BLOCKS // WALK // 3
    acc = lax.fori_loop(0, third, walk, jnp.zeros((LOC, BLOCK), F32))
    step3(2)
    acc = lax.fori_loop(third, 2 * third, walk, acc)
    step3(3)
    step4(1)
    lax.fori_loop(2 * third, 3 * third, walk, acc)
    step5(0)

    def total(d):
        return jnp.where(meta_ref[15, d] > 0, run[meta_ref[7, d]], 0.0)

    for s in range(2 * SLOTS):
        fout[s // SLOTS, s % SLOTS] = total(BLOCKS + s).astype(BF16)
    fcopies = []
    for d, dev in enumerate((below, above)):
        c = rcopy(fout.at[d], fin.at[d], fsend.at[d], frecv.at[d], dev)
        c.start()
        fcopies.append(c)
    sent += fcopies

    def keep(d, _):
        eg[d] = total(d)
        return 0

    lax.fori_loop(0, BLOCKS, keep, 0, unroll=2)
    leave[1].start()
    step4(2)
    step4(3)
    step5(1)
    for c in fcopies:
        c.wait_recv()
    step5(2)
    step5(3)
    for h in range(PARTS):
        arrive(h)
    for c in leave:
        c.wait()
    gather.wait_sends()
    for c in sent:
        c.wait_send()


def norm_call(send, kmap, meta, conv, sums, out_grad, occ, gain, shift, ext, parts):
    quarter = pltpu.VMEM((BLOCKS, LOC, BLOCK), BF16)
    dma = pltpu.SemaphoreType.DMA
    return pl.pallas_call(
        norm_kernel,
        out_shape=(
            jax.ShapeDtypeStruct((LOC, BLOCKS * BLOCK), BF16),
            jax.ShapeDtypeStruct((BLOCKS, LOC, BLOCK), F32),
            jax.ShapeDtypeStruct((2, SLOTS, LOC, BLOCK), BF16),
            jax.ShapeDtypeStruct((PARTS, 2, WROWS, BLOCK), BF16),
            jax.ShapeDtypeStruct((1, BLOCK), F32),
        ),
        in_specs=[SMEM] * 3 + [VMEM, VMEM, ANY, VMEM, VMEM, VMEM, ANY, VMEM],
        out_specs=(ANY, ANY, VMEM, VMEM, VMEM),
        scratch_shapes=[
            pltpu.VMEM((LOC, BLOCKS * BLOCK), BF16),
            pltpu.VMEM((BLOCKS, LOC, BLOCK), F32),
            pltpu.VMEM((LOC, BLOCKS * BLOCK), BF16),
            pltpu.VMEM((EXT + 1, CH, BLOCK), BF16),
            pltpu.VMEM((2, LOC // 2, WPAD), BF16),
            pltpu.VMEM((EXT + 1, BLOCK, CH), BF16),
            pltpu.VMEM((OFFSETS, LOC, CH), F32),
            pltpu.VMEM((CH, WPAD), BF16),
            pltpu.VMEM((WPAD, CH), BF16),
            pltpu.VMEM((OFFSETS * BLOCKS, LOC, BLOCK), BF16),
            pltpu.VMEM((OFFSETS * BLOCKS, LOC, BLOCK), F32),
            quarter,
            quarter,
            quarter,
            quarter,
            pltpu.VMEM((2, 8, 2, BLOCK), F32),
            pltpu.VMEM((2, 8, 1, BLOCK), F32),
            pltpu.VMEM((2, SLOTS, LOC, BLOCK), BF16),
            pltpu.VMEM((PARTS, WROWS, BLOCK), BF16),
            pltpu.VMEM((PARTS, WROWS, BLOCK), BF16),
            pltpu.VMEM((PARTS, WROWS, BLOCK), BF16),
            pltpu.VMEM((PARTS, 3, XROWS, BLOCK), BF16),
            pltpu.VMEM((PARTS, XROWS, BLOCK), BF16),
            pltpu.VMEM((PARTS, 7, ZROWS, BLOCK), BF16),
            dma((3 * NCHUNK,)),
            dma((3 * NCHUNK,)),
            dma((2, 2, 7)),
            dma((2, 2, 7)),
            dma((6,)),
            dma((6,)),
            dma((2,)),
            dma((2,)),
            dma((PARTS, 22)),
            dma((PARTS, 22)),
            dma((4,)),
        ],
        compiler_params=params(2),
        name="norm",
    )(send, kmap, meta, conv, sums, out_grad, occ, gain, shift, ext, parts)


def emit_kernel(
    send_ref, out_ref, eg_ref, fin_ref, res_ref, stat_ref, occ_ref, out_to, in_to, wg_to, gain_to, shift_to, acc
):
    out_to[...] = out_ref[...]
    b = lax.axis_index("box")
    core = lax.rem(b, 2)
    for h in range(PARTS):

        def put(k, _):
            rows = pl.ds(pl.multiple_of(k * LOC, LOC), LOC)
            m, o = res_ref[h, 0, rows, :].astype(F32), res_ref[h, 1, rows, :].astype(F32)
            wg_to[k + KFIRST[h], :, :BLOCK] = jnp.where(core == 0, m, o)
            wg_to[k + KFIRST[h], :, BLOCK:] = jnp.where(core == 0, o, m)
            return 0

        lax.fori_loop(0, KCOUNT[h], put, 0)
    shift_to[...] = stat_ref[:, :LOC]
    gain_to[...] = stat_ref[:, LOC:]
    acc[pl.ds(0, BLOCKS)] = eg_ref[...]
    acc[BLOCKS] = jnp.zeros((LOC, BLOCK), F32)
    for d, ok in ((0, b < NBOX - 1), (1, b > 0)):
        for s in range(SLOTS):
            at = send_ref[0, 1 - d, s]
            acc[at] = acc[at] + jnp.where(ok, fin_ref[d, s].astype(F32), 0.0)

    def settle(d, _):
        in_to[:, pl.ds(pl.multiple_of(d * BLOCK, BLOCK), BLOCK)] = (occ_of(occ_ref, d) * acc[d]).astype(BF16)
        return 0

    lax.fori_loop(0, BLOCKS, settle, 0)


def emit_call(send, occ, out_features, eg, fin, res, stat):
    whole = jax.ShapeDtypeStruct((LOC, BLOCKS * BLOCK), BF16)
    line = jax.ShapeDtypeStruct((1, LOC), F32)
    return pl.pallas_call(
        emit_kernel,
        out_shape=(whole, whole, jax.ShapeDtypeStruct((OFFSETS, LOC, CH), F32), line, line),
        in_specs=[SMEM] + [VMEM] * 6,
        out_specs=(VMEM,) * 5,
        scratch_shapes=[pltpu.VMEM((BLOCKS + 1, LOC, BLOCK), F32)],
        compiler_params=params(),
        name="emit",
    )(send, out_features, eg, fin, res, stat, occ)


def per_device(
    features, occupied, send_lists, kernel_map, weights, norm_gain, norm_shift, out_grad
):
    occ = occupied.reshape(BLOCKS, 1, BLOCK)
    w = weights.reshape(OFFSETS * LOC, CH)
    kernel_map = kernel_map.transpose(1, 0, 2)
    gain, shift = norm_gain.reshape(1, LOC), norm_shift.reshape(1, LOC)
    conv, sums, ext, parts, meta = conv_call(send_lists, kernel_map, features, occ, w)
    results = norm_call(send_lists, kernel_map, meta, conv, sums, out_grad, occ, gain, shift, ext, parts)
    out_features, in_grad, weight_grad, gain_grad, shift_grad = emit_call(send_lists, occ, *results)
    return (out_features, in_grad, weight_grad, gain_grad.reshape(LOC), shift_grad.reshape(LOC))


def solution(mesh):
    in_specs = (
        P("ch", "box"),
        P("box"),
        P("box", None, None),
        P("box", None, None),
        P(None, "ch", None),
        P("ch"),
        P("ch"),
        P("ch", "box"),
    )
    out_specs = (P("ch", "box"), P("ch", "box"), P(None, "ch", None), P("ch"), P("ch"))
    return jax.shard_map(
        per_device, mesh=mesh, in_specs=in_specs, out_specs=out_specs, check_vma=False
    )
```
